32 devices in a mesh: grp: 2 (over y), epoch: 4 (over z), tile: 2 (over x), sub: 2 (over core).
Axes of the slice: x: 2, y: 2, z: 4, core: 2. Of those that a mesh axis runs over, the one named last changes fastest.
Arguments:
- epoch_images: float32 [32, 512, 512], P(('grp', 'epoch'), ('tile', 'sub')), parts along dimension 0, may hold values from -8 to 8
- psf_bank: float32 [16, 16, 16], replicated, may hold values from 0.05 to 1
- psf_index: int32 [32], P(('grp', 'epoch')), parts along dimension 0, may hold values from 0 to 15
- flux_scale: float32 [32], P(('grp', 'epoch')), parts along dimension 0, may hold values from 0.3 to 3
- noise_level: float32 [32], P(('grp', 'epoch')), parts along dimension 0, may hold values from 0.5 to 2
- src_row: int32 [8192], P('grp'), parts along dimension 0, may hold values from 0 to 511
- src_col: int32 [8192], P('grp'), parts along dimension 0, may hold values from 0 to 511
Outputs:
- difference: float32 [32, 512, 512], P(('grp', 'epoch'), ('tile', 'sub')), parts along dimension 0
- fluxes: float32 [32, 4096], P(('grp', 'epoch'), ('tile', 'sub')), parts along dimension 0
The draws below stay inside these ranges and needn't reach their ends.
There are 2 independent parts, one for each index of `grp`. The reference program is written for one: setup_inputs(seed, part) draws one part's arguments, and reference() takes and returns one part's arrays. A program takes and returns all parts, laid end to end along the dimension named above; an argument that names none is the same for every part. Nothing has to cross between parts.
All inputs are finite; a program needn't handle non-finite values.
Results may differ from the reference program's by a relative error of at most 0.0003.
Values sent between devices are 32-bit elements; how exact they have to be, the bound alone decides.
No kernel may reach another device: no remote copies, remote signals or barrier semaphores. Data moves between devices by JAX's collectives and lax.ppermute only.
A program may use at most 128 MiB of HBM per device.

```python
import math
import jax
import jax.numpy as jnp
from jax import lax

TILE = 512
STAMP = 16
NPSF = 16
NSRC = 4096
EPOCHS = 16


def with_ends(entries, own_key, low, top_value):
    dims = entries.shape
    place = [jax.random.randint(jax.random.fold_in(own_key, axis), (), 0, dims[axis]) for axis in range(len(dims))]
    entries = entries.at[tuple(place)].set(low)
    longest = dims.index(max(dims))
    place[longest] = (place[longest] + 1) % dims[longest]
    return entries.at[tuple(place)].set(top_value)


def shard_levels(key, extent, shards, low, top_value):
    factor_of, own = 1.0, jax.random.fold_in(key, 6)
    for position, parts in shards:
        steps = jnp.exp(jax.random.uniform(jax.random.fold_in(own, position), (parts,), jnp.float32, low / len(shards), top_value / len(shards)))
        factor_of = factor_of * jnp.repeat(steps, extent[position] // parts).reshape([-1 if axis == position else 1 for axis in range(len(extent))])
    return factor_of


def bell_draw(stream_key, extent, scale, limit, split=(), kind=jnp.bfloat16):
    values = scale * jax.random.normal(stream_key, extent, jnp.float32)
    if split:
        values = values * shard_levels(stream_key, extent, split, -0.22, 0.18)
    return jnp.clip(values, -limit, limit).astype(kind)


def setup_inputs(seed: int = 0, part: int = 0) -> dict:
    splits = jax.random.split(jax.random.key(seed), 8)
    own_keys = jax.random.split(jax.random.fold_in(splits[7], part), 8)
    return {
        "epoch_images": bell_draw(own_keys[0], (EPOCHS, TILE, TILE), 1.0, 8.0, ((0, 4), (1, 4)), jnp.float32),
        "psf_bank": jnp.clip(jax.random.uniform(splits[1], (NPSF, STAMP, STAMP), jnp.float32, 0.05, 1.0), 0.05, 1.0),
        "psf_index": with_ends(jax.random.randint(own_keys[2], (EPOCHS,), 0, NPSF), jax.random.fold_in(own_keys[2], 1), 0, NPSF - 1).astype(jnp.int32),
        "flux_scale": jnp.clip(jnp.exp(math.log(3.0) - 2.3025851 * jax.random.uniform(own_keys[3], (EPOCHS,), jnp.float32) ** shard_levels(own_keys[3], (EPOCHS,), ((0, 4),), -0.2, 0.2)), 0.3, 3.0),
        "noise_level": jnp.clip(jnp.exp(math.log(2.0) - 1.3862944 * jax.random.uniform(own_keys[4], (EPOCHS,), jnp.float32) ** shard_levels(own_keys[4], (EPOCHS,), ((0, 4),), -0.2, 0.2)), 0.5, 2.0),
        "src_row": with_ends(jax.random.randint(own_keys[5], (NSRC,), 0, TILE), jax.random.fold_in(own_keys[5], 1), 0, TILE - 1).astype(jnp.int32),
        "src_col": with_ends(jax.random.randint(own_keys[6], (NSRC,), 0, TILE), jax.random.fold_in(own_keys[6], 1), 0, TILE - 1).astype(jnp.int32),
    }


def reference(epoch_images, psf_bank, psf_index, flux_scale, noise_level, src_row, src_col):
    stamps = psf_bank[psf_index]
    stamps = stamps / lax.optimization_barrier(jnp.sum(stamps, axis=(1, 2), keepdims=True))
    sumsq = lax.optimization_barrier(jnp.sum(stamps * stamps, axis=(1, 2)))
    padded = jnp.zeros((EPOCHS, TILE, TILE), stamps.dtype).at[:, :STAMP, :STAMP].set(stamps)
    padded = jnp.roll(padded, (-(STAMP // 2), -(STAMP // 2)), (1, 2))
    psf_hat = jnp.fft.fft2(padded)
    image_hat = jnp.fft.fft2(epoch_images)
    psf_power = jnp.real(psf_hat) ** 2 + jnp.imag(psf_hat) ** 2
    weight = (flux_scale / noise_level ** 2)[:, None, None]
    numer = lax.optimization_barrier(jnp.sum(weight * jnp.conj(psf_hat) * image_hat, axis=0))
    q_total = lax.optimization_barrier(jnp.sum((flux_scale ** 2 / noise_level ** 2)[:, None, None] * psf_power, axis=0)) + 0.01
    root_q = jnp.sqrt(q_total)
    template = numer / root_q
    scale = flux_scale[:, None, None]
    noise_norm = jnp.sqrt(noise_level[:, None, None] ** 2 * q_total + scale ** 2 * psf_power + 0.01)
    diff_hat = (root_q * image_hat - scale * psf_hat * template) / noise_norm
    difference = jnp.real(jnp.fft.ifft2(diff_hat))
    flux_map = jnp.real(jnp.fft.ifft2(diff_hat * jnp.conj(psf_hat))) / sumsq[:, None, None]
    fluxes = flux_map[:, src_row, src_col]
    return (difference, fluxes)
```

```python
import math

import jax
import jax.numpy as jnp
import ml_dtypes
import numpy as np
from jax import lax
from jax.experimental import pallas as pl
from jax.experimental.pallas import tpu as pltpu
from jax.sharding import PartitionSpec as P

reg_floor = 0.01
vmem_limit = 40 * 1024 * 1024
bf16, f32 = jnp.bfloat16, jnp.float32


def halves(table):
    table = np.asarray(table, np.float64)
    high = table.astype(ml_dtypes.bfloat16)
    low = (table - high.astype(np.float64)).astype(ml_dtypes.bfloat16)
    return high, low


def split(value):
    high = value.astype(bf16)
    return high, (value - high.astype(f32)).astype(bf16)


def angle(first, second, length):
    return np.outer(first, second) % length * (2.0 * math.pi / length)


def mul(left, right, transposed=False):
    dims = (((1,), (1,)), ((), ())) if transposed else (((1,), (0,)), ((), ()))
    return lax.dot_general(left, right, dims, preferred_element_type=f32)


def mul3(left, right, transposed=False):
    return (
        mul(left[0], right[0], transposed)
        + mul(left[1], right[0], transposed)
        + mul(left[0], right[1], transposed)
    )


class Plan:
    def __init__(self, side, slabs, stamp):
        self.side, self.slabs, self.stamp = side, slabs, stamp
        half = self.half = side // 2
        cols = self.cols = half // slabs
        lanes = self.lanes = 2 * cols
        rows = self.rows = side // slabs
        pairs = self.pairs = slabs // 2
        self.halo = stamp // 2
        self.tall = rows + 2 * self.halo
        self.band = cols + 8
        owner = np.arange(slabs)[:, None]
        freq = 2 * (cols * (owner % pairs) + np.arange(cols)[None, :]) + owner // pairs
        short = np.arange(half)
        taps = np.arange(stamp) - stamp // 2
        order = np.concatenate([2 * short, 2 * short + 1])

        ahead = np.zeros((slabs, lanes, half))
        back = np.zeros((slabs, lanes, half))
        coef = np.zeros((stamp, 2, slabs, lanes))
        shift = np.zeros((slabs, 2, self.band, 2, stamp))
        for d in range(slabs):
            th = angle(freq[d], short, side)
            ahead[d, :cols], ahead[d, cols:] = np.cos(th), -np.sin(th)
            back[d, :cols], back[d, cols:] = 2 * np.cos(th) / side, -2 * np.sin(th) / side
            tb = angle(taps, freq[d], side)
            coef[:, 0, d, :cols] = coef[:, 0, d, cols:] = np.cos(tb)
            coef[:, 1, d, :cols], coef[:, 1, d, cols:] = np.sin(tb), -np.sin(tb)
            extended = np.concatenate([freq[d], [half]])
            te = angle(extended, taps, side)
            ce, se = np.cos(te), np.sin(te)
            shift[d, 0, : cols + 1, 0], shift[d, 0, : cols + 1, 1] = ce, -se
            shift[d, 1, : cols + 1, 0], shift[d, 1, : cols + 1, 1] = -se, -ce
        nyquist = np.cos(math.pi * short)
        ahead[0, cols] = nyquist
        back[0, 0], back[0, cols] = 1.0 / side, nyquist / side
        coef[:, 0, 0, cols], coef[:, 1, 0, cols] = np.cos(math.pi * taps), 0.0
        self.ahead, self.back = halves(ahead), halves(back)
        self.coef = coef.reshape(stamp, 2 * slabs * lanes).astype(np.float32)
        self.shift = shift.reshape(slabs, 2 * self.band, 2 * stamp).astype(np.float32)

        down = np.zeros((2, 2, half, half))
        up = np.zeros((2, half, 2 * half))
        for odd in range(2):
            th = angle(short, 2 * short + odd, side)
            down[odd, 0], down[odd, 1] = np.cos(th), np.sin(th)
            up[odd, :, :half], up[odd, :, half:] = np.cos(th) / side, np.sin(th) / side
        self.down = halves(down.reshape(2, 2, pairs, rows, half))
        self.up = halves(up)
        tu = angle(taps, order, side)
        high, low = halves(np.concatenate([np.cos(tu), np.sin(tu)], 0))
        self.spread = np.concatenate([high, high, low], 0)


def call(kernel, outs, ins, scratch=(), flops=0, moved=0):
    specs = [
        pl.BlockSpec(memory_space=pltpu.SMEM if kind == "s" else pltpu.VMEM) for kind, _ in ins
    ]
    return pl.pallas_call(
        kernel,
        out_shape=tuple(jax.ShapeDtypeStruct(o, f32) for o in outs),
        in_specs=specs,
        out_specs=tuple(pl.BlockSpec(memory_space=pltpu.VMEM) for _ in outs),
        scratch_shapes=list(scratch),
        compiler_params=pltpu.CompilerParams(vmem_limit_bytes=vmem_limit),
        cost_estimate=pl.CostEstimate(flops=flops, bytes_accessed=moved, transcendentals=0),
    )(*[a for _, a in ins])


def row_transform(plan, place, images):
    epochs = images.shape[0]
    width = epochs * plan.rows
    half, lanes, slabs, pairs = plan.half, plan.lanes, plan.slabs, plan.pairs

    def kernel(place_ref, x_ref, high_ref, low_ref, *rest):
        outs = rest[:slabs]
        q = place_ref[0]
        x = x_ref[...].reshape(width, 2 * half)
        first, second = x[:, :half], x[:, half:]
        total = first + second
        change = first - second
        upper = (q >= pairs).astype(jnp.int32)
        flag = jnp.broadcast_to(upper, (1, 1)) > 0
        for group in range(2):
            pick = flag if group == 0 else jnp.logical_not(flag)
            data = split(jnp.where(pick, change, total))
            owners = [q ^ (group * pairs + m) for m in range(pairs)]
            high = jnp.concatenate([high_ref[d] for d in owners], 0)
            low = jnp.concatenate([low_ref[d] for d in owners], 0)
            result = mul3((high, low), data, True)
            for m in range(pairs):
                outs[group * pairs + m][...] = result[m * lanes : (m + 1) * lanes]

    return call(
        kernel,
        [(lanes, width)] * slabs,
        [("s", place), ("v", images), ("v", plan.ahead[0]), ("v", plan.ahead[1])],
        flops=6 * width * half * 2 * half,
        moved=4 * images.size * 2,
    )


def psf_planes(plan, place, bank, index, flux, noise, share):
    epochs = index.shape[0]
    count, stamp = bank.shape[:2]
    side, cols, band, slabs, lanes = plan.side, plan.cols, plan.band, plan.slabs, plan.lanes
    body = epochs * cols
    part = body + 16

    def kernel(
        place_ref, index_ref, flux_ref, noise_ref, share_ref, bank_ref, shift_ref, spread_ref, coef_ref,
        weighted_ref, gain_ref, cross_ref, taps_ref, total_ref,
    ):
        q = place_ref[0]
        lane = lax.broadcasted_iota(jnp.int32, (2 * band, 6 * stamp), 1)
        middle = (lane >= 2 * stamp) & (lane < 4 * stamp)

        def normal(k):
            raw = bank_ref[k]
            return raw / jnp.sum(raw, keepdims=True)

        def spectrum(stamps):
            blank = jnp.zeros((stamp, stamp), f32)
            pair = jnp.concatenate(
                [jnp.concatenate([stamps, blank], 1), jnp.concatenate([blank, stamps], 1)], 0
            )
            triple = jnp.concatenate([pair, pair, pair], 0)
            mixed = lax.dot_general(
                shift_ref[q], triple, (((1,), (1,)), ((), ())),
                precision=lax.Precision.HIGHEST, preferred_element_type=f32,
            )
            high = mixed.astype(bf16).astype(f32)
            left = jnp.where(middle, mixed - high, high).astype(bf16)
            return mul(left, spread_ref[...])

        total_ref[...] = jnp.full((band, side), reg_floor, f32)

        @pl.loop(0, count)
        def _(k):
            plane = spectrum(normal(k))
            re, im = plane[:band], plane[band:]
            total_ref[...] += share_ref[k] * (re * re + im * im)

        weighted_ref[body:part] = jnp.zeros((16, side), f32)
        weighted_ref[part + body :] = jnp.zeros((16, side), f32)
        cross_ref[body:part] = jnp.zeros((16, side), f32)
        cross_ref[part + body :] = jnp.zeros((16, side), f32)
        gain_ref[body:part] = jnp.zeros((16, side), f32)

        for e in range(epochs):
            stamps = normal(index_ref[e])
            plane = spectrum(stamps)
            re, im = plane[:band], plane[band:]
            scale, sigma = flux_ref[e], noise_ref[e]
            q_total = total_ref[...]
            root = jnp.sqrt(q_total)
            inverse = lax.rsqrt(
                sigma * sigma * q_total + scale * scale * (re * re + im * im) + reg_floor
            )
            gain = root * inverse
            ratio = scale * inverse / root
            weight = share_ref[count + e]
            for ref, base, value in (
                (weighted_ref, 0, weight * re), (weighted_ref, part, weight * im),
                (gain_ref, 0, gain),
                (cross_ref, 0, ratio * re), (cross_ref, part, ratio * im),
            ):
                ref[base + e * cols : base + (e + 1) * cols] = value[:cols]
                ref[base + body + e : base + body + e + 1] = value[cols : cols + 1]
            filt = stamps / jnp.sum(stamps * stamps, keepdims=True)
            taps = jnp.dot(
                filt, coef_ref[...], precision=lax.Precision.HIGHEST, preferred_element_type=f32
            )
            for kind in range(2):
                for d in range(slabs):
                    start = (kind * slabs + d) * lanes
                    taps_ref[e, kind, d] = taps[:, start : start + lanes]

    return call(
        kernel,
        [(2 * part, side), (part, side), (2 * part, side), (epochs, 2, slabs, stamp, lanes)],
        [("s", place), ("s", index), ("s", flux), ("s", noise), ("s", share), ("v", bank),
         ("v", plan.shift), ("v", plan.spread), ("v", plan.coef)],
        [pltpu.VMEM((band, side), f32)],
        flops=2 * (count + epochs) * 2 * band * 6 * stamp * side,
        moved=4 * 6 * part * side,
    )


def column_transform(plan, place, blocks, weighted, gain, pieces):
    slabs, pairs, cols, rows, half, side = (
        plan.slabs, plan.pairs, plan.cols, plan.rows, plan.half, plan.side,
    )
    epochs = blocks[0].shape[1] // rows
    body = epochs * cols
    part = body + 16
    band = plan.band
    piece = side // pieces

    def kernel(place_ref, *rest):
        ins = rest[:slabs]
        high_ref, low_ref, weighted_ref, gain_ref = rest[slabs : slabs + 4]
        scaled_ref = rest[slabs + 4]
        outs = rest[slabs + 5 : slabs + 5 + pieces]
        left_high, left_low, numer = rest[slabs + 5 + pieces :]
        q, z = place_ref[0], place_ref[1]
        first = (q == 0).astype(f32)
        sign = jnp.where(q < pairs, 1.0, -1.0).astype(f32)
        row = lax.broadcasted_iota(jnp.int32, (cols, rows), 0)
        keep = 1.0 - first * (row == 0).astype(f32)
        for odd in range(2):
            for m in range(pairs):
                low_part, high_part = ins[m][...], ins[m + pairs][...]
                value = sign * (low_part - high_part) if odd else low_part + high_part
                edges = []
                for e in range(epochs):
                    re = value[:cols, e * rows : (e + 1) * rows]
                    im = value[cols:, e * rows : (e + 1) * rows]
                    edges.append(im[:1] * first)
                    im = im * keep
                    for base, start, entry in (
                        (0, 0, re), (0, half, im), (part, 0, im), (part, half, -re),
                    ):
                        where_row = slice(base + e * cols, base + (e + 1) * cols)
                        where_lane = slice(start + m * rows, start + (m + 1) * rows)
                        high, low = split(entry)
                        left_high[where_row, where_lane] = high
                        left_low[where_row, where_lane] = low
                edge = jnp.concatenate(edges + [jnp.zeros((16 - epochs, rows), f32)], 0)
                for base, start, entry in (
                    (0, 0, edge), (0, half, jnp.zeros_like(edge)),
                    (part, 0, jnp.zeros_like(edge)), (part, half, -edge),
                ):
                    where_row = slice(base + body, base + part)
                    where_lane = slice(start + m * rows, start + (m + 1) * rows)
                    high, low = split(entry)
                    left_high[where_row, where_lane] = high
                    left_low[where_row, where_lane] = low
            order = [(q ^ m) % pairs for m in range(pairs)]
            table = [
                jnp.concatenate([ref[odd, kind, j] for kind in range(2) for j in order], 0)
                for ref in (high_ref, low_ref)
            ]
            plane = mul3((left_high[...], left_low[...]), table)
            lanes = slice(odd * half, (odd + 1) * half)
            re, im = plane[:part], plane[part:]
            wre, wim = weighted_ref[:part, lanes], weighted_ref[part:, lanes]
            numer_re = wre * re + wim * im
            numer_im = wre * im - wim * re
            for base, value in ((0, numer_re), (band, numer_im)):
                body_sum = sum(value[e * cols : (e + 1) * cols] for e in range(epochs))
                edge_sum = jnp.sum(value[body:part], axis=0, keepdims=True)
                whole = jnp.concatenate([body_sum, edge_sum, jnp.zeros((7, half), f32)], 0)
                step = min(piece, half)
                for j in range(half // step):
                    at = odd * half + j * step
                    numer[at // piece, base : base + band, at % piece : at % piece + step] = whole[
                        :, j * step : (j + 1) * step
                    ]
            scaled_ref[:part, lanes] = gain_ref[:, lanes] * re
            scaled_ref[part:, lanes] = gain_ref[:, lanes] * im
        for m in range(pieces):
            outs[m][...] = numer[z ^ m]

    return call(
        kernel,
        [(2 * part, side)] + [(2 * band, piece)] * pieces,
        [("s", place)] + [("v", b) for b in blocks]
        + [("v", plan.down[0]), ("v", plan.down[1]), ("v", weighted), ("v", gain)],
        [pltpu.VMEM((2 * part, side), bf16), pltpu.VMEM((2 * part, side), bf16),
         pltpu.VMEM((pieces, 2 * band, piece), f32)],
        flops=6 * 2 * part * side * side,
        moved=4 * 6 * part * side,
    )


def column_inverse(plan, place, scaled, cross, numer):
    slabs, cols, rows, half, side, lanes, halo, tall = (
        plan.slabs, plan.cols, plan.rows, plan.half, plan.side, plan.lanes, plan.halo, plan.tall,
    )
    part = scaled.shape[0] // 2
    body = part - 16
    epochs = body // cols
    band = plan.band
    pieces = len(numer)
    piece = side // pieces

    def kernel(place_ref, *rest):
        scaled_ref, cross_ref = rest[:2]
        numer_refs = rest[2 : 2 + pieces]
        high_ref, low_ref = rest[2 + pieces : 4 + pieces]
        outs = rest[4 + pieces : 4 + pieces + slabs]
        whole, right_high, right_low, planes = rest[4 + pieces + slabs :]
        q, z = place_ref[0], place_ref[1]
        for m in range(pieces):
            whole[z ^ m] = numer_refs[m][...]
        flag = jnp.broadcast_to(q, (cols, half)) == 0
        row = lax.broadcasted_iota(jnp.int32, (cols, half), 0)
        packed = flag & (row == 0)
        results = []
        for odd in range(2):
            here = slice(odd * half, (odd + 1) * half)
            step = min(piece, half)
            parts = [
                whole[at // piece, :, at % piece : at % piece + step]
                for at in range(odd * half, (odd + 1) * half, step)
            ]
            numer_all = parts[0] if len(parts) == 1 else jnp.concatenate(parts, 1)
            nre, nim = numer_all[:band], numer_all[band:]

            def difference(rows_, nre_, nim_):
                cre = cross_ref[rows_, here]
                below = slice(part + rows_.start, part + rows_.stop)
                cim = cross_ref[below, here]
                re = scaled_ref[rows_, here] - (cre * nre_ - cim * nim_)
                im = scaled_ref[below, here] - (cre * nim_ + cim * nre_)
                return re, im

            edge_re, edge_im = difference(
                slice(body, part), nre[cols : cols + 1], nim[cols : cols + 1]
            )
            for e in range(epochs):
                re, im = difference(slice(e * cols, (e + 1) * cols), nre[:cols], nim[:cols])
                im_left = jnp.where(packed, edge_re[e : e + 1], im)
                im_right = jnp.where(packed, -edge_im[e : e + 1], re)
                for base, start, entry in (
                    (0, 0, re), (0, half, -im), (cols, 0, im_left), (cols, half, im_right),
                ):
                    where_row = slice(e * lanes + base, e * lanes + base + cols)
                    high, low = split(entry)
                    right_high[where_row, start : start + half] = high
                    right_low[where_row, start : start + half] = low
            results.append(
                mul3((high_ref[odd], low_ref[odd]), (right_high[...], right_low[...]), True)
            )
        planes[halo : halo + half] = results[0] + results[1]
        planes[halo + half : halo + side] = results[0] - results[1]
        planes[:halo] = planes[side : side + halo]
        planes[halo + side :] = planes[halo : 2 * halo]
        for m in range(slabs):
            start = pl.multiple_of((q ^ m) * rows, rows)
            for e in range(epochs):
                outs[m][e] = planes[pl.ds(start, tall), e * lanes : (e + 1) * lanes]

    return call(
        kernel,
        [(epochs, tall, lanes)] * slabs,
        [("s", place), ("v", scaled), ("v", cross)] + [("v", n) for n in numer]
        + [("v", plan.up[0]), ("v", plan.up[1])],
        [pltpu.VMEM((pieces, 2 * band, piece), f32),
         pltpu.VMEM((epochs * lanes, side), bf16), pltpu.VMEM((epochs * lanes, side), bf16),
         pltpu.VMEM((side + 2 * halo, epochs * lanes), f32)],
        flops=6 * epochs * lanes * side * side,
        moved=4 * 5 * part * side,
    )


def row_inverse(plan, place, blocks, taps, src_row, src_col, dests):
    slabs, pairs, rows, half, side, lanes, halo, tall, stamp = (
        plan.slabs, plan.pairs, plan.rows, plan.half, plan.side, plan.lanes, plan.halo, plan.tall,
        plan.stamp,
    )
    epochs = blocks[0].shape[0]
    groups, group = src_row.shape
    each = groups // dests

    def kernel(place_ref, row_ref, col_ref, taps_ref, *rest):
        ins = rest[:slabs]
        high_ref, low_ref = rest[slabs : slabs + 2]
        diff_ref = rest[slabs + 2]
        outs = rest[slabs + 3 : slabs + 3 + dests]
        left_high, left_low, flux_high, flux_low, picked = rest[slabs + 3 + dests :]
        q = place_ref[0]
        flux_rows = epochs * rows

        @pl.loop(0, epochs)
        def _(e):
            base = pl.multiple_of(e * rows, rows)
            for m in range(slabs):
                here = slice(m * lanes, (m + 1) * lanes)
                high, low = split(ins[m][e, halo : halo + rows, :])
                left_high[pl.ds(base, rows), here] = high
                left_low[pl.ds(base, rows), here] = low
                d = q ^ m
                for start in range(0, rows, 64):
                    straight = jnp.zeros((64, lanes), f32)
                    crossed = jnp.zeros((64, lanes), f32)
                    for a in range(stamp):
                        value = ins[m][e, start + a : start + a + 64, :]
                        straight += taps_ref[e, 0, d, a : a + 1] * value
                        crossed += taps_ref[e, 1, d, a : a + 1] * value
                    swapped = jnp.concatenate([crossed[:, lanes // 2 :], crossed[:, : lanes // 2]], 1)
                    high, low = split(straight + swapped)
                    left_high[pl.ds(flux_rows + base + start, 64), here] = high
                    left_low[pl.ds(flux_rows + base + start, 64), here] = low

        sign = jnp.where(q < pairs, 1.0, -1.0).astype(f32)
        sums = []
        for side_ in range(2):
            owners = [q ^ (side_ * pairs + m) for m in range(pairs)]
            table = [
                jnp.concatenate([ref[d] for d in owners], 0) for ref in (high_ref, low_ref)
            ]
            here = slice(side_ * pairs * lanes, (side_ + 1) * pairs * lanes)
            sums.append(mul3((left_high[:, here], left_low[:, here]), table))
        for lane_half in range(2):
            value = sums[0] + sums[1] if lane_half == 0 else sign * (sums[0] - sums[1])
            here = slice(lane_half * half, (lane_half + 1) * half)
            diff_ref[:, :, here] = value[:flux_rows].reshape(epochs, rows, half)
            high, low = split(value[flux_rows:])
            flux_high[:, here] = high
            flux_low[:, here] = low

        column = lax.broadcasted_iota(jnp.int32, (side, group), 0)
        line = lax.broadcasted_iota(jnp.int32, (rows, group), 0)
        for g in range(groups):
            chosen = (column == col_ref[g : g + 1]).astype(f32).astype(bf16)
            values = mul(flux_high[...], chosen) + mul(flux_low[...], chosen)
            inside = line == row_ref[g : g + 1] - q * rows
            found = [
                jnp.sum(
                    jnp.where(inside, values[e * rows : (e + 1) * rows], 0.0), axis=0, keepdims=True
                )
                for e in range(epochs)
            ]
            where = (g % each) * group
            picked[g // each, :, where : where + group] = jnp.concatenate(found, 0)
        for m in range(dests):
            outs[m][...] = picked[q ^ m]

    return call(
        kernel,
        [(epochs, rows, side)] + [(epochs, each * group)] * dests,
        [("s", place), ("v", src_row), ("v", src_col), ("v", taps)] + [("v", b) for b in blocks]
        + [("v", plan.back[0]), ("v", plan.back[1])],
        [pltpu.VMEM((2 * epochs * rows, side), bf16), pltpu.VMEM((2 * epochs * rows, side), bf16),
         pltpu.VMEM((epochs * rows, side), bf16), pltpu.VMEM((epochs * rows, side), bf16),
         pltpu.VMEM((dests, epochs, each * group), f32)],
        flops=4 * epochs * rows * side * groups * group,
        moved=4 * 4 * epochs * rows * side,
    )


def trade(parts, axes, count):
    result = list(parts)
    for m in reversed(range(1, count)):
        result[m] = lax.ppermute(parts[m], axes, [(i, i ^ m) for i in range(count)])
    return result


def make_shards(mesh):
    slabs = mesh.shape["tile"] * mesh.shape["sub"]
    ranks = mesh.shape["epoch"]

    def shards(epoch_images, psf_bank, psf_index, flux_scale, noise_level, src_row, src_col):
        epochs, rows, side = epoch_images.shape
        bank_count, stamp = psf_bank.shape[:2]
        plan = Plan(side, slabs, stamp)
        q = lax.axis_index(("tile", "sub"))
        z = lax.axis_index("epoch")
        place = jnp.stack([q, z]).astype(jnp.int32)
        direct = ranks & (ranks - 1) == 0 and side // ranks % 128 == 0

        blocks = row_transform(plan, place, epoch_images)
        blocks = trade(blocks, ("tile", "sub"), slabs)

        power = flux_scale * flux_scale / (noise_level * noise_level)
        chosen = psf_index[:, None] == jnp.arange(bank_count, dtype=jnp.int32)[None, :]
        share = jnp.sum(jnp.where(chosen, power[:, None], 0.0), axis=0)
        if direct:
            share = sum(trade([share] * ranks, "epoch", ranks))
        else:
            share = lax.psum(share, "epoch")
        share = jnp.concatenate([share, flux_scale / (noise_level * noise_level)])
        weighted, gain, cross, taps = psf_planes(
            plan, place, psf_bank, psf_index, flux_scale, noise_level, share
        )
        pieces = ranks if direct else 1
        scaled, *numer = column_transform(
            plan, place if direct else place * jnp.array([1, 0], jnp.int32), blocks, weighted, gain, pieces
        )
        if direct:
            own = sum(trade(numer, "epoch", ranks))
            numer = trade([own] * ranks, "epoch", ranks)
        else:
            numer = [lax.psum(numer[0], "epoch")]
        blocks = column_inverse(
            plan, place if direct else place * jnp.array([1, 0], jnp.int32), scaled, cross, numer
        )
        blocks = trade(blocks, ("tile", "sub"), slabs)
        group = 512
        difference, *picked = row_inverse(
            plan, place, blocks, taps, src_row.reshape(-1, group), src_col.reshape(-1, group), slabs
        )
        fluxes = sum(trade(picked, ("tile", "sub"), slabs))
        return difference, fluxes

    return shards


def solution(mesh):
    in_specs = (
        P(("grp", "epoch"), ("tile", "sub"), None),
        P(),
        P(("grp", "epoch")),
        P(("grp", "epoch")),
        P(("grp", "epoch")),
        P("grp"),
        P("grp"),
    )
    out_specs = (P(("grp", "epoch"), ("tile", "sub"), None), P(("grp", "epoch"), ("tile", "sub")))
    return jax.shard_map(
        make_shards(mesh), mesh=mesh, in_specs=in_specs, out_specs=out_specs, check_vma=False
    )
```

```python
import math

import jax
import jax.numpy as jnp
import ml_dtypes
import numpy as np
from jax import lax
from jax.experimental import pallas as pl
from jax.experimental.pallas import tpu as pltpu
from jax.sharding import PartitionSpec as P

reg_floor = 0.01
vmem_limit = 40 * 1024 * 1024
bf16, f32 = jnp.bfloat16, jnp.float32
edge_rows = 16


def halves(table):
    table = np.asarray(table, np.float64)
    high = table.astype(ml_dtypes.bfloat16)
    return np.stack([high, (table - high.astype(np.float64)).astype(ml_dtypes.bfloat16)])


def split(value):
    high = value.astype(bf16)
    return high, (value - high.astype(f32)).astype(bf16)


def angle(first, second, length):
    return np.outer(first, second) % length * (2.0 * math.pi / length)


def mul(left, right, transposed=False):
    dims = (((1,), (1,)), ((), ())) if transposed else (((1,), (0,)), ((), ()))
    return lax.dot_general(left, right, dims, preferred_element_type=f32)


def mul3(left, right, transposed=False):
    return (
        mul(left[0], right[0], transposed)
        + mul(left[1], right[0], transposed)
        + mul(left[0], right[1], transposed)
    )


class Plan:
    def __init__(self, side, slabs, stamp):
        self.side, self.slabs, self.stamp = side, slabs, stamp
        half = self.half = side // 2
        cols = self.cols = half // slabs
        lanes = self.lanes = 2 * cols
        rows = self.rows = side // slabs
        pairs = self.pairs = slabs // 2
        self.halo = stamp // 2
        self.tall = rows + 2 * self.halo
        self.band = cols + 8
        owner = np.arange(slabs)[:, None]
        freq = 2 * (cols * (owner % pairs) + np.arange(cols)[None, :]) + owner // pairs
        short = np.arange(half)
        taps = np.arange(stamp) - stamp // 2
        order = np.concatenate([2 * short, 2 * short + 1])

        ahead = np.zeros((slabs, 2, cols, half))
        back = np.zeros((slabs, 2, cols, half))
        coef = np.zeros((stamp, 2, slabs, 2, cols))
        shift = np.zeros((slabs, 2, self.band, 2, stamp))
        for d in range(slabs):
            th = angle(freq[d], short, side)
            ahead[d, 0], ahead[d, 1] = np.cos(th), -np.sin(th)
            back[d, 0], back[d, 1] = 2 * np.cos(th) / side, -2 * np.sin(th) / side
            tb = angle(taps, freq[d], side)
            coef[:, 0, d, 0] = coef[:, 0, d, 1] = np.cos(tb)
            coef[:, 1, d, 0], coef[:, 1, d, 1] = np.sin(tb), -np.sin(tb)
            te = angle(np.concatenate([freq[d], [half]]), taps, side)
            ce, se = np.cos(te), np.sin(te)
            shift[d, 0, : cols + 1, 0], shift[d, 0, : cols + 1, 1] = ce, -se
            shift[d, 1, : cols + 1, 0], shift[d, 1, : cols + 1, 1] = -se, -ce
        nyquist = np.cos(math.pi * short)
        ahead[0, 1, 0] = nyquist
        back[0, 0, 0], back[0, 1, 0] = 1.0 / side, nyquist / side
        coef[:, 0, 0, 1, 0], coef[:, 1, 0, 1, 0] = np.cos(math.pi * taps), 0.0
        self.ahead = halves(ahead.reshape(slabs, lanes, half))
        self.back = halves(back.reshape(slabs, lanes, half))
        self.coef = coef.reshape(stamp, 2 * slabs * lanes).astype(np.float32)
        self.shift = halves(shift.reshape(slabs, 2 * self.band, 2 * stamp))

        down = np.zeros((2, 2, half, half))
        up = np.zeros((2, half, 2 * half))
        for odd in range(2):
            th = angle(short, 2 * short + odd, side)
            down[odd, 0], down[odd, 1] = np.cos(th), np.sin(th)
            up[odd, :, :half], up[odd, :, half:] = np.cos(th) / side, np.sin(th) / side
        self.down = halves(down.reshape(2, 2, pairs, rows, half))
        self.up = halves(up)
        tu = angle(taps, order, side)
        high, low = halves(np.concatenate([np.cos(tu), np.sin(tu)], 0))
        self.spread = np.concatenate([high, high, low, np.zeros_like(high)], 0)


def call(kernel, outs, ins, scratch=(), aliases=None):
    space = {"s": pltpu.SMEM, "v": pltpu.VMEM, "h": pl.ANY, "m": pltpu.HBM}
    return pl.pallas_call(
        kernel,
        out_shape=tuple(jax.ShapeDtypeStruct(shape, f32) for _, shape in outs),
        in_specs=[pl.BlockSpec(memory_space=space[kind]) for kind, _ in ins],
        out_specs=tuple(pl.BlockSpec(memory_space=space[kind]) for kind, _ in outs),
        scratch_shapes=list(scratch),
        input_output_aliases=aliases or {},
        compiler_params=pltpu.CompilerParams(vmem_limit_bytes=vmem_limit),
        cost_estimate=pl.CostEstimate(flops=0, bytes_accessed=0, transcendentals=0),
    )(*[a for _, a in ins])


def filter_taps(plan, bank_ref, coef_ref, index_ref, epochs, factor, taps_ref):
    stamp, slabs, lanes = plan.stamp, plan.slabs, plan.lanes
    filters = []
    for e in range(epochs):
        own = bank_ref[index_ref[e]]
        own = own / jnp.sum(own, keepdims=True)
        filters.append(factor(e, own))
    taps = jnp.dot(
        jnp.concatenate(filters, 0), coef_ref[...],
        precision=lax.Precision.HIGHEST, preferred_element_type=f32,
    )
    for kind in range(2):
        for d in range(slabs):
            start = (kind * slabs + d) * lanes
            taps_ref[kind, d] = taps[:, start : start + lanes]


def swap_halves(plan, value):
    return jnp.concatenate([value[:, plan.cols :], value[:, : plan.cols]], 1)


def row_transform(plan, place, index, flux, noise, images, bank):
    epochs, rows, side = images.shape
    width = epochs * rows
    half, slabs, pairs, lanes, tall, stamp = (
        plan.half, plan.slabs, plan.pairs, plan.lanes, plan.tall, plan.stamp,
    )
    step = tall // 2

    def kernel(place_ref, index_ref, flux_ref, noise_ref, bank_ref, coef_ref, image_ref, table_ref, *rest):
        outs, numers = rest[:slabs], rest[slabs : 2 * slabs]
        x_ref, both_ref, taps_ref, padded, gathered, sems = rest[2 * slabs :]
        copies = [
            pltpu.make_async_copy(image_ref, x_ref, sems.at[0]),
            pltpu.make_async_copy(table_ref, both_ref, sems.at[1]),
        ]
        for copy in copies:
            copy.start()
        filter_taps(
            plan, bank_ref, coef_ref, index_ref, epochs,
            lambda e, own: own * (flux_ref[e] / (noise_ref[e] * noise_ref[e])), taps_ref,
        )
        padded[:, :, :stamp] = jnp.zeros((slabs, epochs, stamp, lanes), f32)
        padded[:, :, stamp + rows :] = jnp.zeros((slabs, epochs, stamp, lanes), f32)
        for copy in copies:
            copy.wait()
        q = place_ref[0]
        x = x_ref[...].reshape(width, side)
        first, second = x[:, :half], x[:, half:]
        total = first + second
        change = first - second
        flag = jnp.broadcast_to((q >= pairs).astype(jnp.int32), (1, 1)) > 0
        for group in range(2):
            pick = flag if group == 0 else jnp.logical_not(flag)
            data = split(jnp.where(pick, change, total))
            owners = [q ^ (group * pairs + m) for m in range(pairs)]
            table = [jnp.concatenate([both_ref[n, d] for d in owners], 0) for n in range(2)]
            upright = mul3(data, table, True)
            result = mul3(table, data, True)
            for m in range(pairs):
                here = slice(m * lanes, (m + 1) * lanes)
                outs[group * pairs + m][...] = result[here]
                for e in range(epochs):
                    padded[group * pairs + m, e, stamp : stamp + rows] = upright[
                        e * rows : (e + 1) * rows, here
                    ]

        @pl.loop(0, slabs)
        def _(m):
            d = q ^ m
            for start in range(0, tall, step):
                straight = jnp.zeros((step, lanes), f32)
                crossed = jnp.zeros((step, lanes), f32)
                for e in range(epochs):
                    for a in range(stamp):
                        value = padded[m, e, start + a : start + a + step, :]
                        at = e * stamp + a
                        straight += taps_ref[0, d, at : at + 1] * value
                        crossed += taps_ref[1, d, at : at + 1] * value
                gathered[m, start : start + step] = straight + swap_halves(plan, crossed)

        for m in range(slabs):
            numers[m][...] = gathered[m]

    flat = call(
        kernel,
        [("v", (lanes, width))] * slabs + [("v", (tall, lanes))] * slabs,
        [("s", place), ("s", index), ("s", flux), ("s", noise), ("v", bank), ("v", plan.coef),
         ("m", images), ("m", plan.ahead)],
        [pltpu.VMEM(images.shape, f32), pltpu.VMEM(plan.ahead.shape, bf16),
         pltpu.VMEM((2, slabs, epochs * stamp, lanes), f32),
         pltpu.VMEM((slabs, epochs, rows + 2 * stamp, lanes), f32),
         pltpu.VMEM((slabs, tall, lanes), f32), pltpu.SemaphoreType.DMA((2,))],
    )
    return list(flat[:slabs]), list(flat[slabs:])


def numerator(plan, place, index, flux, noise, blocks, pieces):
    slabs, cols, rows, half, side, lanes, halo, tall = (
        plan.slabs, plan.cols, plan.rows, plan.half, plan.side, plan.lanes, plan.halo, plan.tall,
    )
    epochs = index.shape[0]
    piece = side // pieces

    def kernel(place_ref, index_ref, flux_ref, noise_ref, *rest):
        ins, table_ref = rest[:slabs], rest[slabs]
        outs = rest[slabs + 1 : slabs + 1 + pieces]
        whole, parts = rest[slabs + 1 + pieces :]
        q, z = place_ref[0], place_ref[1] if pieces > 1 else 0
        whole[...] = jnp.zeros((side + 2 * halo, lanes), f32)
        for m in range(slabs):
            at = pl.multiple_of((q ^ m) * rows, rows)
            whole[pl.ds(at, tall)] += ins[m][...]
        whole[side : side + halo] += whole[:halo]
        whole[halo : 2 * halo] += whole[side + halo :]
        top, bottom = whole[halo : halo + half], whole[halo + half : halo + side]
        row = lax.broadcasted_iota(jnp.int32, (cols, half), 0)
        first = (q == 0).astype(f32)
        keep = 1.0 - first * (row == 0).astype(f32)
        line = lax.broadcasted_iota(jnp.int32, (edge_rows, half), 0)
        for odd in range(2):
            value = (top - bottom if odd else top + bottom).T
            re, im = value[:cols], value[cols:]
            edge = jnp.broadcast_to(im[:1] * first, (edge_rows, half))
            im = im * keep
            left = jnp.concatenate(
                [
                    jnp.concatenate([re, im, jnp.where(line == 0, edge, 0.0)], 0),
                    jnp.concatenate([im, -re, jnp.where(line == 1, -edge, 0.0)], 0),
                ],
                1,
            )
            table = [
                jnp.concatenate([table_ref[n, odd, kind].reshape(half, half) for kind in range(2)], 0)
                for n in range(2)
            ]
            plane = mul3(split(left), table)[: lanes + 8]
            step = min(piece, half)
            for i in range(half // step):
                at = odd * half + i * step
                parts[at // piece, :, at % piece : at % piece + step] = plane[:, i * step : (i + 1) * step]
        lane = lax.broadcasted_iota(jnp.int32, (1, piece), 1)
        shares = jnp.zeros((1, piece), f32)
        for e in range(epochs):
            ratio = flux_ref[e] / noise_ref[e]
            shares += jnp.where(lane == index_ref[e], ratio * ratio, 0.0)
        for m in range(pieces):
            parts[m, lanes + 2 : lanes + 3] = shares
        for m in range(pieces):
            outs[m][...] = parts[z ^ m]

    return call(
        kernel,
        [("v", (lanes + 8, piece))] * pieces,
        [("s", place), ("s", index), ("s", flux), ("s", noise)] + [("v", b) for b in blocks]
        + [("v", plan.down)],
        [pltpu.VMEM((side + 2 * halo, lanes), f32), pltpu.VMEM((pieces, lanes + 8, piece), f32)],
    )


def psf_planes(plan, place, bank, index):
    epochs = index.shape[0]
    count, stamp = bank.shape[:2]
    side, cols, band, slabs, lanes = plan.side, plan.cols, plan.band, plan.slabs, plan.lanes
    body = epochs * cols
    size = body + edge_rows
    pitch = 8 * stamp

    def kernel(
        place_ref, index_ref, bank_ref, shift_ref, spread_ref, coef_ref,
        spectrum_ref, power_ref, taps_ref, right_ref, plane_ref,
    ):
        q = place_ref[0]
        stamps = bank_ref[...]
        stamps = stamps / jnp.sum(jnp.sum(stamps, axis=2, keepdims=True), axis=1, keepdims=True)
        blank = jnp.zeros((stamp, stamp), f32)
        for k in range(count):
            pair = jnp.concatenate(
                [jnp.concatenate([stamps[k], blank], 1), jnp.concatenate([blank, stamps[k]], 1)], 0
            )
            for copy in range(4):
                at = k * pitch + copy * 2 * stamp
                right_ref[at : at + 2 * stamp] = pair
        right = split(right_ref[...])
        mixed = mul3((shift_ref[0, q], shift_ref[1, q]), right, True)
        lane = lax.broadcasted_iota(jnp.int32, mixed.shape, 1) % pitch
        middle = (lane >= 2 * stamp) & (lane < 4 * stamp)
        high = mixed.astype(bf16).astype(f32)
        left = jnp.where(middle, mixed - high, high).astype(bf16)
        for k in range(count):
            plane = mul(left[:, k * pitch : (k + 1) * pitch], spread_ref[...])
            plane_ref[k] = plane
            power_ref[k] = plane[:band] * plane[:band] + plane[band:] * plane[band:]
        for e in range(epochs):
            k = index_ref[e]
            for base, start in ((0, 0), (size, band)):
                value = plane_ref[k, start : start + band]
                spectrum_ref[base + e * cols : base + (e + 1) * cols] = value[:cols]
                spectrum_ref[base + body + e : base + body + e + 1] = value[cols : cols + 1]
        none = jnp.zeros((edge_rows - epochs, side), f32)
        spectrum_ref[body + epochs : size] = none
        spectrum_ref[size + body + epochs :] = none
        filter_taps(
            plan, bank_ref, coef_ref, index_ref, epochs,
            lambda e, own: own / jnp.sum(own * own, keepdims=True), taps_ref,
        )

    return call(
        kernel,
        [("v", (2 * size, side)), ("v", (count, band, side)), ("v", (2, slabs, epochs * stamp, lanes))],
        [("s", place), ("s", index), ("v", bank), ("v", plan.shift), ("v", plan.spread), ("v", plan.coef)],
        [pltpu.VMEM((count * pitch, 2 * stamp), f32), pltpu.VMEM((count, 2 * band, side), f32)],
    )


def filter_gains(plan, flux, noise, share, spectrum, power):
    epochs = flux.shape[0]
    count = power.shape[0]
    side, cols = plan.side, plan.cols
    body = epochs * cols
    size = body + edge_rows
    row = plan.lanes + 2

    def kernel(flux_ref, noise_ref, share_ref, spectrum_ref, power_ref, gain_ref, cross_ref):
        shares = [jnp.broadcast_to(share_ref[row : row + 1, k : k + 1], (8, side)) for k in range(count)]
        none = jnp.zeros((edge_rows - epochs, side), f32)
        gain_ref[body + epochs : size] = none
        cross_ref[body + epochs : size] = none
        cross_ref[size + body + epochs :] = none
        for block in range(plan.band // 8):
            total = jnp.full((8, side), reg_floor, f32)
            for k in range(count):
                total += shares[k] * power_ref[k, block * 8 : block * 8 + 8]
            edge = block == cols // 8
            total = total[:1] if edge else total
            lines = 1 if edge else 8
            root = jnp.sqrt(total)
            inverse_root = 1.0 / root
            for e in range(epochs):
                at = body + e if edge else e * cols + block * 8
                re = spectrum_ref[at : at + lines]
                im = spectrum_ref[size + at : size + at + lines]
                scale, sigma = flux_ref[e], noise_ref[e]
                inverse = lax.rsqrt(
                    sigma * sigma * total + scale * scale * (re * re + im * im) + reg_floor
                )
                ratio = scale * inverse * inverse_root
                gain_ref[at : at + lines] = root * inverse
                cross_ref[at : at + lines] = ratio * re
                cross_ref[size + at : size + at + lines] = ratio * im

    return call(
        kernel,
        [("v", (size, side)), ("v", (2 * size, side))],
        [("s", flux), ("s", noise), ("v", share), ("v", spectrum), ("v", power)],
    )


def column_transform(plan, place, blocks):
    slabs, pairs, cols, rows, half, side = plan.slabs, plan.pairs, plan.cols, plan.rows, plan.half, plan.side
    epochs = blocks[0].shape[1] // rows
    body = epochs * cols
    size = body + edge_rows

    def kernel(place_ref, *rest):
        ins = rest[:slabs]
        table_ref, plane_ref, left_high, left_low = rest[slabs:]
        q = place_ref[0]
        first = (q == 0).astype(f32)
        sign = jnp.where(q < pairs, 1.0, -1.0).astype(f32)
        row = lax.broadcasted_iota(jnp.int32, (cols, rows), 0)
        keep = 1.0 - first * (row == 0).astype(f32)

        def put(row_at, lane_at, entry):
            where = (slice(row_at, row_at + entry.shape[0]), slice(lane_at, lane_at + rows))
            left_high[where], left_low[where] = split(entry)

        for odd in range(2):
            for m in range(pairs):
                near, far = ins[m][...], ins[m + pairs][...]
                value = sign * (near - far) if odd else near + far
                edges = []
                for e in range(epochs):
                    re = value[:cols, e * rows : (e + 1) * rows]
                    im = value[cols:, e * rows : (e + 1) * rows]
                    edges.append(im[:1] * first)
                    im = im * keep
                    put(e * cols, m * rows, re)
                    put(e * cols, half + m * rows, im)
                    put(size + e * cols, m * rows, im)
                    put(size + e * cols, half + m * rows, -re)
                edge = jnp.concatenate(edges + [jnp.zeros((edge_rows - epochs, rows), f32)], 0)
                put(body, m * rows, edge)
                put(body, half + m * rows, jnp.zeros_like(edge))
                put(size + body, m * rows, jnp.zeros_like(edge))
                put(size + body, half + m * rows, -edge)
            order = [(q ^ m) % pairs for m in range(pairs)]
            table = [
                jnp.concatenate([table_ref[n, odd, kind, i] for kind in range(2) for i in order], 0)
                for n in range(2)
            ]
            plane_ref[:, odd * half : (odd + 1) * half] = mul3((left_high[...], left_low[...]), table)

    (plane,) = call(
        kernel,
        [("v", (2 * size, side))],
        [("s", place)] + [("v", b) for b in blocks] + [("v", plan.down)],
        [pltpu.VMEM((2 * size, side), bf16), pltpu.VMEM((2 * size, side), bf16)],
    )
    return plane


def column_inverse(plan, place, spectrum, gain, cross, numer, begin, end):
    slabs, cols, rows, half, side, lanes, halo, tall = (
        plan.slabs, plan.cols, plan.rows, plan.half, plan.side, plan.lanes, plan.halo, plan.tall,
    )
    size = gain.shape[0]
    body = size - edge_rows
    epochs = end - begin
    pieces = len(numer)
    piece = side // pieces

    def kernel(place_ref, spectrum_ref, gain_ref, cross_ref, *rest):
        numer_refs, table_ref = rest[:pieces], rest[pieces]
        outs = rest[pieces + 1 : pieces + 1 + slabs]
        whole, right_high, right_low, planes = rest[pieces + 1 + slabs :]
        q, z = place_ref[0], place_ref[1] if pieces > 1 else 0
        for m in range(pieces):
            whole[z ^ m] = numer_refs[m][...]
        flag = jnp.broadcast_to(q, (cols, half)) == 0
        packed = flag & (lax.broadcasted_iota(jnp.int32, (cols, half), 0) == 0)
        results = []
        for odd in range(2):
            here = slice(odd * half, (odd + 1) * half)
            step = min(piece, half)
            parts = [
                whole[at // piece, :, at % piece : at % piece + step]
                for at in range(odd * half, (odd + 1) * half, step)
            ]
            numer_all = parts[0] if len(parts) == 1 else jnp.concatenate(parts, 1)

            def difference(start, stop, nre, nim):
                gain_, cre = gain_ref[start:stop, here], cross_ref[start:stop, here]
                cim = cross_ref[size + start : size + stop, here]
                re = gain_ * spectrum_ref[start:stop, here] - (cre * nre - cim * nim)
                im = gain_ * spectrum_ref[size + start : size + stop, here] - (cre * nim + cim * nre)
                return re, im

            edge_re, edge_im = difference(
                body, size, numer_all[lanes : lanes + 1], numer_all[lanes + 1 : lanes + 2]
            )
            for i in range(epochs):
                e = begin + i
                re, im = difference(e * cols, (e + 1) * cols, numer_all[:cols], numer_all[cols:lanes])
                im_left = jnp.where(packed, edge_re[e : e + 1], im)
                im_right = jnp.where(packed, -edge_im[e : e + 1], re)
                for base, start, entry in (
                    (0, 0, re), (0, half, -im), (cols, 0, im_left), (cols, half, im_right),
                ):
                    where = (
                        slice(i * lanes + base, i * lanes + base + cols),
                        slice(start, start + half),
                    )
                    right_high[where], right_low[where] = split(entry)
            results.append(
                mul3((table_ref[0, odd], table_ref[1, odd]), (right_high[...], right_low[...]), True)
            )
        planes[halo : halo + half] = results[0] + results[1]
        planes[halo + half : halo + side] = results[0] - results[1]
        planes[:halo] = planes[side : side + halo]
        planes[halo + side :] = planes[halo : 2 * halo]
        for m in range(slabs):
            start = pl.multiple_of((q ^ m) * rows, rows)
            for i in range(epochs):
                outs[m][i] = planes[pl.ds(start, tall), i * lanes : (i + 1) * lanes]

    return call(
        kernel,
        [("v", (epochs, tall, lanes))] * slabs,
        [("s", place), ("v", spectrum), ("v", gain), ("v", cross)] + [("v", n) for n in numer]
        + [("v", plan.up)],
        [pltpu.VMEM((pieces, lanes + 8, piece), f32),
         pltpu.VMEM((epochs * lanes, side), bf16), pltpu.VMEM((epochs * lanes, side), bf16),
         pltpu.VMEM((side + 2 * halo, epochs * lanes), f32)],
    )


def row_inverse(plan, place, blocks, taps, begin, epochs, difference, src_row, src_col):
    slabs, pairs, rows, half, side, lanes, halo, stamp = (
        plan.slabs, plan.pairs, plan.rows, plan.half, plan.side, plan.lanes, plan.halo, plan.stamp,
    )
    mine = blocks[0].shape[0]
    groups, group = src_row.shape
    each = groups // slabs
    total = mine * rows
    step = min(64, rows)

    def kernel(place_ref, row_ref, col_ref, taps_ref, *rest):
        ins, table_ref = rest[:slabs], rest[slabs]
        rest = rest[slabs + 1 + (difference is not None) :]
        diff_ref, outs = rest[0], rest[1 : 1 + slabs]
        left_high, left_low, image_ref, flux_ref, picked, sem = rest[1 + slabs :]
        q = place_ref[0]
        for m in range(slabs):
            d = q ^ m
            here = slice(m * lanes, (m + 1) * lanes)
            for i in range(mine):
                base = i * rows
                left_high[base : base + rows, here], left_low[base : base + rows, here] = split(
                    ins[m][i, halo : halo + rows, :]
                )
                for start in range(0, rows, step):
                    straight = jnp.zeros((step, lanes), f32)
                    crossed = jnp.zeros((step, lanes), f32)
                    for a in range(stamp):
                        value = ins[m][i, start + a : start + a + step, :]
                        at = (begin + i) * stamp + a
                        straight += taps_ref[0, d, at : at + 1] * value
                        crossed += taps_ref[1, d, at : at + 1] * value
                    at = total + base + start
                    left_high[at : at + step, here], left_low[at : at + step, here] = split(
                        straight + swap_halves(plan, crossed)
                    )

        sums = []
        for side_ in range(2):
            members = [side_ * pairs + m for m in range(pairs)]
            table = [jnp.concatenate([table_ref[n, q ^ m] for m in members], 0) for n in range(2)]
            here = slice(side_ * pairs * lanes, (side_ + 1) * pairs * lanes)
            sums.append(mul3((left_high[:, here], left_low[:, here]), table))
        sign = jnp.where(q < pairs, 1.0, -1.0).astype(f32)
        for lane_half in range(2):
            value = sums[0] + sums[1] if lane_half == 0 else sign * (sums[0] - sums[1])
            here = slice(lane_half * half, (lane_half + 1) * half)
            image_ref[:, :, here] = value[:total].reshape(mine, rows, half)
            flux_ref[:total, here], flux_ref[total:, here] = split(value[total:])
        copy = pltpu.make_async_copy(image_ref, diff_ref.at[pl.ds(begin, mine)], sem)
        copy.start()
        column = lax.broadcasted_iota(jnp.int32, (side, group), 0)
        line = lax.broadcasted_iota(jnp.int32, (rows, group), 0)
        for g in range(groups):
            chosen = (column == col_ref[g : g + 1]).astype(f32).astype(bf16)
            values = mul(flux_ref[...], chosen)
            values = values[:total] + values[total:]
            inside = line == row_ref[g : g + 1] - q * rows
            found = [
                jnp.sum(
                    jnp.where(inside, values[e * rows : (e + 1) * rows], 0.0), axis=0, keepdims=True
                )
                for e in range(mine)
            ]
            where = (g % each) * group
            picked[g // each, :, where : where + group] = jnp.concatenate(found, 0)
        for m in range(slabs):
            outs[m][...] = picked[q ^ m]
        copy.wait()

    ins = [("s", place), ("v", src_row), ("v", src_col), ("v", taps)]
    ins += [("v", b) for b in blocks] + [("v", plan.back)]
    aliases = {}
    if difference is not None:
        aliases = {len(ins): 0}
        ins.append(("h", difference))
    left = pltpu.VMEM((2 * total, side), bf16)
    return call(
        kernel,
        [("h", (epochs, rows, side))] + [("v", (mine, each * group))] * slabs,
        ins,
        [left, left, pltpu.VMEM((mine, rows, side), f32), left,
         pltpu.VMEM((slabs, mine, each * group), f32), pltpu.SemaphoreType.DMA(())],
        aliases=aliases,
    )


def trade(parts, axes, count):
    result = list(parts)
    for m in reversed(range(1, count)):
        result[m] = lax.ppermute(parts[m], axes, [(i, i ^ m) for i in range(count)])
    return result


def make_shards(mesh):
    slabs = mesh.shape["tile"] * mesh.shape["sub"]
    ranks = mesh.shape["epoch"]
    slab_axes = ("tile", "sub")

    def shards(epoch_images, psf_bank, psf_index, flux_scale, noise_level, src_row, src_col):
        epochs, rows, side = epoch_images.shape
        plan = Plan(side, slabs, psf_bank.shape[1])
        place = jnp.stack([lax.axis_index(slab_axes), lax.axis_index("epoch")]).astype(jnp.int32)
        direct = ranks & (ranks - 1) == 0 and side // ranks % 128 == 0
        pieces = ranks if direct else 1
        parties = 2 if epochs % 2 == 0 else 1
        group = math.gcd(512, src_row.shape[0] // slabs)
        scalars = (psf_index, flux_scale, noise_level)

        blocks, numer = row_transform(plan, place, *scalars, epoch_images, psf_bank)
        numer = trade(numer, slab_axes, slabs)
        numer = numerator(plan, place, *scalars, numer, pieces)
        blocks, numer = lax.optimization_barrier((blocks, numer))
        blocks = trade(blocks, slab_axes, slabs)
        spectrum, power, taps = psf_planes(plan, place, psf_bank, psf_index)
        if direct:
            own = sum(trade(numer, "epoch", ranks))
            numer = trade([own] * ranks, "epoch", ranks)
        else:
            own = lax.psum(numer[0], "epoch")
            numer = [own]
        images = column_transform(plan, place, blocks)
        gain, cross = filter_gains(plan, flux_scale, noise_level, own, spectrum, power)

        difference, fluxes = None, []
        each = epochs // parties
        returned = [
            trade(
                column_inverse(plan, place, images, gain, cross, numer, i * each, (i + 1) * each),
                slab_axes, slabs,
            )
            for i in range(parties)
        ]
        for i in range(parties):
            difference, *picked = row_inverse(
                plan, place, returned[i], taps, i * each, epochs, difference,
                src_row.reshape(-1, group), src_col.reshape(-1, group),
            )
            fluxes.append(sum(trade(picked, slab_axes, slabs)))
        return difference, jnp.concatenate(fluxes, 0)

    return shards


def solution(mesh):
    in_specs = (
        P(("grp", "epoch"), ("tile", "sub"), None),
        P(),
        P(("grp", "epoch")),
        P(("grp", "epoch")),
        P(("grp", "epoch")),
        P("grp"),
        P("grp"),
    )
    out_specs = (P(("grp", "epoch"), ("tile", "sub"), None), P(("grp", "epoch"), ("tile", "sub")))
    return jax.shard_map(
        make_shards(mesh), mesh=mesh, in_specs=in_specs, out_specs=out_specs, check_vma=False
    )
```

```python
import math

import jax
import jax.numpy as jnp
import ml_dtypes
import numpy as np
from jax import lax
from jax.experimental import pallas as pl
from jax.experimental.pallas import tpu as pltpu
from jax.sharding import PartitionSpec as P

reg_floor = 0.01
vmem_limit = 40 * 1024 * 1024
bf16, f32 = jnp.bfloat16, jnp.float32
hbm_rate = 3.69e6
edge_rows = 16


def halves(table):
    table = np.asarray(table, np.float64)
    high = table.astype(ml_dtypes.bfloat16)
    return np.stack([high, (table - high.astype(np.float64)).astype(ml_dtypes.bfloat16)])


def split(value):
    high = value.astype(bf16)
    return high, (value - high.astype(f32)).astype(bf16)


def angle(first, second, length):
    return np.outer(first, second) % length * (2.0 * math.pi / length)


def mul(left, right, transposed=False):
    dims = (((1,), (1,)), ((), ())) if transposed else (((1,), (0,)), ((), ()))
    return lax.dot_general(left, right, dims, preferred_element_type=f32)


def mul3(left, right, transposed=False):
    return (
        mul(left[0], right[0], transposed)
        + mul(left[1], right[0], transposed)
        + mul(left[0], right[1], transposed)
    )


class Plan:
    def __init__(self, side, slabs, stamp):
        self.side, self.slabs, self.stamp = side, slabs, stamp
        half = self.half = side // 2
        cols = self.cols = half // slabs
        lanes = self.lanes = 2 * cols
        rows = self.rows = side // slabs
        pairs = self.pairs = slabs // 2
        self.halo = stamp // 2
        self.tall = rows + 2 * self.halo
        self.band = cols + 8
        owner = np.arange(slabs)[:, None]
        freq = 2 * (cols * (owner % pairs) + np.arange(cols)[None, :]) + owner // pairs
        short = np.arange(half)
        taps = np.arange(stamp) - stamp // 2
        order = np.concatenate([2 * short, 2 * short + 1])

        ahead = np.zeros((slabs, 2, cols, half))
        back = np.zeros((slabs, 2, cols, half))
        coef = np.zeros((stamp, 2, slabs, 2, cols))
        shift = np.zeros((slabs, 2, self.band, 2, stamp))
        for d in range(slabs):
            th = angle(freq[d], short, side)
            ahead[d, 0], ahead[d, 1] = np.cos(th), -np.sin(th)
            back[d, 0], back[d, 1] = 2 * np.cos(th) / side, -2 * np.sin(th) / side
            tb = angle(taps, freq[d], side)
            coef[:, 0, d, 0] = coef[:, 0, d, 1] = np.cos(tb)
            coef[:, 1, d, 0], coef[:, 1, d, 1] = np.sin(tb), -np.sin(tb)
            te = angle(np.concatenate([freq[d], [half]]), taps, side)
            ce, se = np.cos(te), np.sin(te)
            shift[d, 0, : cols + 1, 0], shift[d, 0, : cols + 1, 1] = ce, -se
            shift[d, 1, : cols + 1, 0], shift[d, 1, : cols + 1, 1] = -se, -ce
        nyquist = np.cos(math.pi * short)
        ahead[0, 1, 0] = nyquist
        back[0, 0, 0], back[0, 1, 0] = 1.0 / side, nyquist / side
        coef[:, 0, 0, 1, 0], coef[:, 1, 0, 1, 0] = np.cos(math.pi * taps), 0.0
        self.ahead = halves(ahead.reshape(slabs, lanes, half))
        self.back = halves(back.reshape(slabs, lanes, half))
        self.coef = coef.reshape(stamp, 2 * slabs * lanes).astype(np.float32)
        self.shift = halves(shift.reshape(slabs, 2 * self.band, 2 * stamp))

        down = np.zeros((2, 2, half, half))
        up = np.zeros((2, half, 2 * half))
        for odd in range(2):
            th = angle(short, 2 * short + odd, side)
            down[odd, 0], down[odd, 1] = np.cos(th), np.sin(th)
            up[odd, :, :half], up[odd, :, half:] = np.cos(th) / side, np.sin(th) / side
        self.down = halves(down.reshape(2, 2, pairs, rows, half))
        self.up = halves(up)
        tu = angle(taps, order, side)
        high, low = halves(np.concatenate([np.cos(tu), np.sin(tu)], 0))
        self.spread = np.concatenate([high, high, low, np.zeros_like(high)], 0)


def call(kernel, outs, ins, scratch=(), aliases=None, micros=0.0):
    space = {"s": pltpu.SMEM, "v": pltpu.VMEM, "h": pl.ANY, "m": pltpu.HBM}
    ins = [
        (kind, pltpu.with_memory_space_constraint(jnp.asarray(a), pltpu.HBM) if kind == "m" else a)
        for kind, a in ins
    ]
    return pl.pallas_call(
        kernel,
        out_shape=tuple(jax.ShapeDtypeStruct(shape, (*kind, f32)[0]) for _, shape, *kind in outs),
        in_specs=[pl.BlockSpec(memory_space=space[kind]) for kind, _ in ins],
        out_specs=tuple(pl.BlockSpec(memory_space=space[out[0]]) for out in outs),
        scratch_shapes=list(scratch),
        input_output_aliases=aliases or {},
        compiler_params=pltpu.CompilerParams(vmem_limit_bytes=vmem_limit),
        cost_estimate=pl.CostEstimate(flops=0, bytes_accessed=int(micros * hbm_rate), transcendentals=0),
    )(*[a for _, a in ins])


def filter_taps(plan, bank_ref, coef_ref, index_ref, epochs, factor, taps_ref):
    stamp, slabs, lanes = plan.stamp, plan.slabs, plan.lanes
    filters = []
    for e in range(epochs):
        own = bank_ref[index_ref[e]]
        own = own / jnp.sum(own, keepdims=True)
        filters.append(factor(e, own))
    taps = jnp.dot(
        jnp.concatenate(filters, 0), coef_ref[...],
        precision=lax.Precision.HIGHEST, preferred_element_type=f32,
    )
    for kind in range(2):
        for d in range(slabs):
            start = (kind * slabs + d) * lanes
            taps_ref[kind, d] = taps[:, start : start + lanes]


def swap_halves(plan, value):
    return jnp.concatenate([value[:, plan.cols :], value[:, : plan.cols]], 1)


def owners_of(plan, q, group):
    return [q ^ (group * plan.pairs + m) for m in range(plan.pairs)]


def row_operands(plan, q, group, x_ref, table_ref):
    half = plan.half
    x = x_ref[...].reshape(-1, 2 * half)
    first, second = x[:, :half], x[:, half:]
    sign = jnp.where((q >= plan.pairs) != (group == 1), -1.0, 1.0).astype(f32)
    data = split(first + sign * second)
    table = [
        jnp.concatenate([table_ref[n, d] for d in owners_of(plan, q, group)], 0) for n in range(2)
    ]
    return data, table


def coadd_rows(plan, q, group, x_ref, table_ref, taps_ref, padded, gathered, outs):
    rows, lanes, tall, stamp, pairs = plan.rows, plan.lanes, plan.tall, plan.stamp, plan.pairs
    epochs = x_ref.shape[0]
    step = tall // 2
    padded[:, :, :stamp] = jnp.zeros((pairs, epochs, stamp, lanes), f32)
    padded[:, :, stamp + rows :] = jnp.zeros((pairs, epochs, stamp, lanes), f32)
    data, table = row_operands(plan, q, group, x_ref, table_ref)
    upright = mul3(data, table, True)
    for m in range(pairs):
        for e in range(epochs):
            padded[m, e, stamp : stamp + rows] = upright[
                e * rows : (e + 1) * rows, m * lanes : (m + 1) * lanes
            ]

    @pl.loop(0, pairs)
    def _(m):
        d = q ^ (group * pairs + m)
        for start in range(0, tall, step):
            straight = jnp.zeros((step, lanes), f32)
            crossed = jnp.zeros((step, lanes), f32)
            for e in range(epochs):
                for a in range(stamp):
                    value = padded[m, e, start + a : start + a + step, :]
                    at = e * stamp + a
                    straight += taps_ref[0, d, at : at + 1] * value
                    crossed += taps_ref[1, d, at : at + 1] * value
            gathered[m, start : start + step] = straight + swap_halves(plan, crossed)

    for m in range(pairs):
        outs[m][...] = gathered[m]


def coadd_scratch(plan, epochs):
    return [
        pltpu.VMEM((plan.pairs, epochs, plan.rows + 2 * plan.stamp, plan.lanes), f32),
        pltpu.VMEM((plan.pairs, plan.tall, plan.lanes), f32),
    ]


def row_transform_far(plan, place, index, flux, noise, images, bank):
    epochs = images.shape[0]
    slabs, pairs, lanes, tall, stamp = plan.slabs, plan.pairs, plan.lanes, plan.tall, plan.stamp

    def kernel(place_ref, *rest):
        sources, outs, rest = rest[:7], rest[7 : 7 + pairs], rest[7 + pairs :]
        taps_ref, x_ref, table_ref, index_ref, flux_ref, noise_ref, bank_ref, coef_ref = rest[:8]
        padded, gathered, sems = rest[8:]
        targets = [index_ref, flux_ref, noise_ref, bank_ref, coef_ref, x_ref, table_ref]
        copies = [pltpu.make_async_copy(sources[i], targets[i], sems.at[i]) for i in range(7)]
        for copy in copies:
            copy.start()
        for copy in copies[:5]:
            copy.wait()
        filter_taps(
            plan, bank_ref, coef_ref, index_ref, epochs,
            lambda e, own: own * (flux_ref[e] / (noise_ref[e] * noise_ref[e])), taps_ref,
        )
        for copy in copies[5:]:
            copy.wait()
        coadd_rows(plan, place_ref[0], 1, x_ref, table_ref, taps_ref, padded, gathered, outs)

    flat = call(
        kernel,
        [("v", (tall, lanes))] * pairs
        + [("v", (2, slabs, epochs * stamp, lanes)), ("v", images.shape), ("v", plan.ahead.shape, bf16)],
        [("s", place), ("m", index), ("m", flux), ("m", noise), ("m", bank), ("m", plan.coef),
         ("m", images), ("m", plan.ahead)],
        [pltpu.SMEM(index.shape, jnp.int32), pltpu.SMEM(flux.shape, f32), pltpu.SMEM(noise.shape, f32),
         pltpu.VMEM(bank.shape, f32), pltpu.VMEM(plan.coef.shape, f32)]
        + coadd_scratch(plan, epochs) + [pltpu.SemaphoreType.DMA((7,))],
        micros=4.5,
    )
    return list(flat[:pairs]), *flat[pairs:]


def row_transform_near(plan, place, taps, images, table):
    pairs = plan.pairs

    def kernel(place_ref, taps_ref, x_ref, table_ref, *rest):
        coadd_rows(plan, place_ref[0], 0, x_ref, table_ref, taps_ref, *rest[pairs:], rest[:pairs])

    return list(call(
        kernel,
        [("v", (plan.tall, plan.lanes))] * pairs,
        [("s", place), ("v", taps), ("v", images), ("v", table)],
        coadd_scratch(plan, images.shape[0]),
        micros=3.2,
    ))


def row_transform(plan, place, images, table):
    slabs, pairs, lanes = plan.slabs, plan.pairs, plan.lanes

    def kernel(place_ref, x_ref, table_ref, *outs):
        for group in range(2):
            data, table = row_operands(plan, place_ref[0], group, x_ref, table_ref)
            result = mul3(table, data, True)
            for m in range(pairs):
                outs[group * pairs + m][...] = result[m * lanes : (m + 1) * lanes]

    return list(call(
        kernel,
        [("v", (lanes, images.shape[0] * plan.rows))] * slabs,
        [("s", place), ("v", images), ("v", table)],
        micros=1.3,
    ))


def numerator(plan, place, index, flux, noise, blocks, pieces):
    slabs, cols, rows, half, side, lanes, halo, tall = (
        plan.slabs, plan.cols, plan.rows, plan.half, plan.side, plan.lanes, plan.halo, plan.tall,
    )
    epochs = index.shape[0]
    piece = side // pieces

    def kernel(place_ref, index_ref, flux_ref, noise_ref, *rest):
        ins, table_ref = rest[:slabs], rest[slabs]
        outs = rest[slabs + 1 : slabs + 1 + pieces]
        whole, parts = rest[slabs + 1 + pieces :]
        q, z = place_ref[0], place_ref[1] if pieces > 1 else 0
        whole[...] = jnp.zeros((side + 2 * halo, lanes), f32)
        for m in range(slabs):
            at = pl.multiple_of((q ^ m) * rows, rows)
            whole[pl.ds(at, tall)] += ins[slabs - 1 - m][...]
        whole[side : side + halo] += whole[:halo]
        whole[halo : 2 * halo] += whole[side + halo :]
        top, bottom = whole[halo : halo + half], whole[halo + half : halo + side]
        row = lax.broadcasted_iota(jnp.int32, (cols, half), 0)
        first = (q == 0).astype(f32)
        keep = 1.0 - first * (row == 0).astype(f32)
        line = lax.broadcasted_iota(jnp.int32, (edge_rows, half), 0)
        for odd in range(2):
            value = (top - bottom if odd else top + bottom).T
            re, im = value[:cols], value[cols:]
            edge = jnp.broadcast_to(im[:1] * first, (edge_rows, half))
            im = im * keep
            left = jnp.concatenate(
                [
                    jnp.concatenate([re, im, jnp.where(line == 0, edge, 0.0)], 0),
                    jnp.concatenate([im, -re, jnp.where(line == 1, -edge, 0.0)], 0),
                ],
                1,
            )
            table = [
                jnp.concatenate([table_ref[n, odd, kind].reshape(half, half) for kind in range(2)], 0)
                for n in range(2)
            ]
            plane = mul3(split(left), table)[: lanes + 8]
            step = min(piece, half)
            for i in range(half // step):
                at = odd * half + i * step
                parts[at // piece, :, at % piece : at % piece + step] = plane[:, i * step : (i + 1) * step]
        lane = lax.broadcasted_iota(jnp.int32, (1, piece), 1)
        shares = jnp.zeros((1, piece), f32)
        for e in range(epochs):
            ratio = flux_ref[e] / noise_ref[e]
            shares += jnp.where(lane == index_ref[e], ratio * ratio, 0.0)
        for m in range(pieces):
            parts[m, lanes + 2 : lanes + 3] = shares
        for m in range(pieces):
            outs[m][...] = parts[z ^ m]

    return call(
        kernel,
        [("v", (lanes + 8, piece))] * pieces,
        [("s", place), ("s", index), ("s", flux), ("s", noise)] + [("v", b) for b in reversed(blocks)]
        + [("v", plan.down)],
        [pltpu.VMEM((side + 2 * halo, lanes), f32), pltpu.VMEM((pieces, lanes + 8, piece), f32)],
        micros=1.15,
    )


def psf_planes(plan, place, bank, index):
    epochs = index.shape[0]
    count, stamp = bank.shape[:2]
    side, cols, band, slabs, lanes = plan.side, plan.cols, plan.band, plan.slabs, plan.lanes
    body = epochs * cols
    size = body + edge_rows
    pitch = 8 * stamp

    def kernel(
        place_ref, index_ref, bank_ref, shift_ref, spread_ref, coef_ref,
        spectrum_ref, power_ref, taps_ref, right_ref, plane_ref,
    ):
        q = place_ref[0]
        stamps = bank_ref[...]
        stamps = stamps / jnp.sum(jnp.sum(stamps, axis=2, keepdims=True), axis=1, keepdims=True)
        blank = jnp.zeros((stamp, stamp), f32)
        for k in range(count):
            pair = jnp.concatenate(
                [jnp.concatenate([stamps[k], blank], 1), jnp.concatenate([blank, stamps[k]], 1)], 0
            )
            for copy in range(4):
                at = k * pitch + copy * 2 * stamp
                right_ref[at : at + 2 * stamp] = pair
        right = split(right_ref[...])
        mixed = mul3((shift_ref[0, q], shift_ref[1, q]), right, True)
        lane = lax.broadcasted_iota(jnp.int32, mixed.shape, 1) % pitch
        middle = (lane >= 2 * stamp) & (lane < 4 * stamp)
        high = mixed.astype(bf16).astype(f32)
        left = jnp.where(middle, mixed - high, high).astype(bf16)
        for k in range(count):
            plane = mul(left[:, k * pitch : (k + 1) * pitch], spread_ref[...])
            plane_ref[k] = plane
            power_ref[k] = plane[:band] * plane[:band] + plane[band:] * plane[band:]
        for e in range(epochs):
            k = index_ref[e]
            for base, start in ((0, 0), (size, band)):
                value = plane_ref[k, start : start + band]
                spectrum_ref[base + e * cols : base + (e + 1) * cols] = value[:cols]
                spectrum_ref[base + body + e : base + body + e + 1] = value[cols : cols + 1]
        none = jnp.zeros((edge_rows - epochs, side), f32)
        spectrum_ref[body + epochs : size] = none
        spectrum_ref[size + body + epochs :] = none
        filter_taps(
            plan, bank_ref, coef_ref, index_ref, epochs,
            lambda e, own: own / jnp.sum(own * own, keepdims=True), taps_ref,
        )

    return call(
        kernel,
        [("v", (2 * size, side)), ("v", (count, band, side)), ("v", (2, slabs, epochs * stamp, lanes))],
        [("s", place), ("s", index), ("v", bank), ("v", plan.shift), ("v", plan.spread), ("v", plan.coef)],
        [pltpu.VMEM((count * pitch, 2 * stamp), f32), pltpu.VMEM((count, 2 * band, side), f32)],
        micros=2.35,
    )


def filter_gains(plan, flux, noise, share, spectrum, power):
    epochs = flux.shape[0]
    count = power.shape[0]
    side, cols = plan.side, plan.cols
    body = epochs * cols
    size = body + edge_rows
    row = plan.lanes + 2

    def kernel(flux_ref, noise_ref, share_ref, spectrum_ref, power_ref, gain_ref, cross_ref):
        shares = [jnp.broadcast_to(share_ref[row : row + 1, k : k + 1], (8, side)) for k in range(count)]
        none = jnp.zeros((edge_rows - epochs, side), f32)
        gain_ref[body + epochs : size] = none
        cross_ref[body + epochs : size] = none
        cross_ref[size + body + epochs :] = none
        for block in range(plan.band // 8):
            total = jnp.full((8, side), reg_floor, f32)
            for k in range(count):
                total += shares[k] * power_ref[k, block * 8 : block * 8 + 8]
            edge = block == cols // 8
            total = total[:1] if edge else total
            lines = 1 if edge else 8
            root = jnp.sqrt(total)
            inverse_root = 1.0 / root
            for e in range(epochs):
                at = body + e if edge else e * cols + block * 8
                re = spectrum_ref[at : at + lines]
                im = spectrum_ref[size + at : size + at + lines]
                scale, sigma = flux_ref[e], noise_ref[e]
                inverse = lax.rsqrt(
                    sigma * sigma * total + scale * scale * (re * re + im * im) + reg_floor
                )
                ratio = scale * inverse * inverse_root
                gain_ref[at : at + lines] = root * inverse
                cross_ref[at : at + lines] = ratio * re
                cross_ref[size + at : size + at + lines] = ratio * im

    return call(
        kernel,
        [("v", (size, side)), ("v", (2 * size, side))],
        [("s", flux), ("s", noise), ("v", share), ("v", spectrum), ("v", power)],
        micros=1.15,
    )


def column_transform(plan, place, blocks):
    slabs, pairs, cols, rows, half, side = plan.slabs, plan.pairs, plan.cols, plan.rows, plan.half, plan.side
    epochs = blocks[0].shape[1] // rows
    body = epochs * cols
    size = body + edge_rows

    def kernel(place_ref, *rest):
        ins = rest[:slabs]
        table_ref, plane_ref, left_high, left_low = rest[slabs:]
        q = place_ref[0]
        first = (q == 0).astype(f32)
        sign = jnp.where(q < pairs, 1.0, -1.0).astype(f32)
        row = lax.broadcasted_iota(jnp.int32, (cols, rows), 0)
        keep = 1.0 - first * (row == 0).astype(f32)

        def put(row_at, lane_at, entry):
            where = (slice(row_at, row_at + entry.shape[0]), slice(lane_at, lane_at + rows))
            left_high[where], left_low[where] = split(entry)

        for odd in range(2):
            for m in range(pairs):
                near, far = ins[m][...], ins[m + pairs][...]
                value = sign * (near - far) if odd else near + far
                edges = []
                for e in range(epochs):
                    re = value[:cols, e * rows : (e + 1) * rows]
                    im = value[cols:, e * rows : (e + 1) * rows]
                    edges.append(im[:1] * first)
                    im = im * keep
                    put(e * cols, m * rows, re)
                    put(e * cols, half + m * rows, im)
                    put(size + e * cols, m * rows, im)
                    put(size + e * cols, half + m * rows, -re)
                edge = jnp.concatenate(edges + [jnp.zeros((edge_rows - epochs, rows), f32)], 0)
                put(body, m * rows, edge)
                put(body, half + m * rows, jnp.zeros_like(edge))
                put(size + body, m * rows, jnp.zeros_like(edge))
                put(size + body, half + m * rows, -edge)
            order = [(q ^ m) % pairs for m in range(pairs)]
            table = [
                jnp.concatenate([table_ref[n, odd, kind, i] for kind in range(2) for i in order], 0)
                for n in range(2)
            ]
            plane_ref[:, odd * half : (odd + 1) * half] = mul3((left_high[...], left_low[...]), table)

    (plane,) = call(
        kernel,
        [("v", (2 * size, side))],
        [("s", place)] + [("v", b) for b in blocks] + [("v", plan.down)],
        [pltpu.VMEM((2 * size, side), bf16), pltpu.VMEM((2 * size, side), bf16)],
        micros=1.85,
    )
    return plane


def column_inverse(plan, place, spectrum, gain, cross, numer, begin, end):
    slabs, cols, rows, half, side, lanes, halo, tall = (
        plan.slabs, plan.cols, plan.rows, plan.half, plan.side, plan.lanes, plan.halo, plan.tall,
    )
    size = gain.shape[0]
    body = size - edge_rows
    epochs = end - begin
    pieces = len(numer)
    piece = side // pieces

    def kernel(place_ref, spectrum_ref, gain_ref, cross_ref, *rest):
        numer_refs, table_ref = rest[:pieces], rest[pieces]
        outs = rest[pieces + 1 : pieces + 1 + slabs]
        whole, right_high, right_low, planes = rest[pieces + 1 + slabs :]
        q, z = place_ref[0], place_ref[1] if pieces > 1 else 0
        for m in range(pieces):
            whole[z ^ m] = numer_refs[m][...]
        flag = jnp.broadcast_to(q, (cols, half)) == 0
        packed = flag & (lax.broadcasted_iota(jnp.int32, (cols, half), 0) == 0)
        results = []
        for odd in range(2):
            here = slice(odd * half, (odd + 1) * half)
            step = min(piece, half)
            parts = [
                whole[at // piece, :, at % piece : at % piece + step]
                for at in range(odd * half, (odd + 1) * half, step)
            ]
            numer_all = parts[0] if len(parts) == 1 else jnp.concatenate(parts, 1)

            def difference(start, stop, nre, nim):
                gain_, cre = gain_ref[start:stop, here], cross_ref[start:stop, here]
                cim = cross_ref[size + start : size + stop, here]
                re = gain_ * spectrum_ref[start:stop, here] - (cre * nre - cim * nim)
                im = gain_ * spectrum_ref[size + start : size + stop, here] - (cre * nim + cim * nre)
                return re, im

            edge_re, edge_im = difference(
                body, size, numer_all[lanes : lanes + 1], numer_all[lanes + 1 : lanes + 2]
            )
            for i in range(epochs):
                e = begin + i
                re, im = difference(e * cols, (e + 1) * cols, numer_all[:cols], numer_all[cols:lanes])
                im_left = jnp.where(packed, edge_re[e : e + 1], im)
                im_right = jnp.where(packed, -edge_im[e : e + 1], re)
                for base, start, entry in (
                    (0, 0, re), (0, half, -im), (cols, 0, im_left), (cols, half, im_right),
                ):
                    where = (
                        slice(i * lanes + base, i * lanes + base + cols),
                        slice(start, start + half),
                    )
                    right_high[where], right_low[where] = split(entry)
            results.append(
                mul3((table_ref[0, odd], table_ref[1, odd]), (right_high[...], right_low[...]), True)
            )
        planes[halo : halo + half] = results[0] + results[1]
        planes[halo + half : halo + side] = results[0] - results[1]
        planes[:halo] = planes[side : side + halo]
        planes[halo + side :] = planes[halo : 2 * halo]
        for m in range(slabs):
            start = pl.multiple_of((q ^ m) * rows, rows)
            for i in range(epochs):
                outs[m][i] = planes[pl.ds(start, tall), i * lanes : (i + 1) * lanes]

    return call(
        kernel,
        [("v", (epochs, tall, lanes))] * slabs,
        [("s", place), ("v", spectrum), ("v", gain), ("v", cross)] + [("v", n) for n in numer]
        + [("v", plan.up)],
        [pltpu.VMEM((pieces, lanes + 8, piece), f32),
         pltpu.VMEM((epochs * lanes, side), bf16), pltpu.VMEM((epochs * lanes, side), bf16),
         pltpu.VMEM((side + 2 * halo, epochs * lanes), f32)],
        micros=1.35,
    )


def row_inverse(plan, place, blocks, taps, begin, epochs, difference, earlier, src_row, src_col):
    slabs, pairs, rows, half, side, lanes, halo, stamp = (
        plan.slabs, plan.pairs, plan.rows, plan.half, plan.side, plan.lanes, plan.halo, plan.stamp,
    )
    mine = blocks[0].shape[0]
    groups, group = src_row.shape
    each = groups // slabs
    total = mine * rows
    step = min(64, rows)
    last = begin + mine == epochs
    count = slabs if last else 1
    flux_shapes = [("v", (epochs, each * group))] * slabs if last else [("v", (slabs, begin + mine, each * group))]

    def kernel(place_ref, row_ref, col_ref, taps_ref, *rest):
        ins, table_ref = rest[:slabs], rest[slabs]
        rest = rest[slabs + 1 :]
        if difference is not None:
            earlier_ref, rest = rest[1], rest[2:]
        diff_ref, outs = rest[0], rest[1 : 1 + count]
        left_high, left_low, image_ref, flux_ref, picked, sem = rest[1 + count :]
        q = place_ref[0]
        for m in range(slabs):
            d = q ^ m
            here = slice(m * lanes, (m + 1) * lanes)
            for i in range(mine):
                base = i * rows
                left_high[base : base + rows, here], left_low[base : base + rows, here] = split(
                    ins[m][i, halo : halo + rows, :]
                )
                for start in range(0, rows, step):
                    straight = jnp.zeros((step, lanes), f32)
                    crossed = jnp.zeros((step, lanes), f32)
                    for a in range(stamp):
                        value = ins[m][i, start + a : start + a + step, :]
                        at = (begin + i) * stamp + a
                        straight += taps_ref[0, d, at : at + 1] * value
                        crossed += taps_ref[1, d, at : at + 1] * value
                    at = total + base + start
                    left_high[at : at + step, here], left_low[at : at + step, here] = split(
                        straight + swap_halves(plan, crossed)
                    )

        sums = []
        for side_ in range(2):
            members = [side_ * pairs + m for m in range(pairs)]
            table = [jnp.concatenate([table_ref[n, q ^ m] for m in members], 0) for n in range(2)]
            here = slice(side_ * pairs * lanes, (side_ + 1) * pairs * lanes)
            sums.append(mul3((left_high[:, here], left_low[:, here]), table))
        sign = jnp.where(q < pairs, 1.0, -1.0).astype(f32)
        for lane_half in range(2):
            value = sums[0] + sums[1] if lane_half == 0 else sign * (sums[0] - sums[1])
            here = slice(lane_half * half, (lane_half + 1) * half)
            image_ref[:, :, here] = value[:total].reshape(mine, rows, half)
            flux_ref[:total, here], flux_ref[total:, here] = split(value[total:])
        copy = pltpu.make_async_copy(image_ref, diff_ref.at[pl.ds(begin, mine)], sem)
        copy.start()
        column = lax.broadcasted_iota(jnp.int32, (side, group), 0)
        line = lax.broadcasted_iota(jnp.int32, (rows, group), 0)
        for g in range(groups):
            chosen = (column == col_ref[g : g + 1]).astype(f32).astype(bf16)
            values = mul(flux_ref[...], chosen)
            values = values[:total] + values[total:]
            inside = line == row_ref[g : g + 1] - q * rows
            found = [
                jnp.sum(
                    jnp.where(inside, values[e * rows : (e + 1) * rows], 0.0), axis=0, keepdims=True
                )
                for e in range(mine)
            ]
            where = (g % each) * group
            picked[g // each, :, where : where + group] = jnp.concatenate(found, 0)
        for m in range(slabs):
            out = outs[m] if last else outs[0].at[m]
            owner = q ^ m if last else m
            if begin:
                out[:begin] = earlier_ref[owner]
            out[begin:] = picked[owner]
        copy.wait()

    ins = [("s", place), ("v", src_row), ("v", src_col), ("v", taps)]
    ins += [("v", b) for b in blocks] + [("v", plan.back)]
    aliases = {}
    if difference is not None:
        aliases = {len(ins): 0}
        ins += [("h", difference), ("v", earlier)]
    left = pltpu.VMEM((2 * total, side), bf16)
    return call(
        kernel,
        [("h", (epochs, rows, side))] + flux_shapes,
        ins,
        [left, left, pltpu.VMEM((mine, rows, side), f32), left,
         pltpu.VMEM((slabs, mine, each * group), f32), pltpu.SemaphoreType.DMA(())],
        aliases=aliases,
        micros=5.4,
    )


def trade(parts, axes, count):
    result = list(parts)
    for m in reversed(range(1, count)):
        result[m] = lax.ppermute(parts[m], axes, [(i, i ^ m) for i in range(count)])
    return result


def make_shards(mesh):
    slabs = mesh.shape["tile"] * mesh.shape["sub"]
    ranks = mesh.shape["epoch"]
    slab_axes = ("tile", "sub")

    def shards(epoch_images, psf_bank, psf_index, flux_scale, noise_level, src_row, src_col):
        epochs, rows, side = epoch_images.shape
        plan = Plan(side, slabs, psf_bank.shape[1])
        place = jnp.stack([lax.axis_index(slab_axes), lax.axis_index("epoch")]).astype(jnp.int32)
        direct = ranks & (ranks - 1) == 0 and side // ranks % 128 == 0
        pieces = ranks if direct else 1
        group = math.gcd(512, src_row.shape[0] // slabs)
        scalars = (psf_index, flux_scale, noise_level)

        far, weighted, images, table = row_transform_far(plan, place, *scalars, epoch_images, psf_bank)
        near = row_transform_near(plan, place, weighted, images, table)
        blocks = row_transform(plan, place, images, table)
        numer = trade(near + far, slab_axes, slabs)
        numer = numerator(plan, place, *scalars, numer, pieces)
        bank, numer = lax.optimization_barrier((psf_bank, numer))
        spectrum, power, taps = psf_planes(plan, place, bank, psf_index)
        blocks = trade(blocks, slab_axes, slabs)
        if direct:
            own = sum(trade(numer, "epoch", ranks))
            numer = trade([own] * ranks, "epoch", ranks)
        else:
            own = lax.psum(numer[0], "epoch")
            numer = [own]
        images = column_transform(plan, place, blocks)
        gain, cross = filter_gains(plan, flux_scale, noise_level, own, spectrum, power)

        parties = [0]
        while parties[-1] < epochs:
            parties.append(min(parties[-1] + 2, epochs))
        parties = list(zip(parties, parties[1:]))
        returned = [
            trade(
                column_inverse(plan, place, images, gain, cross, numer, begin, end), slab_axes, slabs
            )
            for begin, end in parties
        ]
        difference, picked = None, [None]
        for i, (begin, _) in enumerate(parties):
            difference, *picked = row_inverse(
                plan, place, returned[i], taps, begin, epochs, difference, picked[0],
                src_row.reshape(-1, group), src_col.reshape(-1, group),
            )
        return difference, sum(trade(picked, slab_axes, slabs))

    return shards


def solution(mesh):
    in_specs = (
        P(("grp", "epoch"), ("tile", "sub"), None),
        P(),
        P(("grp", "epoch")),
        P(("grp", "epoch")),
        P(("grp", "epoch")),
        P("grp"),
        P("grp"),
    )
    out_specs = (P(("grp", "epoch"), ("tile", "sub"), None), P(("grp", "epoch"), ("tile", "sub")))
    return jax.shard_map(
        make_shards(mesh), mesh=mesh, in_specs=in_specs, out_specs=out_specs, check_vma=False
    )
```

```python
import math

import jax
import jax.numpy as jnp
import ml_dtypes
import numpy as np
from jax import lax
from jax.experimental import pallas as pl
from jax.experimental.pallas import tpu as pltpu
from jax.sharding import PartitionSpec as P

reg_floor = 0.01
vmem_limit = 40 * 1024 * 1024
bf16, f32 = jnp.bfloat16, jnp.float32
hbm_rate = 3.69e6
edge_rows = 16


def halves(table):
    table = np.asarray(table, np.float64)
    high = table.astype(ml_dtypes.bfloat16)
    return np.stack([high, (table - high.astype(np.float64)).astype(ml_dtypes.bfloat16)])


def split(value):
    high = value.astype(bf16)
    return high, (value - high.astype(f32)).astype(bf16)


def angle(first, second, length):
    return np.outer(first, second) % length * (2.0 * math.pi / length)


def mul(left, right, transposed=False):
    dims = (((1,), (1,)), ((), ())) if transposed else (((1,), (0,)), ((), ()))
    return lax.dot_general(left, right, dims, preferred_element_type=f32)


def mul3(left, right, transposed=False):
    return (
        mul(left[0], right[0], transposed)
        + mul(left[1], right[0], transposed)
        + mul(left[0], right[1], transposed)
    )


class Plan:
    def __init__(self, side, slabs, stamp):
        self.side, self.slabs, self.stamp = side, slabs, stamp
        half = self.half = side // 2
        cols = self.cols = half // slabs
        lanes = self.lanes = 2 * cols
        rows = self.rows = side // slabs
        pairs = self.pairs = slabs // 2
        self.halo = stamp // 2
        self.tall = rows + 2 * self.halo
        self.band = cols + 8
        owner = np.arange(slabs)[:, None]
        freq = 2 * (cols * (owner % pairs) + np.arange(cols)[None, :]) + owner // pairs
        short = np.arange(half)
        taps = np.arange(stamp) - stamp // 2
        order = np.concatenate([2 * short, 2 * short + 1])

        ahead = np.zeros((slabs, 2, cols, half))
        back = np.zeros((slabs, 2, cols, half))
        coef = np.zeros((stamp, 2, slabs, 2, cols))
        shift = np.zeros((slabs, 2, self.band, 2, stamp))
        for d in range(slabs):
            th = angle(freq[d], short, side)
            ahead[d, 0], ahead[d, 1] = np.cos(th), -np.sin(th)
            back[d, 0], back[d, 1] = 2 * np.cos(th) / side, -2 * np.sin(th) / side
            tb = angle(taps, freq[d], side)
            coef[:, 0, d, 0] = coef[:, 0, d, 1] = np.cos(tb)
            coef[:, 1, d, 0], coef[:, 1, d, 1] = np.sin(tb), -np.sin(tb)
            te = angle(np.concatenate([freq[d], [half]]), taps, side)
            ce, se = np.cos(te), np.sin(te)
            shift[d, 0, : cols + 1, 0], shift[d, 0, : cols + 1, 1] = ce, -se
            shift[d, 1, : cols + 1, 0], shift[d, 1, : cols + 1, 1] = -se, -ce
        nyquist = np.cos(math.pi * short)
        ahead[0, 1, 0] = nyquist
        back[0, 0, 0], back[0, 1, 0] = 1.0 / side, nyquist / side
        coef[:, 0, 0, 1, 0], coef[:, 1, 0, 1, 0] = np.cos(math.pi * taps), 0.0
        self.ahead = halves(ahead.reshape(slabs, lanes, half))
        self.back = halves(back.reshape(slabs, lanes, half))
        self.coef = coef.reshape(stamp, 2 * slabs * lanes).astype(np.float32)
        self.shift = halves(shift.reshape(slabs, 2 * self.band, 2 * stamp))

        down = np.zeros((2, 2, half, half))
        up = np.zeros((2, half, 2 * half))
        for odd in range(2):
            th = angle(short, 2 * short + odd, side)
            down[odd, 0], down[odd, 1] = np.cos(th), np.sin(th)
            up[odd, :, :half], up[odd, :, half:] = np.cos(th) / side, np.sin(th) / side
        self.down = halves(down.reshape(2, 2, pairs, rows, half))
        self.up = halves(up)
        tu = angle(taps, order, side)
        high, low = halves(np.concatenate([np.cos(tu), np.sin(tu)], 0))
        self.spread = np.concatenate([high, high, low, np.zeros_like(high)], 0)


def call(kernel, outs, ins, scratch=(), aliases=None, micros=0.0):
    space = {"s": pltpu.SMEM, "v": pltpu.VMEM, "h": pl.ANY, "m": pltpu.HBM}
    ins = [
        (kind, pltpu.with_memory_space_constraint(jnp.asarray(a), pltpu.HBM) if kind == "m" else a)
        for kind, a in ins
    ]
    return pl.pallas_call(
        kernel,
        out_shape=tuple(jax.ShapeDtypeStruct(shape, (*kind, f32)[0]) for _, shape, *kind in outs),
        in_specs=[pl.BlockSpec(memory_space=space[kind]) for kind, _ in ins],
        out_specs=tuple(pl.BlockSpec(memory_space=space[out[0]]) for out in outs),
        scratch_shapes=list(scratch),
        input_output_aliases=aliases or {},
        compiler_params=pltpu.CompilerParams(vmem_limit_bytes=vmem_limit),
        cost_estimate=pl.CostEstimate(flops=0, bytes_accessed=int(micros * hbm_rate), transcendentals=0),
    )(*[a for _, a in ins])


def filter_taps(plan, bank_ref, coef_ref, index_ref, epochs, factor, taps_ref):
    stamp, slabs, lanes = plan.stamp, plan.slabs, plan.lanes
    filters = []
    for e in range(epochs):
        own = bank_ref[index_ref[e]]
        own = own / jnp.sum(own, keepdims=True)
        filters.append(factor(e, own))
    taps = jnp.dot(
        jnp.concatenate(filters, 0), coef_ref[...],
        precision=lax.Precision.HIGHEST, preferred_element_type=f32,
    )
    for kind in range(2):
        for d in range(slabs):
            start = (kind * slabs + d) * lanes
            taps_ref[kind, d] = taps[:, start : start + lanes]


def swap_halves(plan, value):
    return jnp.concatenate([value[:, plan.cols :], value[:, : plan.cols]], 1)


def owners_of(plan, q, group):
    return [q ^ (group * plan.pairs + m) for m in range(plan.pairs)]


def row_operands(plan, q, group, x_ref, table_ref):
    half = plan.half
    x = x_ref[...].reshape(-1, 2 * half)
    first, second = x[:, :half], x[:, half:]
    sign = jnp.where((q >= plan.pairs) != (group == 1), -1.0, 1.0).astype(f32)
    data = split(first + sign * second)
    table = [
        jnp.concatenate([table_ref[n, d] for d in owners_of(plan, q, group)], 0) for n in range(2)
    ]
    return data, table


def coadd_rows(plan, q, group, x_ref, table_ref, taps_ref, padded, gathered, outs):
    rows, lanes, tall, stamp, pairs = plan.rows, plan.lanes, plan.tall, plan.stamp, plan.pairs
    epochs = x_ref.shape[0]
    step = tall // 2
    padded[:, :, :stamp] = jnp.zeros((pairs, epochs, stamp, lanes), f32)
    padded[:, :, stamp + rows :] = jnp.zeros((pairs, epochs, stamp, lanes), f32)
    data, table = row_operands(plan, q, group, x_ref, table_ref)
    upright = mul3(data, table, True)
    for m in range(pairs):
        for e in range(epochs):
            padded[m, e, stamp : stamp + rows] = upright[
                e * rows : (e + 1) * rows, m * lanes : (m + 1) * lanes
            ]

    @pl.loop(0, pairs)
    def _(m):
        d = q ^ (group * pairs + m)
        for start in range(0, tall, step):
            straight = jnp.zeros((step, lanes), f32)
            crossed = jnp.zeros((step, lanes), f32)
            for e in range(epochs):
                for shift in range(8):
                    shifted = padded[m, e, start + shift : start + shift + step + stamp - 8, :]
                    for base in range(0, stamp, 8):
                        value = shifted[base : base + step]
                        at = e * stamp + base + shift
                        straight += taps_ref[0, d, at : at + 1] * value
                        crossed += taps_ref[1, d, at : at + 1] * value
            gathered[m, start : start + step] = straight + swap_halves(plan, crossed)

    for m in range(pairs):
        outs[m][...] = gathered[m]


def coadd_scratch(plan, epochs):
    return [
        pltpu.VMEM((plan.pairs, epochs, plan.rows + 2 * plan.stamp, plan.lanes), f32),
        pltpu.VMEM((plan.pairs, plan.tall, plan.lanes), f32),
    ]


def row_transform_far(plan, place, index, flux, noise, images, bank):
    epochs = images.shape[0]
    slabs, pairs, lanes, tall, stamp = plan.slabs, plan.pairs, plan.lanes, plan.tall, plan.stamp

    def kernel(place_ref, *rest):
        sources, outs, rest = rest[:7], rest[7 : 7 + pairs], rest[7 + pairs :]
        taps_ref, x_ref, table_ref, index_ref, flux_ref, noise_ref, bank_ref, coef_ref = rest[:8]
        padded, gathered, sems = rest[8:]
        targets = [index_ref, flux_ref, noise_ref, bank_ref, coef_ref, x_ref, table_ref]
        copies = [pltpu.make_async_copy(sources[i], targets[i], sems.at[i]) for i in range(7)]
        for copy in copies:
            copy.start()
        for copy in copies[:5]:
            copy.wait()
        filter_taps(
            plan, bank_ref, coef_ref, index_ref, epochs,
            lambda e, own: own * (flux_ref[e] / (noise_ref[e] * noise_ref[e])), taps_ref,
        )
        for copy in copies[5:]:
            copy.wait()
        coadd_rows(plan, place_ref[0], 1, x_ref, table_ref, taps_ref, padded, gathered, outs)

    flat = call(
        kernel,
        [("v", (tall, lanes))] * pairs
        + [("v", (2, slabs, epochs * stamp, lanes)), ("v", images.shape), ("v", plan.ahead.shape, bf16)],
        [("s", place), ("m", index), ("m", flux), ("m", noise), ("m", bank), ("m", plan.coef),
         ("m", images), ("m", plan.ahead)],
        [pltpu.SMEM(index.shape, jnp.int32), pltpu.SMEM(flux.shape, f32), pltpu.SMEM(noise.shape, f32),
         pltpu.VMEM(bank.shape, f32), pltpu.VMEM(plan.coef.shape, f32)]
        + coadd_scratch(plan, epochs) + [pltpu.SemaphoreType.DMA((7,))],
        micros=4.5,
    )
    return list(flat[:pairs]), *flat[pairs:]


def row_transform_near(plan, place, taps, images, table):
    pairs = plan.pairs

    def kernel(place_ref, taps_ref, x_ref, table_ref, *rest):
        coadd_rows(plan, place_ref[0], 0, x_ref, table_ref, taps_ref, *rest[pairs:], rest[:pairs])

    return list(call(
        kernel,
        [("v", (plan.tall, plan.lanes))] * pairs,
        [("s", place), ("v", taps), ("v", images), ("v", table)],
        coadd_scratch(plan, images.shape[0]),
        micros=3.2,
    ))


def row_transform(plan, place, images, table, parties):
    slabs, pairs, lanes, rows = plan.slabs, plan.pairs, plan.lanes, plan.rows

    def kernel(place_ref, x_ref, table_ref, *outs):
        for group in range(2):
            data, table = row_operands(plan, place_ref[0], group, x_ref, table_ref)
            result = mul3(table, data, True)
            for i, (begin, end) in enumerate(parties):
                for m in range(pairs):
                    outs[i * slabs + group * pairs + m][...] = result[
                        m * lanes : (m + 1) * lanes, begin * rows : end * rows
                    ]

    flat = call(
        kernel,
        [("v", (lanes, (end - begin) * rows)) for begin, end in parties for _ in range(slabs)],
        [("s", place), ("v", images), ("v", table)],
        micros=1.3,
    )
    return [list(flat[i * slabs : (i + 1) * slabs]) for i in range(len(parties))]


def numerator(plan, place, index, flux, noise, blocks, pieces):
    slabs, cols, rows, half, side, lanes, halo, tall = (
        plan.slabs, plan.cols, plan.rows, plan.half, plan.side, plan.lanes, plan.halo, plan.tall,
    )
    epochs = index.shape[0]
    piece = side // pieces

    def kernel(place_ref, index_ref, flux_ref, noise_ref, *rest):
        ins, table_ref = rest[:slabs], rest[slabs]
        outs = rest[slabs + 1 : slabs + 1 + pieces]
        whole, parts = rest[slabs + 1 + pieces :]
        q, z = place_ref[0], place_ref[1] if pieces > 1 else 0
        whole[...] = jnp.zeros((side + 2 * halo, lanes), f32)
        for m in range(slabs):
            at = pl.multiple_of((q ^ m) * rows, rows)
            whole[pl.ds(at, tall)] += ins[slabs - 1 - m][...]
        whole[side : side + halo] += whole[:halo]
        whole[halo : 2 * halo] += whole[side + halo :]
        top, bottom = whole[halo : halo + half], whole[halo + half : halo + side]
        row = lax.broadcasted_iota(jnp.int32, (cols, half), 0)
        first = (q == 0).astype(f32)
        keep = 1.0 - first * (row == 0).astype(f32)
        line = lax.broadcasted_iota(jnp.int32, (edge_rows, half), 0)
        for odd in range(2):
            value = (top - bottom if odd else top + bottom).T
            re, im = value[:cols], value[cols:]
            edge = jnp.broadcast_to(im[:1] * first, (edge_rows, half))
            im = im * keep
            left = jnp.concatenate(
                [
                    jnp.concatenate([re, im, jnp.where(line == 0, edge, 0.0)], 0),
                    jnp.concatenate([im, -re, jnp.where(line == 1, -edge, 0.0)], 0),
                ],
                1,
            )
            table = [
                jnp.concatenate([table_ref[n, odd, kind].reshape(half, half) for kind in range(2)], 0)
                for n in range(2)
            ]
            plane = mul3(split(left), table)[: lanes + 8]
            step = min(piece, half)
            for i in range(half // step):
                at = odd * half + i * step
                parts[at // piece, :, at % piece : at % piece + step] = plane[:, i * step : (i + 1) * step]
        lane = lax.broadcasted_iota(jnp.int32, (1, piece), 1)
        shares = jnp.zeros((1, piece), f32)
        for e in range(epochs):
            ratio = flux_ref[e] / noise_ref[e]
            shares += jnp.where(lane == index_ref[e], ratio * ratio, 0.0)
        for m in range(pieces):
            parts[m, lanes + 2 : lanes + 3] = shares
        for m in range(pieces):
            outs[m][...] = parts[z ^ m]

    return call(
        kernel,
        [("v", (lanes + 8, piece))] * pieces,
        [("s", place), ("s", index), ("s", flux), ("s", noise)] + [("v", b) for b in reversed(blocks)]
        + [("v", plan.down)],
        [pltpu.VMEM((side + 2 * halo, lanes), f32), pltpu.VMEM((pieces, lanes + 8, piece), f32)],
        micros=1.15,
    )


def psf_planes(plan, place, bank, index):
    epochs = index.shape[0]
    count, stamp = bank.shape[:2]
    side, cols, band, slabs, lanes = plan.side, plan.cols, plan.band, plan.slabs, plan.lanes
    body = epochs * cols
    size = body + edge_rows
    pitch = 8 * stamp

    def kernel(
        place_ref, index_ref, bank_ref, shift_ref, spread_ref, coef_ref,
        spectrum_ref, power_ref, taps_ref, right_ref, plane_ref,
    ):
        q = place_ref[0]
        stamps = bank_ref[...]
        stamps = stamps / jnp.sum(jnp.sum(stamps, axis=2, keepdims=True), axis=1, keepdims=True)
        blank = jnp.zeros((stamp, stamp), f32)
        for k in range(count):
            pair = jnp.concatenate(
                [jnp.concatenate([stamps[k], blank], 1), jnp.concatenate([blank, stamps[k]], 1)], 0
            )
            for copy in range(4):
                at = k * pitch + copy * 2 * stamp
                right_ref[at : at + 2 * stamp] = pair
        right = split(right_ref[...])
        mixed = mul3((shift_ref[0, q], shift_ref[1, q]), right, True)
        lane = lax.broadcasted_iota(jnp.int32, mixed.shape, 1) % pitch
        middle = (lane >= 2 * stamp) & (lane < 4 * stamp)
        high = mixed.astype(bf16).astype(f32)
        left = jnp.where(middle, mixed - high, high).astype(bf16)
        for k in range(count):
            plane = mul(left[:, k * pitch : (k + 1) * pitch], spread_ref[...])
            plane_ref[k] = plane
            power_ref[k] = plane[:band] * plane[:band] + plane[band:] * plane[band:]
        for e in range(epochs):
            k = index_ref[e]
            for base, start in ((0, 0), (size, band)):
                value = plane_ref[k, start : start + band]
                spectrum_ref[base + e * cols : base + (e + 1) * cols] = value[:cols]
                spectrum_ref[base + body + e : base + body + e + 1] = value[cols : cols + 1]
        none = jnp.zeros((edge_rows - epochs, side), f32)
        spectrum_ref[body + epochs : size] = none
        spectrum_ref[size + body + epochs :] = none
        filter_taps(
            plan, bank_ref, coef_ref, index_ref, epochs,
            lambda e, own: own / jnp.sum(own * own, keepdims=True), taps_ref,
        )

    return call(
        kernel,
        [("v", (2 * size, side)), ("v", (count, band, side)), ("v", (2, slabs, epochs * stamp, lanes))],
        [("s", place), ("s", index), ("v", bank), ("v", plan.shift), ("v", plan.spread), ("v", plan.coef)],
        [pltpu.VMEM((count * pitch, 2 * stamp), f32), pltpu.VMEM((count, 2 * band, side), f32)],
        micros=2.35,
    )


def filter_gains(plan, flux, noise, share, spectrum, power):
    epochs = flux.shape[0]
    count = power.shape[0]
    side, cols = plan.side, plan.cols
    body = epochs * cols
    size = body + edge_rows
    row = plan.lanes + 2

    def kernel(flux_ref, noise_ref, share_ref, spectrum_ref, power_ref, gain_ref, cross_ref):
        shares = [jnp.broadcast_to(share_ref[row : row + 1, k : k + 1], (8, side)) for k in range(count)]
        none = jnp.zeros((edge_rows - epochs, side), f32)
        gain_ref[body + epochs : size] = none
        cross_ref[body + epochs : size] = none
        cross_ref[size + body + epochs :] = none
        for block in range(plan.band // 8):
            total = jnp.full((8, side), reg_floor, f32)
            for k in range(count):
                total += shares[k] * power_ref[k, block * 8 : block * 8 + 8]
            edge = block == cols // 8
            total = total[:1] if edge else total
            lines = 1 if edge else 8
            root = jnp.sqrt(total)
            inverse_root = 1.0 / root
            for e in range(epochs):
                at = body + e if edge else e * cols + block * 8
                re = spectrum_ref[at : at + lines]
                im = spectrum_ref[size + at : size + at + lines]
                scale, sigma = flux_ref[e], noise_ref[e]
                inverse = lax.rsqrt(
                    sigma * sigma * total + scale * scale * (re * re + im * im) + reg_floor
                )
                ratio = scale * inverse * inverse_root
                gain_ref[at : at + lines] = root * inverse
                cross_ref[at : at + lines] = ratio * re
                cross_ref[size + at : size + at + lines] = ratio * im

    return call(
        kernel,
        [("v", (size, side)), ("v", (2 * size, side))],
        [("s", flux), ("s", noise), ("v", share), ("v", spectrum), ("v", power)],
        micros=1.15,
    )


def column_transform(plan, place, blocks):
    slabs, pairs, cols, rows, half, side = plan.slabs, plan.pairs, plan.cols, plan.rows, plan.half, plan.side
    epochs = blocks[0].shape[1] // rows
    body = epochs * cols
    size = body + edge_rows

    def kernel(place_ref, *rest):
        ins = rest[:slabs][::-1]
        table_ref, plane_ref, left_high, left_low = rest[slabs:]
        q = place_ref[0]
        first = (q == 0).astype(f32)
        sign = jnp.where(q < pairs, 1.0, -1.0).astype(f32)
        row = lax.broadcasted_iota(jnp.int32, (cols, rows), 0)
        keep = 1.0 - first * (row == 0).astype(f32)

        def put(row_at, lane_at, entry):
            where = (slice(row_at, row_at + entry.shape[0]), slice(lane_at, lane_at + rows))
            left_high[where], left_low[where] = split(entry)

        for odd in range(2):
            for m in range(pairs):
                near, far = ins[m][...], ins[m + pairs][...]
                value = sign * (near - far) if odd else near + far
                edges = []
                for e in range(epochs):
                    re = value[:cols, e * rows : (e + 1) * rows]
                    im = value[cols:, e * rows : (e + 1) * rows]
                    edges.append(im[:1] * first)
                    im = im * keep
                    put(e * cols, m * rows, re)
                    put(e * cols, half + m * rows, im)
                    put(size + e * cols, m * rows, im)
                    put(size + e * cols, half + m * rows, -re)
                edge = jnp.concatenate(edges + [jnp.zeros((edge_rows - epochs, rows), f32)], 0)
                put(body, m * rows, edge)
                put(body, half + m * rows, jnp.zeros_like(edge))
                put(size + body, m * rows, jnp.zeros_like(edge))
                put(size + body, half + m * rows, -edge)
            order = [(q ^ m) % pairs for m in range(pairs)]
            table = [
                jnp.concatenate([table_ref[n, odd, kind, i] for kind in range(2) for i in order], 0)
                for n in range(2)
            ]
            plane_ref[:, odd * half : (odd + 1) * half] = mul3((left_high[...], left_low[...]), table)

    (plane,) = call(
        kernel,
        [("v", (2 * size, side))],
        [("s", place)] + [("v", b) for b in reversed(blocks)] + [("v", plan.down)],
        [pltpu.VMEM((2 * size, side), bf16), pltpu.VMEM((2 * size, side), bf16)],
        micros=1.85,
    )
    return plane


def column_inverse(plan, place, spectrum, gain, cross, numer, begin, end):
    slabs, cols, rows, half, side, lanes, halo, tall = (
        plan.slabs, plan.cols, plan.rows, plan.half, plan.side, plan.lanes, plan.halo, plan.tall,
    )
    size = gain.shape[0]
    body = size - edge_rows
    epochs = end - begin
    pieces = len(numer)
    piece = side // pieces

    def kernel(place_ref, spectrum_ref, gain_ref, cross_ref, *rest):
        numer_refs, table_ref = rest[:pieces], rest[pieces]
        outs = rest[pieces + 1 : pieces + 1 + slabs]
        whole, right_high, right_low, planes = rest[pieces + 1 + slabs :]
        q, z = place_ref[0], place_ref[1] if pieces > 1 else 0
        for m in range(pieces):
            whole[z ^ m] = numer_refs[m][...]
        flag = jnp.broadcast_to(q, (cols, half)) == 0
        packed = flag & (lax.broadcasted_iota(jnp.int32, (cols, half), 0) == 0)
        results = []
        for odd in range(2):
            here = slice(odd * half, (odd + 1) * half)
            step = min(piece, half)
            parts = [
                whole[at // piece, :, at % piece : at % piece + step]
                for at in range(odd * half, (odd + 1) * half, step)
            ]
            numer_all = parts[0] if len(parts) == 1 else jnp.concatenate(parts, 1)

            def difference(at, lines, nre, nim):
                gain_, cre = gain_ref[at : at + lines, here], cross_ref[at : at + lines, here]
                cim = cross_ref[size + at : size + at + lines, here]
                mre = spectrum_ref[at : at + lines, here]
                mim = spectrum_ref[size + at : size + at + lines, here]
                return gain_ * mre - (cre * nre - cim * nim), gain_ * mim - (cre * nim + cim * nre)

            for i in range(epochs):
                e = begin + i
                edge_re, edge_im = difference(
                    body + e, 1,
                    numer_all[lanes : lanes + 1], numer_all[lanes + 1 : lanes + 2],
                )
                re, im = difference(e * cols, cols, numer_all[:cols], numer_all[cols:lanes])
                im_left = jnp.where(packed, edge_re, im)
                im_right = jnp.where(packed, -edge_im, re)
                for base, start, entry in (
                    (0, 0, re), (0, half, -im), (cols, 0, im_left), (cols, half, im_right),
                ):
                    where = (
                        slice(i * lanes + base, i * lanes + base + cols),
                        slice(start, start + half),
                    )
                    right_high[where], right_low[where] = split(entry)
            results.append(
                mul3((table_ref[0, odd], table_ref[1, odd]), (right_high[...], right_low[...]), True)
            )
        planes[halo : halo + half] = results[0] + results[1]
        planes[halo + half : halo + side] = results[0] - results[1]
        planes[:halo] = planes[side : side + halo]
        planes[halo + side :] = planes[halo : 2 * halo]
        for m in range(slabs):
            start = pl.multiple_of((q ^ m) * rows, rows)
            for i in range(epochs):
                outs[m][i] = planes[pl.ds(start, tall), i * lanes : (i + 1) * lanes]

    return call(
        kernel,
        [("v", (epochs, tall, lanes))] * slabs,
        [("s", place), ("v", spectrum), ("v", gain), ("v", cross)] + [("v", n) for n in numer]
        + [("v", plan.up)],
        [pltpu.VMEM((pieces, lanes + 8, piece), f32),
         pltpu.VMEM((epochs * lanes, side), bf16), pltpu.VMEM((epochs * lanes, side), bf16),
         pltpu.VMEM((side + 2 * halo, epochs * lanes), f32)],
        micros=1.35,
    )


def column_choice(side, src_col):
    groups, group = src_col.shape

    def kernel(col_ref, out_ref):
        column = lax.broadcasted_iota(jnp.int32, (side, group), 0)

        @pl.loop(0, groups)
        def _(g):
            out_ref[g] = (column == col_ref[pl.ds(g, 1)]).astype(f32).astype(bf16)

    (chosen,) = call(
        kernel, [("v", (groups, side, group), bf16)], [("v", src_col)], micros=2.0
    )
    return chosen


def inverse_rows(plan, q, left, table_ref):
    pairs, lanes = plan.pairs, plan.lanes
    sums = []
    for group in range(2):
        table = [
            jnp.concatenate([table_ref[n, d] for d in owners_of(plan, q, group)], 0) for n in range(2)
        ]
        here = slice(group * pairs * lanes, (group + 1) * pairs * lanes)
        sums.append(mul3((left[0][:, here], left[1][:, here]), table))
    sign = jnp.where(q < pairs, 1.0, -1.0).astype(f32)
    return sums[0] + sums[1], sign * (sums[0] - sums[1])


def row_images(plan, place, returned):
    slabs, rows, half, side, lanes, halo = (
        plan.slabs, plan.rows, plan.half, plan.side, plan.lanes, plan.halo,
    )
    counts = [blocks[0].shape[0] for blocks in returned]
    epochs = sum(counts)

    def kernel(place_ref, *rest):
        ins, table_ref, diff_ref = rest[: -6], rest[-6], rest[-5]
        left_high, left_low, image_ref, sems = rest[-4:]
        q = place_ref[0]
        copies = []
        begin = 0
        for i, count in enumerate(counts):
            total = count * rows
            for m in range(slabs):
                here = slice(m * lanes, (m + 1) * lanes)
                value = ins[i * slabs + m][:, halo : halo + rows, :].reshape(total, lanes)
                left_high[:total, here], left_low[:total, here] = split(value)
            left = (left_high[:total], left_low[:total])
            for part, value in enumerate(inverse_rows(plan, q, left, table_ref)):
                image_ref[begin : begin + count, :, part * half : (part + 1) * half] = value.reshape(
                    count, rows, half
                )
            where = pl.ds(begin, count)
            copies.append(pltpu.make_async_copy(image_ref.at[where], diff_ref.at[where], sems.at[i]))
            copies[-1].start()
            begin += count
        for copy in copies:
            copy.wait()

    left = pltpu.VMEM((max(counts) * rows, side), bf16)
    (difference,) = call(
        kernel,
        [("h", (epochs, rows, side))],
        [("s", place)] + [("v", b) for blocks in returned for b in blocks] + [("v", plan.back)],
        [left, left, pltpu.VMEM((epochs, rows, side), f32), pltpu.SemaphoreType.DMA((len(counts),))],
        micros=2.2,
    )
    return difference


def row_fluxes(plan, place, blocks, taps, begin, epochs, earlier, src_row, chosen):
    slabs, rows, half, side, lanes, stamp = (
        plan.slabs, plan.rows, plan.half, plan.side, plan.lanes, plan.stamp,
    )
    mine = blocks[0].shape[0]
    groups, group = src_row.shape
    each = groups // slabs
    total = mine * rows
    step = min(64, rows)
    last = begin + mine == epochs

    def kernel(place_ref, row_ref, chosen_ref, taps_ref, *rest):
        ins, table_ref = rest[:slabs][::-1], rest[slabs]
        rest = rest[slabs + 1 :]
        if begin:
            earlier_ref, rest = rest[0], rest[1:]
        outs = rest[:-4]
        left_high, left_low, flux_ref, picked = rest[-4:]
        q = place_ref[0]
        for m in range(slabs):
            d = q ^ m
            here = slice(m * lanes, (m + 1) * lanes)
            for i in range(mine):
                for start in range(0, rows, step):
                    straight = jnp.zeros((step, lanes), f32)
                    crossed = jnp.zeros((step, lanes), f32)
                    for shift in range(8):
                        shifted = ins[m][i, start + shift : start + shift + step + stamp - 8, :]
                        for base in range(0, stamp, 8):
                            value = shifted[base : base + step]
                            at = (begin + i) * stamp + base + shift
                            straight += taps_ref[0, d, at : at + 1] * value
                            crossed += taps_ref[1, d, at : at + 1] * value
                    at = i * rows + start
                    left_high[at : at + step, here], left_low[at : at + step, here] = split(
                        straight + swap_halves(plan, crossed)
                    )
        for part, value in enumerate(
            inverse_rows(plan, q, (left_high[...], left_low[...]), table_ref)
        ):
            here = slice(part * half, (part + 1) * half)
            flux_ref[:total, here], flux_ref[total:, here] = split(value)
        line = lax.broadcasted_iota(jnp.int32, (rows, group), 0)
        for g in range(groups):
            values = mul(flux_ref[...], chosen_ref[g])
            values = values[:total] + values[total:]
            inside = line == row_ref[g : g + 1] - q * rows
            found = [
                jnp.sum(
                    jnp.where(inside, values[e * rows : (e + 1) * rows], 0.0), axis=0, keepdims=True
                )
                for e in range(mine)
            ]
            where = (g % each) * group
            picked[g // each, :, where : where + group] = jnp.concatenate(found, 0)
        for m in range(slabs):
            out = outs[m] if last else outs[0].at[m]
            owner = q ^ m if last else m
            if begin:
                out[:begin] = earlier_ref[owner]
            out[begin:] = picked[owner]

    ins = [("s", place), ("v", src_row), ("v", chosen), ("v", taps)]
    ins += [("v", b) for b in reversed(blocks)] + [("v", plan.back)]
    if begin:
        ins.append(("v", earlier))
    left = pltpu.VMEM((total, side), bf16)
    return call(
        kernel,
        [("v", (epochs, each * group))] * slabs if last else [("v", (slabs, begin + mine, each * group))],
        ins,
        [left, left, pltpu.VMEM((2 * total, side), bf16), pltpu.VMEM((slabs, mine, each * group), f32)],
        micros=4.0,
    )


def trade(parts, axes, count):
    result = list(parts)
    for m in reversed(range(1, count)):
        result[m] = lax.ppermute(parts[m], axes, [(i, i ^ m) for i in range(count)])
    return result


def make_shards(mesh):
    slabs = mesh.shape["tile"] * mesh.shape["sub"]
    ranks = mesh.shape["epoch"]
    slab_axes = ("tile", "sub")

    def shards(epoch_images, psf_bank, psf_index, flux_scale, noise_level, src_row, src_col):
        epochs, rows, side = epoch_images.shape
        plan = Plan(side, slabs, psf_bank.shape[1])
        place = jnp.stack([lax.axis_index(slab_axes), lax.axis_index("epoch")]).astype(jnp.int32)
        direct = ranks & (ranks - 1) == 0 and side // ranks % 128 == 0
        pieces = ranks if direct else 1
        group = math.gcd(512, src_row.shape[0] // slabs)
        scalars = (psf_index, flux_scale, noise_level)

        edges = list(range(0, epochs, 2)) + [epochs]
        parties = list(zip(edges, edges[1:]))

        far, weighted, images, table = row_transform_far(plan, place, *scalars, epoch_images, psf_bank)
        near = row_transform_near(plan, place, weighted, images, table)
        (blocks,) = row_transform(plan, place, images, table, [(0, epochs)])
        numer = trade(near + far, slab_axes, slabs)
        numer, blocks = lax.optimization_barrier((numer[::-1], blocks))
        numer = numerator(plan, place, *scalars, numer[::-1], pieces)
        bank, numer = lax.optimization_barrier((psf_bank, numer))
        spectrum, power, taps = psf_planes(plan, place, bank, psf_index)
        blocks = trade(blocks, slab_axes, slabs)
        if direct:
            own = sum(trade(numer, "epoch", ranks)[::-1])
            own, spectrum = lax.optimization_barrier((own, spectrum))
            numer = trade([own] * ranks, "epoch", ranks)
        else:
            own = lax.psum(numer[0], "epoch")
            numer = [own]
        gain, cross = filter_gains(plan, flux_scale, noise_level, own, spectrum, power)
        image = column_transform(plan, place, blocks)
        returned = []
        for begin, end in parties:
            rows_back = column_inverse(plan, place, image, gain, cross, numer, begin, end)
            returned.append(trade(rows_back, slab_axes, slabs))
        chosen = column_choice(side, src_col.reshape(-1, group))
        picked = [None]
        for (begin, _), block in zip(parties, returned):
            picked = row_fluxes(
                plan, place, block, taps, begin, epochs, picked[0], src_row.reshape(-1, group), chosen
            )
        difference = row_images(plan, place, returned)
        return difference, sum(trade(picked, slab_axes, slabs)[::-1])

    return shards


def solution(mesh):
    in_specs = (
        P(("grp", "epoch"), ("tile", "sub"), None),
        P(),
        P(("grp", "epoch")),
        P(("grp", "epoch")),
        P(("grp", "epoch")),
        P("grp"),
        P("grp"),
    )
    out_specs = (P(("grp", "epoch"), ("tile", "sub"), None), P(("grp", "epoch"), ("tile", "sub")))
    return jax.shard_map(
        make_shards(mesh), mesh=mesh, in_specs=in_specs, out_specs=out_specs, check_vma=False
    )
```

```python
import math

import jax
import jax.numpy as jnp
import ml_dtypes
import numpy as np
from jax import lax
from jax.experimental import pallas as pl
from jax.experimental.pallas import tpu as pltpu
from jax.sharding import PartitionSpec as P

reg_floor = 0.01
vmem_limit = 40 * 1024 * 1024
bf16, f32 = jnp.bfloat16, jnp.float32
hbm_rate = 3.69e6
slab_axes = ("tile", "sub")
edge_rows = 16


def halves(table):
    table = np.asarray(table, np.float64)
    high = table.astype(ml_dtypes.bfloat16)
    return np.stack([high, (table - high.astype(np.float64)).astype(ml_dtypes.bfloat16)])


def split(value):
    high = value.astype(bf16)
    return high, (value - high.astype(f32)).astype(bf16)


def slab_of():
    return lax.axis_index(slab_axes)


def angle(first, second, length):
    return np.outer(first, second) % length * (2.0 * math.pi / length)


def mul(left, right, transposed=False):
    dims = (((1,), (1,)), ((), ())) if transposed else (((1,), (0,)), ((), ()))
    return lax.dot_general(left, right, dims, preferred_element_type=f32)


def mul3(left, right, transposed=False):
    return (
        mul(left[0], right[0], transposed)
        + mul(left[1], right[0], transposed)
        + mul(left[0], right[1], transposed)
    )


class Plan:
    def __init__(self, side, slabs, stamp):
        self.side, self.slabs, self.stamp = side, slabs, stamp
        half = self.half = side // 2
        cols = self.cols = half // slabs
        lanes = self.lanes = 2 * cols
        rows = self.rows = side // slabs
        pairs = self.pairs = slabs // 2
        self.halo = stamp // 2
        self.tall = rows + 2 * self.halo
        self.band = cols + 8
        owner = np.arange(slabs)[:, None]
        freq = 2 * (cols * (owner % pairs) + np.arange(cols)[None, :]) + owner // pairs
        short = np.arange(half)
        taps = np.arange(stamp) - stamp // 2
        order = np.concatenate([2 * short, 2 * short + 1])

        ahead = np.zeros((slabs, 2, cols, half))
        back = np.zeros((slabs, 2, cols, half))
        coef = np.zeros((stamp, 2, slabs, 2, cols))
        shift = np.zeros((slabs, 2, self.band, 2, stamp))
        for d in range(slabs):
            th = angle(freq[d], short, side)
            ahead[d, 0], ahead[d, 1] = np.cos(th), -np.sin(th)
            back[d, 0], back[d, 1] = 2 * np.cos(th) / side, -2 * np.sin(th) / side
            tb = angle(taps, freq[d], side)
            coef[:, 0, d, 0] = coef[:, 0, d, 1] = np.cos(tb)
            coef[:, 1, d, 0], coef[:, 1, d, 1] = np.sin(tb), -np.sin(tb)
            te = angle(np.concatenate([freq[d], [half]]), taps, side)
            ce, se = np.cos(te), np.sin(te)
            shift[d, 0, : cols + 1, 0], shift[d, 0, : cols + 1, 1] = ce, -se
            shift[d, 1, : cols + 1, 0], shift[d, 1, : cols + 1, 1] = -se, -ce
        nyquist = np.cos(math.pi * short)
        ahead[0, 1, 0] = nyquist
        back[0, 0, 0], back[0, 1, 0] = 1.0 / side, nyquist / side
        coef[:, 0, 0, 1, 0], coef[:, 1, 0, 1, 0] = np.cos(math.pi * taps), 0.0
        self.ahead = halves(ahead.reshape(slabs, lanes, half))
        self.back = halves(back.reshape(slabs, lanes, half))
        self.coef = coef.reshape(stamp, 2 * slabs * lanes).astype(np.float32)
        self.shift = halves(shift.reshape(slabs, 2 * self.band, 2 * stamp))

        down = np.zeros((2, 2, half, half))
        up = np.zeros((2, half, 2 * half))
        for odd in range(2):
            th = angle(short, 2 * short + odd, side)
            down[odd, 0], down[odd, 1] = np.cos(th), np.sin(th)
            up[odd, :, :half], up[odd, :, half:] = np.cos(th) / side, np.sin(th) / side
        self.down = halves(down.reshape(2, 2, pairs, rows, half))
        self.up = halves(up)
        tu = angle(taps, order, side)
        high, low = halves(np.concatenate([np.cos(tu), np.sin(tu)], 0))
        self.spread = np.concatenate([high, high, low, np.zeros_like(high)], 0)


def call(kernel, outs, ins, scratch=(), aliases=None, micros=0.0):
    space = {"s": pltpu.SMEM, "v": pltpu.VMEM, "h": pl.ANY, "m": pltpu.HBM}
    ins = [
        (kind, pltpu.with_memory_space_constraint(jnp.asarray(a), pltpu.HBM) if kind == "m" else a)
        for kind, a in ins
    ]
    return pl.pallas_call(
        kernel,
        out_shape=tuple(jax.ShapeDtypeStruct(shape, (*kind, f32)[0]) for _, shape, *kind in outs),
        in_specs=[pl.BlockSpec(memory_space=space[kind]) for kind, _ in ins],
        out_specs=tuple(pl.BlockSpec(memory_space=space[out[0]]) for out in outs),
        scratch_shapes=list(scratch),
        input_output_aliases=aliases or {},
        compiler_params=pltpu.CompilerParams(vmem_limit_bytes=vmem_limit),
        cost_estimate=pl.CostEstimate(flops=0, bytes_accessed=int(micros * hbm_rate), transcendentals=0),
    )(*[a for _, a in ins])


def filter_taps(plan, bank_ref, coef_ref, index_ref, epochs, factor, taps_ref):
    stamp, slabs, lanes = plan.stamp, plan.slabs, plan.lanes
    filters = []
    for e in range(epochs):
        own = bank_ref[index_ref[e]]
        own = own / jnp.sum(own, keepdims=True)
        filters.append(factor(e, own))
    taps = jnp.dot(
        jnp.concatenate(filters, 0), coef_ref[...],
        precision=lax.Precision.HIGHEST, preferred_element_type=f32,
    )
    for kind in range(2):
        for d in range(slabs):
            start = (kind * slabs + d) * lanes
            taps_ref[kind, d] = taps[:, start : start + lanes]


def swap_halves(plan, value):
    return jnp.concatenate([value[:, plan.cols :], value[:, : plan.cols]], 1)


def owners_of(plan, q, group):
    return [q ^ (group * plan.pairs + m) for m in range(plan.pairs)]


def row_operands(plan, q, group, x_ref, table_ref):
    half = plan.half
    x = x_ref[...].reshape(-1, 2 * half)
    first, second = x[:, :half], x[:, half:]
    sign = jnp.where((q >= plan.pairs) != (group == 1), -1.0, 1.0).astype(f32)
    data = split(first + sign * second)
    table = [
        jnp.concatenate([table_ref[n, d] for d in owners_of(plan, q, group)], 0) for n in range(2)
    ]
    return data, table


def coadd_rows(plan, q, group, x_ref, table_ref, taps_ref, padded, gathered, outs):
    rows, lanes, tall, stamp, pairs = plan.rows, plan.lanes, plan.tall, plan.stamp, plan.pairs
    epochs = x_ref.shape[0]
    step = tall // 2
    padded[:, :, :stamp] = jnp.zeros((pairs, epochs, stamp, lanes), f32)
    padded[:, :, stamp + rows :] = jnp.zeros((pairs, epochs, stamp, lanes), f32)
    data, table = row_operands(plan, q, group, x_ref, table_ref)
    upright = mul3(data, table, True)
    for m in range(pairs):
        for e in range(epochs):
            padded[m, e, stamp : stamp + rows] = upright[
                e * rows : (e + 1) * rows, m * lanes : (m + 1) * lanes
            ]

    @pl.loop(0, pairs)
    def _(m):
        d = q ^ (group * pairs + m)
        for start in range(0, tall, step):
            straight = jnp.zeros((step, lanes), f32)
            crossed = jnp.zeros((step, lanes), f32)
            for e in range(epochs):
                for shift in range(8):
                    shifted = padded[m, e, start + shift : start + shift + step + stamp - 8, :]
                    for base in range(0, stamp, 8):
                        value = shifted[base : base + step]
                        at = e * stamp + base + shift
                        straight += taps_ref[0, d, at : at + 1] * value
                        crossed += taps_ref[1, d, at : at + 1] * value
            gathered[m, start : start + step] = straight + swap_halves(plan, crossed)

    for m in range(pairs):
        outs[m][...] = gathered[m]


def coadd_scratch(plan, epochs):
    return [
        pltpu.VMEM((plan.pairs, epochs, plan.rows + 2 * plan.stamp, plan.lanes), f32),
        pltpu.VMEM((plan.pairs, plan.tall, plan.lanes), f32),
    ]


def row_transform_far(plan, index, flux, noise, images, bank, piece):
    epochs = images.shape[0]
    slabs, pairs, lanes, tall, stamp = plan.slabs, plan.pairs, plan.lanes, plan.tall, plan.stamp

    def kernel(*rest):
        sources, outs, rest = rest[:7], rest[7 : 7 + pairs], rest[7 + pairs :]
        shares_ref, taps_ref, x_ref, table_ref, index_ref, flux_ref, noise_ref, bank_ref, coef_ref = rest[:9]
        padded, gathered, sems = rest[9:]
        targets = [index_ref, flux_ref, noise_ref, bank_ref, coef_ref, x_ref, table_ref]
        copies = [pltpu.make_async_copy(sources[i], targets[i], sems.at[i]) for i in range(7)]
        for copy in copies:
            copy.start()
        for copy in copies[:5]:
            copy.wait()
        filter_taps(
            plan, bank_ref, coef_ref, index_ref, epochs,
            lambda e, own: own * (flux_ref[e] / (noise_ref[e] * noise_ref[e])), taps_ref,
        )
        lane = lax.broadcasted_iota(jnp.int32, (1, piece), 1)
        shares = jnp.zeros((1, piece), f32)
        for e in range(epochs):
            ratio = flux_ref[e] / noise_ref[e]
            shares += jnp.where(lane == index_ref[e], ratio * ratio, 0.0)
        shares_ref[...] = shares
        for copy in copies[5:]:
            copy.wait()
        coadd_rows(plan, slab_of(), 1, x_ref, table_ref, taps_ref, padded, gathered, outs)

    flat = call(
        kernel,
        [("v", (tall, lanes))] * pairs
        + [("v", (1, piece)), ("v", (2, slabs, epochs * stamp, lanes)), ("v", images.shape), ("v", plan.ahead.shape, bf16)],
        [("m", index), ("m", flux), ("m", noise), ("m", bank), ("m", plan.coef),
         ("m", images), ("m", plan.ahead)],
        [pltpu.SMEM(index.shape, jnp.int32), pltpu.SMEM(flux.shape, f32), pltpu.SMEM(noise.shape, f32),
         pltpu.VMEM(bank.shape, f32), pltpu.VMEM(plan.coef.shape, f32)]
        + coadd_scratch(plan, epochs) + [pltpu.SemaphoreType.DMA((7,))],
        micros=4.5,
    )
    return list(flat[:pairs]), *flat[pairs:]


def row_transform_near(plan, taps, images, table):
    pairs = plan.pairs

    def kernel(taps_ref, x_ref, table_ref, *rest):
        coadd_rows(plan, slab_of(), 0, x_ref, table_ref, taps_ref, *rest[pairs:], rest[:pairs])

    return list(call(
        kernel,
        [("v", (plan.tall, plan.lanes))] * pairs,
        [("v", taps), ("v", images), ("v", table)],
        coadd_scratch(plan, images.shape[0]),
        micros=3.2,
    ))


def row_transform(plan, images, table, parties):
    slabs, pairs, lanes, rows = plan.slabs, plan.pairs, plan.lanes, plan.rows

    def kernel(x_ref, table_ref, *outs):
        for group in range(2):
            data, table = row_operands(plan, slab_of(), group, x_ref, table_ref)
            result = mul3(table, data, True)
            for i, (begin, end) in enumerate(parties):
                for m in range(pairs):
                    outs[i * slabs + group * pairs + m][...] = result[
                        m * lanes : (m + 1) * lanes, begin * rows : end * rows
                    ]

    flat = call(
        kernel,
        [("v", (lanes, (end - begin) * rows)) for begin, end in parties for _ in range(slabs)],
        [("v", images), ("v", table)],
        micros=1.3,
    )
    return [list(flat[i * slabs : (i + 1) * slabs]) for i in range(len(parties))]


def numerator(plan, shares, blocks, pieces):
    slabs, cols, rows, half, side, lanes, halo, tall = (
        plan.slabs, plan.cols, plan.rows, plan.half, plan.side, plan.lanes, plan.halo, plan.tall,
    )
    piece = side // pieces

    def kernel(shares_ref, *rest):
        ins, table_ref = rest[:slabs], rest[slabs]
        outs = rest[slabs + 1 : slabs + 1 + pieces]
        whole, parts = rest[slabs + 1 + pieces :]
        q, z = slab_of(), lax.axis_index("epoch") if pieces > 1 else 0
        whole[...] = jnp.zeros((side + 2 * halo, lanes), f32)
        for m in range(slabs):
            at = pl.multiple_of((q ^ m) * rows, rows)
            whole[pl.ds(at, tall)] += ins[slabs - 1 - m][...]
        whole[side : side + halo] += whole[:halo]
        whole[halo : 2 * halo] += whole[side + halo :]
        top, bottom = whole[halo : halo + half], whole[halo + half : halo + side]
        row = lax.broadcasted_iota(jnp.int32, (cols, half), 0)
        first = (q == 0).astype(f32)
        keep = 1.0 - first * (row == 0).astype(f32)
        line = lax.broadcasted_iota(jnp.int32, (edge_rows, half), 0)
        for odd in range(2):
            value = (top - bottom if odd else top + bottom).T
            re, im = value[:cols], value[cols:]
            edge = jnp.broadcast_to(im[:1] * first, (edge_rows, half))
            im = im * keep
            left = jnp.concatenate(
                [
                    jnp.concatenate([re, im, jnp.where(line == 0, edge, 0.0)], 0),
                    jnp.concatenate([im, -re, jnp.where(line == 1, -edge, 0.0)], 0),
                ],
                1,
            )
            table = [
                jnp.concatenate([table_ref[n, odd, kind].reshape(half, half) for kind in range(2)], 0)
                for n in range(2)
            ]
            plane = mul3(split(left), table)[: lanes + 8]
            step = min(piece, half)
            for i in range(half // step):
                at = odd * half + i * step
                parts[at // piece, :, at % piece : at % piece + step] = plane[:, i * step : (i + 1) * step]
        for m in range(pieces):
            parts[m, lanes + 2 : lanes + 3] = shares_ref[...]
        for m in range(pieces):
            outs[m][...] = parts[z ^ m]

    return call(
        kernel,
        [("v", (lanes + 8, piece))] * pieces,
        [("v", shares)] + [("v", b) for b in reversed(blocks)]
        + [("v", plan.down)],
        [pltpu.VMEM((side + 2 * halo, lanes), f32), pltpu.VMEM((pieces, lanes + 8, piece), f32)],
        micros=1.15,
    )


def psf_planes(plan, bank, index):
    epochs = index.shape[0]
    count, stamp = bank.shape[:2]
    side, cols, band, slabs, lanes = plan.side, plan.cols, plan.band, plan.slabs, plan.lanes
    body = epochs * cols
    size = body + edge_rows
    pitch = 8 * stamp

    def kernel(
        index_ref, bank_ref, shift_ref, spread_ref, coef_ref,
        spectrum_ref, power_ref, taps_ref, right_ref, plane_ref,
    ):
        q = slab_of()
        stamps = bank_ref[...]
        stamps = stamps / jnp.sum(jnp.sum(stamps, axis=2, keepdims=True), axis=1, keepdims=True)
        blank = jnp.zeros((stamp, stamp), f32)
        for k in range(count):
            pair = jnp.concatenate(
                [jnp.concatenate([stamps[k], blank], 1), jnp.concatenate([blank, stamps[k]], 1)], 0
            )
            for copy in range(4):
                at = k * pitch + copy * 2 * stamp
                right_ref[at : at + 2 * stamp] = pair
        right = split(right_ref[...])
        mixed = mul3((shift_ref[0, q], shift_ref[1, q]), right, True)
        lane = lax.broadcasted_iota(jnp.int32, mixed.shape, 1) % pitch
        middle = (lane >= 2 * stamp) & (lane < 4 * stamp)
        high = mixed.astype(bf16).astype(f32)
        left = jnp.where(middle, mixed - high, high).astype(bf16)
        for k in range(count):
            plane = mul(left[:, k * pitch : (k + 1) * pitch], spread_ref[...])
            plane_ref[k] = plane
            power_ref[k] = plane[:band] * plane[:band] + plane[band:] * plane[band:]
        for e in range(epochs):
            k = index_ref[e]
            for base, start in ((0, 0), (size, band)):
                value = plane_ref[k, start : start + band]
                spectrum_ref[base + e * cols : base + (e + 1) * cols] = value[:cols]
                spectrum_ref[base + body + e : base + body + e + 1] = value[cols : cols + 1]
        none = jnp.zeros((edge_rows - epochs, side), f32)
        spectrum_ref[body + epochs : size] = none
        spectrum_ref[size + body + epochs :] = none
        filter_taps(
            plan, bank_ref, coef_ref, index_ref, epochs,
            lambda e, own: own / jnp.sum(own * own, keepdims=True), taps_ref,
        )

    return call(
        kernel,
        [("v", (2 * size, side)), ("v", (count, band, side)), ("v", (2, slabs, epochs * stamp, lanes))],
        [("s", index), ("v", bank), ("v", plan.shift), ("v", plan.spread), ("v", plan.coef)],
        [pltpu.VMEM((count * pitch, 2 * stamp), f32), pltpu.VMEM((count, 2 * band, side), f32)],
        micros=2.35,
    )


def filter_gains(plan, flux, noise, share, spectrum, power):
    epochs = flux.shape[0]
    count = power.shape[0]
    side, cols = plan.side, plan.cols
    body = epochs * cols
    size = body + edge_rows
    row = plan.lanes + 2

    def kernel(flux_ref, noise_ref, share_ref, spectrum_ref, power_ref, gain_ref, cross_ref):
        shares = [jnp.broadcast_to(share_ref[row : row + 1, k : k + 1], (8, side)) for k in range(count)]
        none = jnp.zeros((edge_rows - epochs, side), f32)
        gain_ref[body + epochs : size] = none
        cross_ref[body + epochs : size] = none
        cross_ref[size + body + epochs :] = none
        for block in range(plan.band // 8):
            total = jnp.full((8, side), reg_floor, f32)
            for k in range(count):
                total += shares[k] * power_ref[k, block * 8 : block * 8 + 8]
            edge = block == cols // 8
            total = total[:1] if edge else total
            lines = 1 if edge else 8
            root = jnp.sqrt(total)
            inverse_root = 1.0 / root
            for e in range(epochs):
                at = body + e if edge else e * cols + block * 8
                re = spectrum_ref[at : at + lines]
                im = spectrum_ref[size + at : size + at + lines]
                scale, sigma = flux_ref[e], noise_ref[e]
                inverse = lax.rsqrt(
                    sigma * sigma * total + scale * scale * (re * re + im * im) + reg_floor
                )
                ratio = scale * inverse * inverse_root
                gain_ref[at : at + lines] = root * inverse
                cross_ref[at : at + lines] = ratio * re
                cross_ref[size + at : size + at + lines] = ratio * im

    return call(
        kernel,
        [("v", (size, side)), ("v", (2 * size, side))],
        [("s", flux), ("s", noise), ("v", share), ("v", spectrum), ("v", power)],
        micros=1.15,
    )


def column_transform(plan, members, blocks, partial):
    pairs, cols, rows, half, side = plan.pairs, plan.cols, plan.rows, plan.half, plan.side
    epochs = blocks[0].shape[1] // rows
    body = epochs * cols
    size = body + edge_rows
    count = len(members)
    depth = count * rows

    def kernel(*rest):
        far, near = rest[:count], rest[count : 2 * count]
        table_ref, rest = rest[2 * count], rest[2 * count + 1 :]
        if partial is not None:
            partial_ref, rest = rest[0], rest[1:]
        plane_ref, left_high, left_low = rest
        q = slab_of()
        first = (q == 0).astype(f32)
        sign = jnp.where(q < pairs, 1.0, -1.0).astype(f32)
        row = lax.broadcasted_iota(jnp.int32, (cols, rows), 0)
        keep = 1.0 - first * (row == 0).astype(f32)

        def put(row_at, lane_at, entry):
            where = (slice(row_at, row_at + entry.shape[0]), slice(lane_at, lane_at + rows))
            left_high[where], left_low[where] = split(entry)

        for odd in range(2):
            for n in range(count):
                lower, upper = near[n][...], far[n][...]
                value = sign * (lower - upper) if odd else lower + upper
                edges = []
                for e in range(epochs):
                    re = value[:cols, e * rows : (e + 1) * rows]
                    im = value[cols:, e * rows : (e + 1) * rows]
                    edges.append(im[:1] * first)
                    im = im * keep
                    put(e * cols, n * rows, re)
                    put(e * cols, depth + n * rows, im)
                    put(size + e * cols, n * rows, im)
                    put(size + e * cols, depth + n * rows, -re)
                edge = jnp.concatenate(edges + [jnp.zeros((edge_rows - epochs, rows), f32)], 0)
                put(body, n * rows, edge)
                put(body, depth + n * rows, jnp.zeros_like(edge))
                put(size + body, n * rows, jnp.zeros_like(edge))
                put(size + body, depth + n * rows, -edge)
            order = [(q ^ m) % pairs for m in members]
            table = [
                jnp.concatenate([table_ref[n, odd, kind, i] for kind in range(2) for i in order], 0)
                for n in range(2)
            ]
            here = slice(odd * half, (odd + 1) * half)
            plane = mul3((left_high[...], left_low[...]), table)
            plane_ref[:, here] = plane if partial is None else plane + partial_ref[:, here]

    ins = [("v", blocks[m + pairs]) for m in members] + [("v", blocks[m]) for m in members]
    ins.append(("v", plan.down))
    if partial is not None:
        ins.append(("v", partial))
    (plane,) = call(
        kernel,
        [("v", (2 * size, side))],
        ins,
        [pltpu.VMEM((2 * size, 2 * depth), bf16), pltpu.VMEM((2 * size, 2 * depth), bf16)],
        micros=1.0,
    )
    return plane


def column_inverse(plan, spectrum, gain, cross, numer, begin, end):
    slabs, cols, rows, half, side, lanes, halo, tall = (
        plan.slabs, plan.cols, plan.rows, plan.half, plan.side, plan.lanes, plan.halo, plan.tall,
    )
    size = gain.shape[0]
    body = size - edge_rows
    epochs = end - begin
    pieces = len(numer)
    piece = side // pieces

    def kernel(spectrum_ref, gain_ref, cross_ref, *rest):
        numer_refs, table_ref = rest[:pieces], rest[pieces]
        outs = rest[pieces + 1 : pieces + 1 + slabs]
        whole, right_high, right_low, planes = rest[pieces + 1 + slabs :]
        q, z = slab_of(), lax.axis_index("epoch") if pieces > 1 else 0
        for m in range(pieces):
            whole[z ^ m] = numer_refs[m][...]
        flag = jnp.broadcast_to(q, (cols, half)) == 0
        packed = flag & (lax.broadcasted_iota(jnp.int32, (cols, half), 0) == 0)
        results = []
        for odd in range(2):
            here = slice(odd * half, (odd + 1) * half)
            step = min(piece, half)
            parts = [
                whole[at // piece, :, at % piece : at % piece + step]
                for at in range(odd * half, (odd + 1) * half, step)
            ]
            numer_all = parts[0] if len(parts) == 1 else jnp.concatenate(parts, 1)

            def difference(at, lines, nre, nim):
                gain_, cre = gain_ref[at : at + lines, here], cross_ref[at : at + lines, here]
                cim = cross_ref[size + at : size + at + lines, here]
                mre = spectrum_ref[at : at + lines, here]
                mim = spectrum_ref[size + at : size + at + lines, here]
                return gain_ * mre - (cre * nre - cim * nim), gain_ * mim - (cre * nim + cim * nre)

            for i in range(epochs):
                e = begin + i
                edge_re, edge_im = difference(
                    body + e, 1,
                    numer_all[lanes : lanes + 1], numer_all[lanes + 1 : lanes + 2],
                )
                re, im = difference(e * cols, cols, numer_all[:cols], numer_all[cols:lanes])
                im_left = jnp.where(packed, edge_re, im)
                im_right = jnp.where(packed, -edge_im, re)
                for base, start, entry in (
                    (0, 0, re), (0, half, -im), (cols, 0, im_left), (cols, half, im_right),
                ):
                    where = (
                        slice(i * lanes + base, i * lanes + base + cols),
                        slice(start, start + half),
                    )
                    right_high[where], right_low[where] = split(entry)
            results.append(
                mul3((table_ref[0, odd], table_ref[1, odd]), (right_high[...], right_low[...]), True)
            )
        planes[halo : halo + half] = results[0] + results[1]
        planes[halo + half : halo + side] = results[0] - results[1]
        planes[:halo] = planes[side : side + halo]
        planes[halo + side :] = planes[halo : 2 * halo]
        for m in range(slabs):
            start = pl.multiple_of((q ^ m) * rows, rows)
            for i in range(epochs):
                outs[m][i] = planes[pl.ds(start, tall), i * lanes : (i + 1) * lanes]

    return call(
        kernel,
        [("v", (epochs, tall, lanes))] * slabs,
        [("v", spectrum), ("v", gain), ("v", cross)] + [("v", n) for n in numer]
        + [("v", plan.up)],
        [pltpu.VMEM((pieces, lanes + 8, piece), f32),
         pltpu.VMEM((epochs * lanes, side), bf16), pltpu.VMEM((epochs * lanes, side), bf16),
         pltpu.VMEM((side + 2 * halo, epochs * lanes), f32)],
        micros=1.35,
    )


def column_choice(side, src_col):
    groups, group = src_col.shape

    def kernel(col_ref, out_ref):
        column = lax.broadcasted_iota(jnp.int32, (side, group), 0)

        @pl.loop(0, groups)
        def _(g):
            out_ref[g] = (column == col_ref[pl.ds(g, 1)]).astype(f32).astype(bf16)

    (chosen,) = call(
        kernel, [("v", (groups, side, group), bf16)], [("v", src_col)], micros=2.0
    )
    return chosen


def inverse_rows(plan, q, left, table_ref):
    pairs, lanes = plan.pairs, plan.lanes
    sums = []
    for group in range(2):
        table = [
            jnp.concatenate([table_ref[n, d] for d in owners_of(plan, q, group)], 0) for n in range(2)
        ]
        here = slice(group * pairs * lanes, (group + 1) * pairs * lanes)
        sums.append(mul3((left[0][:, here], left[1][:, here]), table))
    sign = jnp.where(q < pairs, 1.0, -1.0).astype(f32)
    return sums[0] + sums[1], sign * (sums[0] - sums[1])


def row_images(plan, returned):
    slabs, rows, half, side, lanes, halo = (
        plan.slabs, plan.rows, plan.half, plan.side, plan.lanes, plan.halo,
    )
    counts = [blocks[0].shape[0] for blocks in returned]
    epochs = sum(counts)

    def kernel(*rest):
        ins, table_ref, diff_ref = rest[: -6], rest[-6], rest[-5]
        left_high, left_low, image_ref, sems = rest[-4:]
        q = slab_of()
        copies = []
        begin = 0
        for i, count in enumerate(counts):
            total = count * rows
            for m in range(slabs):
                here = slice(m * lanes, (m + 1) * lanes)
                value = ins[i * slabs + m][:, halo : halo + rows, :].reshape(total, lanes)
                left_high[:total, here], left_low[:total, here] = split(value)
            left = (left_high[:total], left_low[:total])
            for part, value in enumerate(inverse_rows(plan, q, left, table_ref)):
                image_ref[begin : begin + count, :, part * half : (part + 1) * half] = value.reshape(
                    count, rows, half
                )
            where = pl.ds(begin, count)
            copies.append(pltpu.make_async_copy(image_ref.at[where], diff_ref.at[where], sems.at[i]))
            copies[-1].start()
            begin += count
        for copy in copies:
            copy.wait()

    left = pltpu.VMEM((max(counts) * rows, side), bf16)
    (difference,) = call(
        kernel,
        [("h", (epochs, rows, side))],
        [("v", b) for blocks in returned for b in blocks] + [("v", plan.back)],
        [left, left, pltpu.VMEM((epochs, rows, side), f32), pltpu.SemaphoreType.DMA((len(counts),))],
        micros=2.2,
    )
    return difference


def pick(plan, q, flux_ref, chosen_ref, row_ref, groups):
    rows = plan.rows
    total = flux_ref.shape[0] // 2
    line = lax.broadcasted_iota(jnp.int32, (rows, row_ref.shape[1]), 0)
    parts = []
    for g in groups:
        values = mul(flux_ref[...], chosen_ref[g])
        values = values[:total] + values[total:]
        inside = line == row_ref[pl.ds(g, 1)] - q * rows
        found = [
            jnp.sum(jnp.where(inside, values[at : at + rows], 0.0), axis=0, keepdims=True)
            for at in range(0, total, rows)
        ]
        parts.append(jnp.concatenate(found, 0))
    return jnp.concatenate(parts, 1)


def row_fluxes(plan, blocks, taps, begin, epochs, src_row, chosen, earlier):
    slabs, pairs, rows, half, side, lanes, stamp = (
        plan.slabs, plan.pairs, plan.rows, plan.half, plan.side, plan.lanes, plan.stamp,
    )
    mine = blocks[0].shape[0]
    groups, group = src_row.shape
    each = groups // slabs
    total = mine * rows
    step = min(64, rows)
    last = begin + mine == epochs

    def kernel(row_ref, chosen_ref, taps_ref, *rest):
        ins, table_ref, rest = rest[:slabs][::-1], rest[slabs], rest[slabs + 1 :]
        if begin:
            earlier_ref, rest = rest[0], rest[1:]
        flux_ref, *outs, left_high, left_low = rest
        q = slab_of()
        for m in range(slabs):
            d = q ^ m
            here = slice(m * lanes, (m + 1) * lanes)
            for i in range(mine):
                for start in range(0, rows, step):
                    straight = jnp.zeros((step, lanes), f32)
                    crossed = jnp.zeros((step, lanes), f32)
                    for shift in range(8):
                        shifted = ins[m][i, start + shift : start + shift + step + stamp - 8, :]
                        for base in range(0, stamp, 8):
                            value = shifted[base : base + step]
                            at = (begin + i) * stamp + base + shift
                            straight += taps_ref[0, d, at : at + 1] * value
                            crossed += taps_ref[1, d, at : at + 1] * value
                    at = i * rows + start
                    left_high[at : at + step, here], left_low[at : at + step, here] = split(
                        straight + swap_halves(plan, crossed)
                    )
        for part, value in enumerate(
            inverse_rows(plan, q, (left_high[...], left_low[...]), table_ref)
        ):
            here = slice(part * half, (part + 1) * half)
            flux_ref[:total, here], flux_ref[total:, here] = split(value)
        for m in range(1 if last else 0, slabs):
            owner = q ^ m if last else m
            out = outs[m - 1] if last else outs[0].at[m]
            if begin:
                out[:begin] = earlier_ref[owner]
            out[begin:] = pick(
                plan, q, flux_ref, chosen_ref, row_ref, [owner * each + i for i in range(each)]
            )

    left = pltpu.VMEM((total, side), bf16)
    shape = (begin + mine, each * group)
    ins = [("v", src_row), ("v", chosen), ("v", taps)]
    ins += [("v", b) for b in reversed(blocks)] + [("v", plan.back)]
    if begin:
        ins.append(("v", earlier))
    flux, *picked = call(
        kernel,
        [("v", (2 * total, side), bf16)] + ([("v", shape)] * (slabs - 1) if last else [("v", (slabs, *shape))]),
        ins,
        [left, left],
        micros=3.5,
    )
    return flux, picked


def own_fluxes(plan, flux, begin, src_row, chosen, earlier):
    groups, group = src_row.shape
    each = groups // plan.slabs
    epochs = begin + flux.shape[0] // 2 // plan.rows

    def kernel(row_ref, chosen_ref, flux_ref, *rest):
        out, q = rest[-1], slab_of()
        if begin:
            out[:begin] = rest[0][q]
        out[begin:] = pick(plan, q, flux_ref, chosen_ref, row_ref, [q * each + i for i in range(each)])

    ins = [("v", src_row), ("v", chosen), ("v", flux)]
    return call(
        kernel,
        [("v", (epochs, each * group))],
        ins + ([("v", earlier)] if begin else []),
        micros=0.9,
    )


def trade(parts, axes, count):
    result = list(parts)
    for m in reversed(range(1, count)):
        result[m] = lax.ppermute(parts[m], axes, [(i, i ^ m) for i in range(count)])
    return result


def make_shards(mesh):
    slabs = mesh.shape["tile"] * mesh.shape["sub"]
    ranks = mesh.shape["epoch"]

    def shards(epoch_images, psf_bank, psf_index, flux_scale, noise_level, src_row, src_col):
        epochs, rows, side = epoch_images.shape
        plan = Plan(side, slabs, psf_bank.shape[1])
        direct = ranks & (ranks - 1) == 0 and side // ranks % 128 == 0
        pieces = ranks if direct else 1
        group = math.gcd(512, src_row.shape[0] // slabs)
        scalars = (psf_index, flux_scale, noise_level)

        edges = list(range(0, epochs, 2)) + [epochs]
        parties = list(zip(edges, edges[1:]))

        far, shares, weighted, images, table = row_transform_far(
            plan, *scalars, epoch_images, psf_bank, side // pieces
        )
        near = row_transform_near(plan, weighted, images, table)
        (blocks,) = row_transform(plan, images, table, [(0, epochs)])
        numer = trade(near + far, slab_axes, slabs)
        numer, blocks = lax.optimization_barrier((numer[::-1], blocks))
        numer = numerator(plan, shares, numer[::-1], pieces)
        bank, numer = lax.optimization_barrier((psf_bank, numer))
        spectrum, power, taps = psf_planes(plan, bank, psf_index)
        blocks = trade(blocks, slab_axes, slabs)
        if direct:
            own = sum(trade(numer, "epoch", ranks)[::-1])
            own, spectrum = lax.optimization_barrier((own, spectrum))
            numer = trade([own] * ranks, "epoch", ranks)
        else:
            own = lax.psum(numer[0], "epoch")
            numer = [own]
        gain, cross = filter_gains(plan, flux_scale, noise_level, own, spectrum, power)
        image = None
        if plan.pairs > 1:
            image = column_transform(plan, list(range(1, plan.pairs)), blocks, None)
        image = column_transform(plan, [0], blocks, image)
        returned = []
        for begin, end in parties:
            rows_back = column_inverse(plan, image, gain, cross, numer, begin, end)
            returned.append(trade(rows_back, slab_axes, slabs))
        chosen = column_choice(side, src_col.reshape(-1, group))
        src_row = src_row.reshape(-1, group)
        earlier = None
        for (begin, end), block in zip(parties, returned):
            flux, picked = row_fluxes(plan, block, taps, begin, epochs, src_row, chosen, earlier)
            if end < epochs:
                (earlier,) = picked
        picked = [*own_fluxes(plan, flux, begin, src_row, chosen, earlier), *picked]
        difference = row_images(plan, returned)
        return difference, sum(trade(picked, slab_axes, slabs)[::-1])

    return shards


def solution(mesh):
    in_specs = (
        P(("grp", "epoch"), ("tile", "sub"), None),
        P(),
        P(("grp", "epoch")),
        P(("grp", "epoch")),
        P(("grp", "epoch")),
        P("grp"),
        P("grp"),
    )
    out_specs = (P(("grp", "epoch"), ("tile", "sub"), None), P(("grp", "epoch"), ("tile", "sub")))
    return jax.shard_map(
        make_shards(mesh), mesh=mesh, in_specs=in_specs, out_specs=out_specs, check_vma=False
    )
```

```python
import math

import jax
import jax.numpy as jnp
import ml_dtypes
import numpy as np
from jax import lax
from jax.experimental import pallas as pl
from jax.experimental.pallas import tpu as pltpu
from jax.sharding import PartitionSpec as P

reg_floor = 0.01
vmem_limit = 40 * 1024 * 1024
bf16, f32 = jnp.bfloat16, jnp.float32
hbm_rate = 3.69e6
slab_axes = ("tile", "sub")
edge_rows = 16


def halves(table):
    table = np.asarray(table, np.float64)
    high = table.astype(ml_dtypes.bfloat16)
    return np.stack([high, (table - high.astype(np.float64)).astype(ml_dtypes.bfloat16)])


def split(value):
    high = value.astype(bf16)
    return high, (value - high.astype(f32)).astype(bf16)


def slab_of():
    return lax.axis_index(slab_axes)


def angle(first, second, length):
    return np.outer(first, second) % length * (2.0 * math.pi / length)


def mul(left, right, transposed=False):
    dims = (((1,), (1,)), ((), ())) if transposed else (((1,), (0,)), ((), ()))
    return lax.dot_general(left, right, dims, preferred_element_type=f32)


def mul3(left, right, transposed=False):
    return (
        mul(left[0], right[0], transposed)
        + mul(left[1], right[0], transposed)
        + mul(left[0], right[1], transposed)
    )


class Plan:
    def __init__(self, side, slabs, stamp):
        self.side, self.slabs, self.stamp = side, slabs, stamp
        half = self.half = side // 2
        cols = self.cols = half // slabs
        lanes = self.lanes = 2 * cols
        rows = self.rows = side // slabs
        pairs = self.pairs = slabs // 2
        self.halo = stamp // 2
        self.tall = rows + 2 * self.halo
        self.band = cols + 8
        owner = np.arange(slabs)[:, None]
        freq = 2 * (cols * (owner % pairs) + np.arange(cols)[None, :]) + owner // pairs
        short = np.arange(half)
        taps = np.arange(stamp) - stamp // 2
        order = np.concatenate([2 * short, 2 * short + 1])

        ahead = np.zeros((slabs, 2, cols, half))
        back = np.zeros((slabs, 2, cols, half))
        coef = np.zeros((stamp, 2, slabs, 2, cols))
        shift = np.zeros((slabs, 2, self.band, 2, stamp))
        for d in range(slabs):
            th = angle(freq[d], short, side)
            ahead[d, 0], ahead[d, 1] = np.cos(th), -np.sin(th)
            back[d, 0], back[d, 1] = 2 * np.cos(th) / side, -2 * np.sin(th) / side
            tb = angle(taps, freq[d], side)
            coef[:, 0, d, 0] = coef[:, 0, d, 1] = np.cos(tb)
            coef[:, 1, d, 0], coef[:, 1, d, 1] = np.sin(tb), -np.sin(tb)
            te = angle(np.concatenate([freq[d], [half]]), taps, side)
            ce, se = np.cos(te), np.sin(te)
            shift[d, 0, : cols + 1, 0], shift[d, 0, : cols + 1, 1] = ce, -se
            shift[d, 1, : cols + 1, 0], shift[d, 1, : cols + 1, 1] = -se, -ce
        nyquist = np.cos(math.pi * short)
        ahead[0, 1, 0] = nyquist
        back[0, 0, 0], back[0, 1, 0] = 1.0 / side, nyquist / side
        coef[:, 0, 0, 1, 0], coef[:, 1, 0, 1, 0] = np.cos(math.pi * taps), 0.0
        self.ahead = halves(ahead.reshape(slabs, lanes, half))
        self.back = halves(back.reshape(slabs, lanes, half))
        self.coef = coef.reshape(stamp, 2 * slabs * lanes).astype(np.float32)
        self.shift = halves(shift.reshape(slabs, 2 * self.band, 2 * stamp))

        down = np.zeros((2, 2, half, half))
        up = np.zeros((2, half, 2 * half))
        for odd in range(2):
            th = angle(short, 2 * short + odd, side)
            down[odd, 0], down[odd, 1] = np.cos(th), np.sin(th)
            up[odd, :, :half], up[odd, :, half:] = np.cos(th) / side, np.sin(th) / side
        self.down = halves(down.reshape(2, 2, pairs, rows, half))
        self.up = halves(up)
        tu = angle(taps, order, side)
        high, low = halves(np.concatenate([np.cos(tu), np.sin(tu)], 0))
        self.spread = np.concatenate([high, high, low, np.zeros_like(high)], 0)


def call(kernel, outs, ins, scratch=(), aliases=None, micros=0.0):
    space = {"s": pltpu.SMEM, "v": pltpu.VMEM, "h": pl.ANY, "m": pltpu.HBM}
    ins = [
        (kind, pltpu.with_memory_space_constraint(jnp.asarray(a), pltpu.HBM) if kind == "m" else a)
        for kind, a in ins
    ]
    return pl.pallas_call(
        kernel,
        out_shape=tuple(jax.ShapeDtypeStruct(shape, (*kind, f32)[0]) for _, shape, *kind in outs),
        in_specs=[pl.BlockSpec(memory_space=space[kind]) for kind, _ in ins],
        out_specs=tuple(pl.BlockSpec(memory_space=space[out[0]]) for out in outs),
        scratch_shapes=list(scratch),
        input_output_aliases=aliases or {},
        compiler_params=pltpu.CompilerParams(vmem_limit_bytes=vmem_limit),
        cost_estimate=pl.CostEstimate(flops=0, bytes_accessed=int(micros * hbm_rate), transcendentals=0),
    )(*[a for _, a in ins])


def filter_taps(plan, bank_ref, coef_ref, index_ref, epochs, factor, taps_ref):
    stamp, slabs, lanes = plan.stamp, plan.slabs, plan.lanes
    filters = []
    for e in range(epochs):
        own = bank_ref[index_ref[e]]
        own = own / jnp.sum(own, keepdims=True)
        filters.append(factor(e, own))
    taps = jnp.dot(
        jnp.concatenate(filters, 0), coef_ref[...],
        precision=lax.Precision.HIGHEST, preferred_element_type=f32,
    )
    for kind in range(2):
        for d in range(slabs):
            start = (kind * slabs + d) * lanes
            taps_ref[kind, d] = taps[:, start : start + lanes]


def swap_halves(plan, value):
    return jnp.concatenate([value[:, plan.cols :], value[:, : plan.cols]], 1)


def owners_of(plan, q, group):
    return [q ^ (group * plan.pairs + m) for m in range(plan.pairs)]


def row_operands(plan, q, group, x_ref, table_ref):
    half = plan.half
    x = x_ref[...].reshape(-1, 2 * half)
    first, second = x[:, :half], x[:, half:]
    sign = jnp.where((q >= plan.pairs) != (group == 1), -1.0, 1.0).astype(f32)
    data = split(first + sign * second)
    table = [
        jnp.concatenate([table_ref[n, d] for d in owners_of(plan, q, group)], 0) for n in range(2)
    ]
    return data, table


def lay_rows(plan, q, group, x_ref, table_ref, padded):
    rows, lanes, stamp, pairs = plan.rows, plan.lanes, plan.stamp, plan.pairs
    epochs = x_ref.shape[0]
    padded[:, :, :stamp] = jnp.zeros((pairs, epochs, stamp, lanes), f32)
    padded[:, :, stamp + rows :] = jnp.zeros((pairs, epochs, stamp, lanes), f32)
    data, table = row_operands(plan, q, group, x_ref, table_ref)
    upright = mul3(data, table, True)
    for m in range(pairs):
        for e in range(epochs):
            padded[m, e, stamp : stamp + rows] = upright[
                e * rows : (e + 1) * rows, m * lanes : (m + 1) * lanes
            ]


def coadd_rows(plan, q, mask, padded, taps_ref, out):
    lanes, tall, stamp = plan.lanes, plan.tall, plan.stamp
    step = tall // 2
    d, m = q ^ mask, mask % plan.pairs
    for start in range(0, tall, step):
        straight = jnp.zeros((step, lanes), f32)
        crossed = jnp.zeros((step, lanes), f32)
        for e in range(padded.shape[1]):
            for shift in range(8):
                shifted = padded[m, e, start + shift : start + shift + step + stamp - 8, :]
                for base in range(0, stamp, 8):
                    value = shifted[base : base + step]
                    at = e * stamp + base + shift
                    straight += taps_ref[0, d, at : at + 1] * value
                    crossed += taps_ref[1, d, at : at + 1] * value
        out[start : start + step] = straight + swap_halves(plan, crossed)


def padded_shape(plan, epochs):
    return plan.pairs, epochs, plan.rows + 2 * plan.stamp, plan.lanes


def row_transform_far(plan, index, flux, noise, images, bank, piece):
    epochs = images.shape[0]
    slabs, pairs, lanes, stamp = plan.slabs, plan.pairs, plan.lanes, plan.stamp

    def kernel(*rest):
        sources, outs, rest = rest[:7], rest[7 : 7 + pairs], rest[7 + pairs :]
        shares_ref, taps_ref, x_ref, table_ref, index_ref, flux_ref, noise_ref, bank_ref, coef_ref = rest[:9]
        padded, sems = rest[9:]
        targets = [index_ref, flux_ref, noise_ref, bank_ref, coef_ref, x_ref, table_ref]
        copies = [pltpu.make_async_copy(sources[i], targets[i], sems.at[i]) for i in range(7)]
        for copy in copies:
            copy.start()
        for copy in copies[:5]:
            copy.wait()
        filter_taps(
            plan, bank_ref, coef_ref, index_ref, epochs,
            lambda e, own: own * (flux_ref[e] / (noise_ref[e] * noise_ref[e])), taps_ref,
        )
        lane = lax.broadcasted_iota(jnp.int32, (1, piece), 1)
        shares = jnp.zeros((1, piece), f32)
        for e in range(epochs):
            ratio = flux_ref[e] / noise_ref[e]
            shares += jnp.where(lane == index_ref[e], ratio * ratio, 0.0)
        shares_ref[...] = shares
        for copy in copies[5:]:
            copy.wait()
        lay_rows(plan, slab_of(), 1, x_ref, table_ref, padded)
        for m in range(pairs):
            coadd_rows(plan, slab_of(), pairs + m, padded, taps_ref, outs[m])

    flat = call(
        kernel,
        [("v", (plan.tall, lanes))] * pairs
        + [("v", (1, piece)), ("v", (2, slabs, epochs * stamp, lanes)), ("v", images.shape), ("v", plan.ahead.shape, bf16)],
        [("m", index), ("m", flux), ("m", noise), ("m", bank), ("m", plan.coef),
         ("m", images), ("m", plan.ahead)],
        [pltpu.SMEM(index.shape, jnp.int32), pltpu.SMEM(flux.shape, f32), pltpu.SMEM(noise.shape, f32),
         pltpu.VMEM(bank.shape, f32), pltpu.VMEM(plan.coef.shape, f32)]
        + [pltpu.VMEM(padded_shape(plan, epochs), f32), pltpu.SemaphoreType.DMA((7,))],
        micros=3.2,
    )
    return list(flat[:pairs]), *flat[pairs:]


def row_transform_near(plan, taps, images, table):
    pairs = plan.pairs

    def kernel(taps_ref, x_ref, table_ref, out, padded):
        lay_rows(plan, slab_of(), 0, x_ref, table_ref, padded)
        coadd_rows(plan, slab_of(), pairs - 1, padded, taps_ref, out)

    return call(
        kernel,
        [("v", (plan.tall, plan.lanes)), ("v", padded_shape(plan, images.shape[0]))],
        [("v", taps), ("v", images), ("v", table)],
        micros=1.6,
    )


def coadd_rest(plan, taps, padded, masks):
    def kernel(taps_ref, padded_ref, *outs):
        for mask, out in zip(masks, outs):
            coadd_rows(plan, slab_of(), mask, padded_ref, taps_ref, out)

    return list(call(
        kernel,
        [("v", (plan.tall, plan.lanes))] * len(masks),
        [("v", taps), ("v", padded)],
        micros=1.0 * len(masks),
    ))


def row_transform(plan, images, table, parties):
    slabs, pairs, lanes, rows = plan.slabs, plan.pairs, plan.lanes, plan.rows

    def kernel(x_ref, table_ref, *outs):
        for group in range(2):
            data, table = row_operands(plan, slab_of(), group, x_ref, table_ref)
            result = mul3(table, data, True)
            for i, (begin, end) in enumerate(parties):
                for m in range(pairs):
                    outs[i * slabs + group * pairs + m][...] = result[
                        m * lanes : (m + 1) * lanes, begin * rows : end * rows
                    ]

    flat = call(
        kernel,
        [("v", (lanes, (end - begin) * rows)) for begin, end in parties for _ in range(slabs)],
        [("v", images), ("v", table)],
        micros=1.3,
    )
    return [list(flat[i * slabs : (i + 1) * slabs]) for i in range(len(parties))]


def numerator(plan, shares, order, blocks, pieces):
    slabs, cols, rows, half, side, lanes, halo, tall = (
        plan.slabs, plan.cols, plan.rows, plan.half, plan.side, plan.lanes, plan.halo, plan.tall,
    )
    piece = side // pieces

    def kernel(shares_ref, *rest):
        ins, table_ref = rest[:slabs], rest[slabs]
        outs = rest[slabs + 1 : slabs + 1 + pieces]
        whole, parts = rest[slabs + 1 + pieces :]
        q, z = slab_of(), lax.axis_index("epoch") if pieces > 1 else 0
        whole[...] = jnp.zeros((side + 2 * halo, lanes), f32)
        for m, block in zip(order, ins):
            at = pl.multiple_of((q ^ m) * rows, rows)
            whole[pl.ds(at, tall)] += block[...]
        whole[side : side + halo] += whole[:halo]
        whole[halo : 2 * halo] += whole[side + halo :]
        top, bottom = whole[halo : halo + half], whole[halo + half : halo + side]
        row = lax.broadcasted_iota(jnp.int32, (cols, half), 0)
        first = (q == 0).astype(f32)
        keep = 1.0 - first * (row == 0).astype(f32)
        line = lax.broadcasted_iota(jnp.int32, (edge_rows, half), 0)
        for odd in range(2):
            value = (top - bottom if odd else top + bottom).T
            re, im = value[:cols], value[cols:]
            edge = jnp.broadcast_to(im[:1] * first, (edge_rows, half))
            im = im * keep
            left = jnp.concatenate(
                [
                    jnp.concatenate([re, im, jnp.where(line == 0, edge, 0.0)], 0),
                    jnp.concatenate([im, -re, jnp.where(line == 1, -edge, 0.0)], 0),
                ],
                1,
            )
            table = [
                jnp.concatenate([table_ref[n, odd, kind].reshape(half, half) for kind in range(2)], 0)
                for n in range(2)
            ]
            plane = mul3(split(left), table)[: lanes + 8]
            step = min(piece, half)
            for i in range(half // step):
                at = odd * half + i * step
                parts[at // piece, :, at % piece : at % piece + step] = plane[:, i * step : (i + 1) * step]
        for m in range(pieces):
            parts[m, lanes + 2 : lanes + 3] = shares_ref[...]
        for m in range(pieces):
            outs[m][...] = parts[z ^ m]

    return call(
        kernel,
        [("v", (lanes + 8, piece))] * pieces,
        [("v", shares)] + [("v", b) for b in blocks]
        + [("v", plan.down)],
        [pltpu.VMEM((side + 2 * halo, lanes), f32), pltpu.VMEM((pieces, lanes + 8, piece), f32)],
        micros=1.15,
    )


def psf_planes(plan, bank, index):
    epochs = index.shape[0]
    count, stamp = bank.shape[:2]
    side, cols, band, slabs, lanes = plan.side, plan.cols, plan.band, plan.slabs, plan.lanes
    body = epochs * cols
    size = body + edge_rows
    pitch = 8 * stamp

    def kernel(
        index_ref, bank_ref, shift_ref, spread_ref, coef_ref,
        spectrum_ref, power_ref, taps_ref, right_ref, plane_ref,
    ):
        q = slab_of()
        stamps = bank_ref[...]
        stamps = stamps / jnp.sum(jnp.sum(stamps, axis=2, keepdims=True), axis=1, keepdims=True)
        blank = jnp.zeros((stamp, stamp), f32)
        for k in range(count):
            pair = jnp.concatenate(
                [jnp.concatenate([stamps[k], blank], 1), jnp.concatenate([blank, stamps[k]], 1)], 0
            )
            for copy in range(4):
                at = k * pitch + copy * 2 * stamp
                right_ref[at : at + 2 * stamp] = pair
        right = split(right_ref[...])
        mixed = mul3((shift_ref[0, q], shift_ref[1, q]), right, True)
        lane = lax.broadcasted_iota(jnp.int32, mixed.shape, 1) % pitch
        middle = (lane >= 2 * stamp) & (lane < 4 * stamp)
        high = mixed.astype(bf16).astype(f32)
        left = jnp.where(middle, mixed - high, high).astype(bf16)
        for k in range(count):
            plane = mul(left[:, k * pitch : (k + 1) * pitch], spread_ref[...])
            plane_ref[k] = plane
            power_ref[k] = plane[:band] * plane[:band] + plane[band:] * plane[band:]
        for e in range(epochs):
            k = index_ref[e]
            for base, start in ((0, 0), (size, band)):
                value = plane_ref[k, start : start + band]
                spectrum_ref[base + e * cols : base + (e + 1) * cols] = value[:cols]
                spectrum_ref[base + body + e : base + body + e + 1] = value[cols : cols + 1]
        none = jnp.zeros((edge_rows - epochs, side), f32)
        spectrum_ref[body + epochs : size] = none
        spectrum_ref[size + body + epochs :] = none
        filter_taps(
            plan, bank_ref, coef_ref, index_ref, epochs,
            lambda e, own: own / jnp.sum(own * own, keepdims=True), taps_ref,
        )

    return call(
        kernel,
        [("v", (2 * size, side)), ("v", (count, band, side)), ("v", (2, slabs, epochs * stamp, lanes))],
        [("s", index), ("v", bank), ("v", plan.shift), ("v", plan.spread), ("v", plan.coef)],
        [pltpu.VMEM((count * pitch, 2 * stamp), f32), pltpu.VMEM((count, 2 * band, side), f32)],
        micros=2.35,
    )


def filter_gains(plan, flux, noise, share, spectrum, power):
    epochs = flux.shape[0]
    count = power.shape[0]
    side, cols = plan.side, plan.cols
    body = epochs * cols
    size = body + edge_rows
    row = plan.lanes + 2

    def kernel(flux_ref, noise_ref, share_ref, spectrum_ref, power_ref, gain_ref, cross_ref):
        shares = [jnp.broadcast_to(share_ref[row : row + 1, k : k + 1], (8, side)) for k in range(count)]
        none = jnp.zeros((edge_rows - epochs, side), f32)
        gain_ref[body + epochs : size] = none
        cross_ref[body + epochs : size] = none
        cross_ref[size + body + epochs :] = none
        for block in range(plan.band // 8):
            total = jnp.full((8, side), reg_floor, f32)
            for k in range(count):
                total += shares[k] * power_ref[k, block * 8 : block * 8 + 8]
            edge = block == cols // 8
            total = total[:1] if edge else total
            lines = 1 if edge else 8
            root = jnp.sqrt(total)
            inverse_root = 1.0 / root
            for e in range(epochs):
                at = body + e if edge else e * cols + block * 8
                re = spectrum_ref[at : at + lines]
                im = spectrum_ref[size + at : size + at + lines]
                scale, sigma = flux_ref[e], noise_ref[e]
                inverse = lax.rsqrt(
                    sigma * sigma * total + scale * scale * (re * re + im * im) + reg_floor
                )
                ratio = scale * inverse * inverse_root
                gain_ref[at : at + lines] = root * inverse
                cross_ref[at : at + lines] = ratio * re
                cross_ref[size + at : size + at + lines] = ratio * im

    return call(
        kernel,
        [("v", (size, side)), ("v", (2 * size, side))],
        [("s", flux), ("s", noise), ("v", share), ("v", spectrum), ("v", power)],
        micros=1.15,
    )


def column_transform(plan, members, blocks, partial):
    pairs, cols, rows, half, side = plan.pairs, plan.cols, plan.rows, plan.half, plan.side
    epochs = blocks[0].shape[1] // rows
    body = epochs * cols
    size = body + edge_rows
    count = len(members)
    depth = count * rows

    def kernel(*rest):
        far, near = rest[:count], rest[count : 2 * count]
        table_ref, rest = rest[2 * count], rest[2 * count + 1 :]
        if partial is not None:
            partial_ref, rest = rest[0], rest[1:]
        plane_ref, left_high, left_low = rest
        q = slab_of()
        first = (q == 0).astype(f32)
        sign = jnp.where(q < pairs, 1.0, -1.0).astype(f32)
        row = lax.broadcasted_iota(jnp.int32, (cols, rows), 0)
        keep = 1.0 - first * (row == 0).astype(f32)

        def put(row_at, lane_at, entry):
            where = (slice(row_at, row_at + entry.shape[0]), slice(lane_at, lane_at + rows))
            left_high[where], left_low[where] = split(entry)

        for odd in range(2):
            for n in range(count):
                lower, upper = near[n][...], far[n][...]
                value = sign * (lower - upper) if odd else lower + upper
                edges = []
                for e in range(epochs):
                    re = value[:cols, e * rows : (e + 1) * rows]
                    im = value[cols:, e * rows : (e + 1) * rows]
                    edges.append(im[:1] * first)
                    im = im * keep
                    put(e * cols, n * rows, re)
                    put(e * cols, depth + n * rows, im)
                    put(size + e * cols, n * rows, im)
                    put(size + e * cols, depth + n * rows, -re)
                edge = jnp.concatenate(edges + [jnp.zeros((edge_rows - epochs, rows), f32)], 0)
                put(body, n * rows, edge)
                put(body, depth + n * rows, jnp.zeros_like(edge))
                put(size + body, n * rows, jnp.zeros_like(edge))
                put(size + body, depth + n * rows, -edge)
            order = [(q ^ m) % pairs for m in members]
            table = [
                jnp.concatenate([table_ref[n, odd, kind, i] for kind in range(2) for i in order], 0)
                for n in range(2)
            ]
            here = slice(odd * half, (odd + 1) * half)
            plane = mul3((left_high[...], left_low[...]), table)
            plane_ref[:, here] = plane if partial is None else plane + partial_ref[:, here]

    ins = [("v", blocks[m + pairs]) for m in members] + [("v", blocks[m]) for m in members]
    ins.append(("v", plan.down))
    if partial is not None:
        ins.append(("v", partial))
    (plane,) = call(
        kernel,
        [("v", (2 * size, side))],
        ins,
        [pltpu.VMEM((2 * size, 2 * depth), bf16), pltpu.VMEM((2 * size, 2 * depth), bf16)],
        micros=1.0,
    )
    return plane


def column_inverse(plan, spectrum, gain, cross, numer, begin, end):
    slabs, cols, rows, half, side, lanes, halo, tall = (
        plan.slabs, plan.cols, plan.rows, plan.half, plan.side, plan.lanes, plan.halo, plan.tall,
    )
    size = gain.shape[0]
    body = size - edge_rows
    epochs = end - begin
    pieces = len(numer)
    piece = side // pieces

    def kernel(spectrum_ref, gain_ref, cross_ref, *rest):
        numer_refs, table_ref = rest[:pieces], rest[pieces]
        outs = rest[pieces + 1 : pieces + 1 + slabs]
        whole, right_high, right_low, planes = rest[pieces + 1 + slabs :]
        q, z = slab_of(), lax.axis_index("epoch") if pieces > 1 else 0
        for m in range(pieces):
            whole[z ^ m] = numer_refs[m][...]
        flag = jnp.broadcast_to(q, (cols, half)) == 0
        packed = flag & (lax.broadcasted_iota(jnp.int32, (cols, half), 0) == 0)
        results = []
        for odd in range(2):
            here = slice(odd * half, (odd + 1) * half)
            step = min(piece, half)
            parts = [
                whole[at // piece, :, at % piece : at % piece + step]
                for at in range(odd * half, (odd + 1) * half, step)
            ]
            numer_all = parts[0] if len(parts) == 1 else jnp.concatenate(parts, 1)

            def difference(at, lines, nre, nim):
                gain_, cre = gain_ref[at : at + lines, here], cross_ref[at : at + lines, here]
                cim = cross_ref[size + at : size + at + lines, here]
                mre = spectrum_ref[at : at + lines, here]
                mim = spectrum_ref[size + at : size + at + lines, here]
                return gain_ * mre - (cre * nre - cim * nim), gain_ * mim - (cre * nim + cim * nre)

            for i in range(epochs):
                e = begin + i
                edge_re, edge_im = difference(
                    body + e, 1,
                    numer_all[lanes : lanes + 1], numer_all[lanes + 1 : lanes + 2],
                )
                re, im = difference(e * cols, cols, numer_all[:cols], numer_all[cols:lanes])
                im_left = jnp.where(packed, edge_re, im)
                im_right = jnp.where(packed, -edge_im, re)
                for base, start, entry in (
                    (0, 0, re), (0, half, -im), (cols, 0, im_left), (cols, half, im_right),
                ):
                    where = (
                        slice(i * lanes + base, i * lanes + base + cols),
                        slice(start, start + half),
                    )
                    right_high[where], right_low[where] = split(entry)
            results.append(
                mul3((table_ref[0, odd], table_ref[1, odd]), (right_high[...], right_low[...]), True)
            )
        planes[halo : halo + half] = results[0] + results[1]
        planes[halo + half : halo + side] = results[0] - results[1]
        planes[:halo] = planes[side : side + halo]
        planes[halo + side :] = planes[halo : 2 * halo]
        for m in range(slabs):
            start = pl.multiple_of((q ^ m) * rows, rows)
            for i in range(epochs):
                outs[m][i] = planes[pl.ds(start, tall), i * lanes : (i + 1) * lanes]

    return call(
        kernel,
        [("v", (epochs, tall, lanes))] * slabs,
        [("v", spectrum), ("v", gain), ("v", cross)] + [("v", n) for n in numer]
        + [("v", plan.up)],
        [pltpu.VMEM((pieces, lanes + 8, piece), f32),
         pltpu.VMEM((epochs * lanes, side), bf16), pltpu.VMEM((epochs * lanes, side), bf16),
         pltpu.VMEM((side + 2 * halo, epochs * lanes), f32)],
        micros=1.35,
    )


def column_choice(side, src_col):
    groups, group = src_col.shape

    def kernel(col_ref, out_ref):
        column = lax.broadcasted_iota(jnp.int32, (side, group), 0)

        @pl.loop(0, groups)
        def _(g):
            out_ref[g] = (column == col_ref[pl.ds(g, 1)]).astype(f32).astype(bf16)

    (chosen,) = call(
        kernel, [("v", (groups, side, group), bf16)], [("v", src_col)], micros=2.0
    )
    return chosen


def inverse_rows(plan, q, left, table_ref):
    pairs, lanes = plan.pairs, plan.lanes
    sums = []
    for group in range(2):
        table = [
            jnp.concatenate([table_ref[n, d] for d in owners_of(plan, q, group)], 0) for n in range(2)
        ]
        here = slice(group * pairs * lanes, (group + 1) * pairs * lanes)
        sums.append(mul3((left[0][:, here], left[1][:, here]), table))
    sign = jnp.where(q < pairs, 1.0, -1.0).astype(f32)
    return sums[0] + sums[1], sign * (sums[0] - sums[1])


def row_images(plan, returned):
    slabs, rows, half, side, lanes, halo = (
        plan.slabs, plan.rows, plan.half, plan.side, plan.lanes, plan.halo,
    )
    counts = [blocks[0].shape[0] for blocks in returned]
    epochs = sum(counts)

    def kernel(*rest):
        ins, table_ref, diff_ref = rest[: -6], rest[-6], rest[-5]
        left_high, left_low, image_ref, sems = rest[-4:]
        q = slab_of()
        copies = []
        begin = 0
        for i, count in enumerate(counts):
            total = count * rows
            for m in range(slabs):
                here = slice(m * lanes, (m + 1) * lanes)
                value = ins[i * slabs + m][:, halo : halo + rows, :].reshape(total, lanes)
                left_high[:total, here], left_low[:total, here] = split(value)
            left = (left_high[:total], left_low[:total])
            for part, value in enumerate(inverse_rows(plan, q, left, table_ref)):
                image_ref[begin : begin + count, :, part * half : (part + 1) * half] = value.reshape(
                    count, rows, half
                )
            where = pl.ds(begin, count)
            copies.append(pltpu.make_async_copy(image_ref.at[where], diff_ref.at[where], sems.at[i]))
            copies[-1].start()
            begin += count
        for copy in copies:
            copy.wait()

    left = pltpu.VMEM((max(counts) * rows, side), bf16)
    (difference,) = call(
        kernel,
        [("h", (epochs, rows, side))],
        [("v", b) for blocks in returned for b in blocks] + [("v", plan.back)],
        [left, left, pltpu.VMEM((epochs, rows, side), f32), pltpu.SemaphoreType.DMA((len(counts),))],
        micros=2.2,
    )
    return difference


def pick(plan, q, flux_ref, chosen_ref, row_ref, groups):
    rows = plan.rows
    total = flux_ref.shape[0] // 2
    line = lax.broadcasted_iota(jnp.int32, (rows, row_ref.shape[1]), 0)
    parts = []
    for g in groups:
        values = mul(flux_ref[...], chosen_ref[g])
        values = values[:total] + values[total:]
        inside = line == row_ref[pl.ds(g, 1)] - q * rows
        found = [
            jnp.sum(jnp.where(inside, values[at : at + rows], 0.0), axis=0, keepdims=True)
            for at in range(0, total, rows)
        ]
        parts.append(jnp.concatenate(found, 0))
    return jnp.concatenate(parts, 1)


def row_fluxes(plan, order, blocks, taps, begin, epochs, src_row, chosen, earlier):
    slabs, pairs, rows, half, side, lanes, stamp = (
        plan.slabs, plan.pairs, plan.rows, plan.half, plan.side, plan.lanes, plan.stamp,
    )
    mine = blocks[0].shape[0]
    groups, group = src_row.shape
    each = groups // slabs
    total = mine * rows
    step = min(64, rows)
    last = begin + mine == epochs

    def kernel(row_ref, chosen_ref, taps_ref, *rest):
        ins, table_ref, rest = rest[:slabs], rest[slabs], rest[slabs + 1 :]
        ins = [ins[order.index(m)] for m in range(slabs)]
        if begin:
            earlier_ref, rest = rest[0], rest[1:]
        flux_ref, *outs, left_high, left_low = rest
        q = slab_of()
        for m in range(slabs):
            d = q ^ m
            here = slice(m * lanes, (m + 1) * lanes)
            for i in range(mine):
                for start in range(0, rows, step):
                    straight = jnp.zeros((step, lanes), f32)
                    crossed = jnp.zeros((step, lanes), f32)
                    for shift in range(8):
                        shifted = ins[m][i, start + shift : start + shift + step + stamp - 8, :]
                        for base in range(0, stamp, 8):
                            value = shifted[base : base + step]
                            at = (begin + i) * stamp + base + shift
                            straight += taps_ref[0, d, at : at + 1] * value
                            crossed += taps_ref[1, d, at : at + 1] * value
                    at = i * rows + start
                    left_high[at : at + step, here], left_low[at : at + step, here] = split(
                        straight + swap_halves(plan, crossed)
                    )
        for part, value in enumerate(
            inverse_rows(plan, q, (left_high[...], left_low[...]), table_ref)
        ):
            here = slice(part * half, (part + 1) * half)
            flux_ref[:total, here], flux_ref[total:, here] = split(value)
        for m in range(1 if last else 0, slabs):
            owner = q ^ m if last else m
            out = outs[m - 1] if last else outs[0].at[m]
            if begin:
                out[:begin] = earlier_ref[owner]
            out[begin:] = pick(
                plan, q, flux_ref, chosen_ref, row_ref, [owner * each + i for i in range(each)]
            )

    left = pltpu.VMEM((total, side), bf16)
    shape = (begin + mine, each * group)
    ins = [("v", src_row), ("v", chosen), ("v", taps)]
    ins += [("v", blocks[m]) for m in order] + [("v", plan.back)]
    if begin:
        ins.append(("v", earlier))
    flux, *picked = call(
        kernel,
        [("v", (2 * total, side), bf16)] + ([("v", shape)] * (slabs - 1) if last else [("v", (slabs, *shape))]),
        ins,
        [left, left],
        micros=3.5,
    )
    return flux, picked


def own_fluxes(plan, flux, begin, src_row, chosen, earlier):
    groups, group = src_row.shape
    each = groups // plan.slabs
    epochs = begin + flux.shape[0] // 2 // plan.rows

    def kernel(row_ref, chosen_ref, flux_ref, *rest):
        out, q = rest[-1], slab_of()
        if begin:
            out[:begin] = rest[0][q]
        out[begin:] = pick(plan, q, flux_ref, chosen_ref, row_ref, [q * each + i for i in range(each)])

    ins = [("v", src_row), ("v", chosen), ("v", flux)]
    return call(
        kernel,
        [("v", (epochs, each * group))],
        ins + ([("v", earlier)] if begin else []),
        micros=0.9,
    )


def trade(parts, axes, count):
    result = list(parts)
    for m in reversed(range(1, count)):
        result[m] = lax.ppermute(parts[m], axes, [(i, i ^ m) for i in range(count)])
    return result


def make_shards(mesh):
    slabs = mesh.shape["tile"] * mesh.shape["sub"]
    ranks = mesh.shape["epoch"]

    def shards(epoch_images, psf_bank, psf_index, flux_scale, noise_level, src_row, src_col):
        epochs, rows, side = epoch_images.shape
        plan = Plan(side, slabs, psf_bank.shape[1])
        direct = ranks & (ranks - 1) == 0 and side // ranks % 128 == 0
        pieces = ranks if direct else 1
        group = math.gcd(512, src_row.shape[0] // slabs)
        scalars = (psf_index, flux_scale, noise_level)

        edges = list(range(0, epochs, 2)) + [epochs]
        parties = list(zip(edges, edges[1:]))

        far, shares, weighted, images, table = row_transform_far(
            plan, *scalars, epoch_images, psf_bank, side // pieces
        )
        half = slabs // 2
        near, near_rows = row_transform_near(plan, weighted, images, table)
        near = coadd_rest(plan, weighted, near_rows, list(range(half - 1))) + [near]
        (blocks,) = row_transform(plan, images, table, [(0, epochs)])
        numer = trade(near + far, slab_axes, slabs)
        order = list(range(half, slabs)) + list(range(half))[::-1]
        numer, blocks = lax.optimization_barrier(([numer[m] for m in order], blocks))
        numer = numerator(plan, shares, order, numer, pieces)
        bank, numer = lax.optimization_barrier((psf_bank, numer))
        spectrum, power, taps = psf_planes(plan, bank, psf_index)
        blocks = trade(blocks, slab_axes, slabs)
        if direct:
            own = sum(trade(numer, "epoch", ranks)[::-1])
            own, spectrum = lax.optimization_barrier((own, spectrum))
            numer = trade([own] * ranks, "epoch", ranks)
        else:
            own = lax.psum(numer[0], "epoch")
            numer = [own]
        gain, cross = filter_gains(plan, flux_scale, noise_level, own, spectrum, power)
        image = None
        if plan.pairs > 1:
            image = column_transform(plan, [0], blocks, None)
        image = column_transform(plan, list(range(1, plan.pairs)), blocks, image)
        returned = []
        for begin, end in parties:
            rows_back = column_inverse(plan, image, gain, cross, numer, begin, end)
            returned.append(trade(rows_back, slab_axes, slabs))
        chosen = column_choice(side, src_col.reshape(-1, group))
        src_row = src_row.reshape(-1, group)
        earlier = None
        for (begin, end), block in zip(parties, returned):
            flux, picked = row_fluxes(plan, order, block, taps, begin, epochs, src_row, chosen, earlier)
            if end < epochs:
                (earlier,) = picked
        picked = [*own_fluxes(plan, flux, begin, src_row, chosen, earlier), *picked]
        difference = row_images(plan, returned)
        return difference, sum(trade(picked, slab_axes, slabs)[::-1])

    return shards


def solution(mesh):
    in_specs = (
        P(("grp", "epoch"), ("tile", "sub"), None),
        P(),
        P(("grp", "epoch")),
        P(("grp", "epoch")),
        P(("grp", "epoch")),
        P("grp"),
        P("grp"),
    )
    out_specs = (P(("grp", "epoch"), ("tile", "sub"), None), P(("grp", "epoch"), ("tile", "sub")))
    return jax.shard_map(
        make_shards(mesh), mesh=mesh, in_specs=in_specs, out_specs=out_specs, check_vma=False
    )
```

```python
import math

import jax
import jax.numpy as jnp
import ml_dtypes
import numpy as np
from jax import lax
from jax.experimental import pallas as pl
from jax.experimental.pallas import tpu as pltpu
from jax.sharding import PartitionSpec as P

reg_floor = 0.01
vmem_limit = 40 * 1024 * 1024
bf16, f32 = jnp.bfloat16, jnp.float32
hbm_rate = 3.69e6
slab_axes = ("tile", "sub")
edge_rows = 16


def halves(table):
    table = np.asarray(table, np.float64)
    high = table.astype(ml_dtypes.bfloat16)
    return np.stack([high, (table - high.astype(np.float64)).astype(ml_dtypes.bfloat16)])


def split(value):
    high = value.astype(bf16)
    return high, (value - high.astype(f32)).astype(bf16)


def slab_of():
    return lax.axis_index(slab_axes)


def angle(first, second, length):
    return np.outer(first, second) % length * (2.0 * math.pi / length)


def mul(left, right, transposed=False):
    dims = (((1,), (1,)), ((), ())) if transposed else (((1,), (0,)), ((), ()))
    return lax.dot_general(left, right, dims, preferred_element_type=f32)


def mul3(left, right, transposed=False):
    return (
        mul(left[0], right[0], transposed)
        + mul(left[1], right[0], transposed)
        + mul(left[0], right[1], transposed)
    )


class Plan:
    def __init__(self, side, slabs, stamp):
        self.side, self.slabs, self.stamp = side, slabs, stamp
        half = self.half = side // 2
        cols = self.cols = half // slabs
        lanes = self.lanes = 2 * cols
        rows = self.rows = side // slabs
        pairs = self.pairs = slabs // 2
        self.halo = stamp // 2
        self.tall = rows + 2 * self.halo
        self.band = cols + 8
        owner = np.arange(slabs)[:, None]
        freq = 2 * (cols * (owner % pairs) + np.arange(cols)[None, :]) + owner // pairs
        short = np.arange(half)
        taps = np.arange(stamp) - stamp // 2
        order = np.concatenate([2 * short, 2 * short + 1])

        ahead = np.zeros((slabs, 2, cols, half))
        back = np.zeros((slabs, 2, cols, half))
        coef = np.zeros((stamp, 2, slabs, 2, cols))
        shift = np.zeros((slabs, 2, self.band, 2, stamp))
        for d in range(slabs):
            th = angle(freq[d], short, side)
            ahead[d, 0], ahead[d, 1] = np.cos(th), -np.sin(th)
            back[d, 0], back[d, 1] = 2 * np.cos(th) / side, -2 * np.sin(th) / side
            tb = angle(taps, freq[d], side)
            coef[:, 0, d, 0] = coef[:, 0, d, 1] = np.cos(tb)
            coef[:, 1, d, 0], coef[:, 1, d, 1] = np.sin(tb), -np.sin(tb)
            te = angle(np.concatenate([freq[d], [half]]), taps, side)
            ce, se = np.cos(te), np.sin(te)
            shift[d, 0, : cols + 1, 0], shift[d, 0, : cols + 1, 1] = ce, -se
            shift[d, 1, : cols + 1, 0], shift[d, 1, : cols + 1, 1] = -se, -ce
        nyquist = np.cos(math.pi * short)
        ahead[0, 1, 0] = nyquist
        back[0, 0, 0], back[0, 1, 0] = 1.0 / side, nyquist / side
        coef[:, 0, 0, 1, 0], coef[:, 1, 0, 1, 0] = np.cos(math.pi * taps), 0.0
        self.ahead = halves(ahead.reshape(slabs, lanes, half))
        self.back = halves(back.reshape(slabs, lanes, half))
        self.coef = coef.reshape(stamp, 2 * slabs * lanes).astype(np.float32)
        self.shift = halves(shift.reshape(slabs, 2 * self.band, 2 * stamp))

        down = np.zeros((2, 2, half, half))
        up = np.zeros((2, half, 2 * half))
        for odd in range(2):
            th = angle(short, 2 * short + odd, side)
            down[odd, 0], down[odd, 1] = np.cos(th), np.sin(th)
            up[odd, :, :half], up[odd, :, half:] = np.cos(th) / side, np.sin(th) / side
        self.down = halves(down.reshape(2, 2, pairs, rows, half))
        self.up = halves(up)
        tu = angle(taps, order, side)
        high, low = halves(np.concatenate([np.cos(tu), np.sin(tu)], 0))
        self.spread = np.concatenate([high, high, low, np.zeros_like(high)], 0)


def call(kernel, outs, ins, scratch=(), aliases=None, micros=0.0):
    space = {"s": pltpu.SMEM, "v": pltpu.VMEM, "h": pl.ANY, "m": pltpu.HBM}
    ins = [
        (kind, pltpu.with_memory_space_constraint(jnp.asarray(a), pltpu.HBM) if kind == "m" else a)
        for kind, a in ins
    ]
    return pl.pallas_call(
        kernel,
        out_shape=tuple(jax.ShapeDtypeStruct(shape, (*kind, f32)[0]) for _, shape, *kind in outs),
        in_specs=[pl.BlockSpec(memory_space=space[kind]) for kind, _ in ins],
        out_specs=tuple(pl.BlockSpec(memory_space=space[out[0]]) for out in outs),
        scratch_shapes=list(scratch),
        input_output_aliases=aliases or {},
        compiler_params=pltpu.CompilerParams(vmem_limit_bytes=vmem_limit),
        cost_estimate=pl.CostEstimate(flops=0, bytes_accessed=int(micros * hbm_rate), transcendentals=0),
    )(*[a for _, a in ins])


def filter_taps(plan, bank_ref, coef_ref, index_ref, epochs, factor, taps_ref):
    stamp, slabs, lanes = plan.stamp, plan.slabs, plan.lanes
    filters = []
    for e in range(epochs):
        own = bank_ref[index_ref[e]]
        own = own / jnp.sum(own, keepdims=True)
        filters.append(factor(e, own))
    taps = jnp.dot(
        jnp.concatenate(filters, 0), coef_ref[...],
        precision=lax.Precision.HIGHEST, preferred_element_type=f32,
    )
    for kind in range(2):
        for d in range(slabs):
            start = (kind * slabs + d) * lanes
            taps_ref[kind, d] = taps[:, start : start + lanes]


def swap_halves(plan, value):
    return jnp.concatenate([value[:, plan.cols :], value[:, : plan.cols]], 1)


def owners_of(plan, q, group):
    return [q ^ (group * plan.pairs + m) for m in range(plan.pairs)]


def row_operands(plan, q, group, x_ref, table_ref):
    half = plan.half
    x = x_ref[...].reshape(-1, 2 * half)
    first, second = x[:, :half], x[:, half:]
    sign = jnp.where((q >= plan.pairs) != (group == 1), -1.0, 1.0).astype(f32)
    data = split(first + sign * second)
    table = [
        jnp.concatenate([table_ref[n, d] for d in owners_of(plan, q, group)], 0) for n in range(2)
    ]
    return data, table


def lay_rows(plan, q, group, x_ref, table_ref, padded):
    rows, lanes, stamp, pairs = plan.rows, plan.lanes, plan.stamp, plan.pairs
    epochs = x_ref.shape[0]
    padded[:, :, :stamp] = jnp.zeros((pairs, epochs, stamp, lanes), f32)
    padded[:, :, stamp + rows :] = jnp.zeros((pairs, epochs, stamp, lanes), f32)
    data, table = row_operands(plan, q, group, x_ref, table_ref)
    upright = mul3(data, table, True)
    for m in range(pairs):
        for e in range(epochs):
            padded[m, e, stamp : stamp + rows] = upright[
                e * rows : (e + 1) * rows, m * lanes : (m + 1) * lanes
            ]


def coadd_rows(plan, q, mask, padded, taps_ref, out):
    lanes, tall, stamp = plan.lanes, plan.tall, plan.stamp
    step = tall // 2
    d, m = q ^ mask, mask % plan.pairs
    for start in range(0, tall, step):
        straight = jnp.zeros((step, lanes), f32)
        crossed = jnp.zeros((step, lanes), f32)
        for e in range(padded.shape[1]):
            for shift in range(8):
                shifted = padded[m, e, start + shift : start + shift + step + stamp - 8, :]
                for base in range(0, stamp, 8):
                    value = shifted[base : base + step]
                    at = e * stamp + base + shift
                    straight += taps_ref[0, d, at : at + 1] * value
                    crossed += taps_ref[1, d, at : at + 1] * value
        out[start : start + step] = straight + swap_halves(plan, crossed)


def padded_shape(plan, epochs):
    return plan.pairs, epochs, plan.rows + 2 * plan.stamp, plan.lanes


def row_transform_far(plan, index, flux, noise, images, bank, piece):
    epochs = images.shape[0]
    slabs, pairs, lanes, stamp = plan.slabs, plan.pairs, plan.lanes, plan.stamp

    def kernel(*rest):
        sources, outs, rest = rest[:7], rest[7 : 7 + pairs], rest[7 + pairs :]
        shares_ref, taps_ref, x_ref, table_ref, index_ref, flux_ref, noise_ref, bank_ref, coef_ref = rest[:9]
        padded, sems = rest[9:]
        targets = [index_ref, flux_ref, noise_ref, bank_ref, coef_ref, x_ref, table_ref]
        copies = [pltpu.make_async_copy(sources[i], targets[i], sems.at[i]) for i in range(7)]
        for copy in copies:
            copy.start()
        for copy in copies[:5]:
            copy.wait()
        filter_taps(
            plan, bank_ref, coef_ref, index_ref, epochs,
            lambda e, own: own * (flux_ref[e] / (noise_ref[e] * noise_ref[e])), taps_ref,
        )
        lane = lax.broadcasted_iota(jnp.int32, (1, piece), 1)
        shares = jnp.zeros((1, piece), f32)
        for e in range(epochs):
            ratio = flux_ref[e] / noise_ref[e]
            shares += jnp.where(lane == index_ref[e], ratio * ratio, 0.0)
        shares_ref[...] = shares
        for copy in copies[5:]:
            copy.wait()
        lay_rows(plan, slab_of(), 1, x_ref, table_ref, padded)
        for m in range(pairs):
            coadd_rows(plan, slab_of(), pairs + m, padded, taps_ref, outs[m])

    flat = call(
        kernel,
        [("v", (plan.tall, lanes))] * pairs
        + [("v", (1, piece)), ("v", (2, slabs, epochs * stamp, lanes)), ("v", images.shape), ("v", plan.ahead.shape, bf16)],
        [("m", index), ("m", flux), ("m", noise), ("m", bank), ("m", plan.coef),
         ("m", images), ("m", plan.ahead)],
        [pltpu.SMEM(index.shape, jnp.int32), pltpu.SMEM(flux.shape, f32), pltpu.SMEM(noise.shape, f32),
         pltpu.VMEM(bank.shape, f32), pltpu.VMEM(plan.coef.shape, f32)]
        + [pltpu.VMEM(padded_shape(plan, epochs), f32), pltpu.SemaphoreType.DMA((7,))],
        micros=3.2,
    )
    return list(flat[:pairs]), *flat[pairs:]


def row_transform_near(plan, taps, images, table):
    pairs = plan.pairs

    def kernel(taps_ref, x_ref, table_ref, out, padded):
        lay_rows(plan, slab_of(), 0, x_ref, table_ref, padded)
        coadd_rows(plan, slab_of(), pairs - 1, padded, taps_ref, out)

    return call(
        kernel,
        [("v", (plan.tall, plan.lanes)), ("v", padded_shape(plan, images.shape[0]))],
        [("v", taps), ("v", images), ("v", table)],
        micros=1.6,
    )


def coadd_rest(plan, taps, padded, masks):
    def kernel(taps_ref, padded_ref, *outs):
        for mask, out in zip(masks, outs):
            coadd_rows(plan, slab_of(), mask, padded_ref, taps_ref, out)

    return list(call(
        kernel,
        [("v", (plan.tall, plan.lanes))] * len(masks),
        [("v", taps), ("v", padded)],
        micros=1.0 * len(masks),
    ))


def row_transform(plan, images, table, parties):
    slabs, pairs, lanes, rows = plan.slabs, plan.pairs, plan.lanes, plan.rows

    def kernel(x_ref, table_ref, *outs):
        for group in range(2):
            data, table = row_operands(plan, slab_of(), group, x_ref, table_ref)
            result = mul3(table, data, True)
            for i, (begin, end) in enumerate(parties):
                for m in range(pairs):
                    outs[i * slabs + group * pairs + m][...] = result[
                        m * lanes : (m + 1) * lanes, begin * rows : end * rows
                    ]

    flat = call(
        kernel,
        [("v", (lanes, (end - begin) * rows)) for begin, end in parties for _ in range(slabs)],
        [("v", images), ("v", table)],
        micros=1.3,
    )
    return [list(flat[i * slabs : (i + 1) * slabs]) for i in range(len(parties))]


def numerator(plan, shares, order, blocks, pieces):
    slabs, cols, rows, half, side, lanes, halo, tall = (
        plan.slabs, plan.cols, plan.rows, plan.half, plan.side, plan.lanes, plan.halo, plan.tall,
    )
    piece = side // pieces

    def kernel(shares_ref, *rest):
        ins, table_ref = rest[:slabs], rest[slabs]
        outs = rest[slabs + 1 : slabs + 1 + pieces]
        whole, parts = rest[slabs + 1 + pieces :]
        q, z = slab_of(), lax.axis_index("epoch") if pieces > 1 else 0
        whole[...] = jnp.zeros((side + 2 * halo, lanes), f32)
        for m, block in zip(order, ins):
            at = pl.multiple_of((q ^ m) * rows, rows)
            whole[pl.ds(at, tall)] += block[...]
        whole[side : side + halo] += whole[:halo]
        whole[halo : 2 * halo] += whole[side + halo :]
        top, bottom = whole[halo : halo + half], whole[halo + half : halo + side]
        row = lax.broadcasted_iota(jnp.int32, (cols, half), 0)
        first = (q == 0).astype(f32)
        keep = 1.0 - first * (row == 0).astype(f32)
        line = lax.broadcasted_iota(jnp.int32, (edge_rows, half), 0)
        for odd in range(2):
            value = (top - bottom if odd else top + bottom).T
            re, im = value[:cols], value[cols:]
            edge = jnp.broadcast_to(im[:1] * first, (edge_rows, half))
            im = im * keep
            left = jnp.concatenate(
                [
                    jnp.concatenate([re, im, jnp.where(line == 0, edge, 0.0)], 0),
                    jnp.concatenate([im, -re, jnp.where(line == 1, -edge, 0.0)], 0),
                ],
                1,
            )
            table = [
                jnp.concatenate([table_ref[n, odd, kind].reshape(half, half) for kind in range(2)], 0)
                for n in range(2)
            ]
            plane = mul3(split(left), table)[: lanes + 8]
            step = min(piece, half)
            for i in range(half // step):
                at = odd * half + i * step
                parts[at // piece, :, at % piece : at % piece + step] = plane[:, i * step : (i + 1) * step]
        for m in range(pieces):
            parts[m, lanes + 2 : lanes + 3] = shares_ref[...]
        for m in range(pieces):
            outs[m][...] = parts[z ^ m]

    return call(
        kernel,
        [("v", (lanes + 8, piece))] * pieces,
        [("v", shares)] + [("v", b) for b in blocks]
        + [("v", plan.down)],
        [pltpu.VMEM((side + 2 * halo, lanes), f32), pltpu.VMEM((pieces, lanes + 8, piece), f32)],
        micros=1.15,
    )


def psf_planes(plan, bank, index):
    epochs = index.shape[0]
    count, stamp = bank.shape[:2]
    side, cols, band, slabs, lanes = plan.side, plan.cols, plan.band, plan.slabs, plan.lanes
    body = epochs * cols
    size = body + edge_rows
    pitch = 8 * stamp

    def kernel(
        index_ref, bank_ref, shift_ref, spread_ref, coef_ref,
        spectrum_ref, power_ref, taps_ref, right_ref, plane_ref,
    ):
        q = slab_of()
        stamps = bank_ref[...]
        stamps = stamps / jnp.sum(jnp.sum(stamps, axis=2, keepdims=True), axis=1, keepdims=True)
        blank = jnp.zeros((stamp, stamp), f32)
        for k in range(count):
            pair = jnp.concatenate(
                [jnp.concatenate([stamps[k], blank], 1), jnp.concatenate([blank, stamps[k]], 1)], 0
            )
            for copy in range(4):
                at = k * pitch + copy * 2 * stamp
                right_ref[at : at + 2 * stamp] = pair
        right = split(right_ref[...])
        mixed = mul3((shift_ref[0, q], shift_ref[1, q]), right, True)
        lane = lax.broadcasted_iota(jnp.int32, mixed.shape, 1) % pitch
        middle = (lane >= 2 * stamp) & (lane < 4 * stamp)
        high = mixed.astype(bf16).astype(f32)
        left = jnp.where(middle, mixed - high, high).astype(bf16)
        for k in range(count):
            plane = mul(left[:, k * pitch : (k + 1) * pitch], spread_ref[...])
            plane_ref[k] = plane
            power_ref[k] = plane[:band] * plane[:band] + plane[band:] * plane[band:]
        for e in range(epochs):
            k = index_ref[e]
            for base, start in ((0, 0), (size, band)):
                value = plane_ref[k, start : start + band]
                spectrum_ref[base + e * cols : base + (e + 1) * cols] = value[:cols]
                spectrum_ref[base + body + e : base + body + e + 1] = value[cols : cols + 1]
        none = jnp.zeros((edge_rows - epochs, side), f32)
        spectrum_ref[body + epochs : size] = none
        spectrum_ref[size + body + epochs :] = none
        filter_taps(
            plan, bank_ref, coef_ref, index_ref, epochs,
            lambda e, own: own / jnp.sum(own * own, keepdims=True), taps_ref,
        )

    return call(
        kernel,
        [("v", (2 * size, side)), ("v", (count, band, side)), ("v", (2, slabs, epochs * stamp, lanes))],
        [("s", index), ("v", bank), ("v", plan.shift), ("v", plan.spread), ("v", plan.coef)],
        [pltpu.VMEM((count * pitch, 2 * stamp), f32), pltpu.VMEM((count, 2 * band, side), f32)],
        micros=2.35,
    )


def filter_gains(plan, flux, noise, share, spectrum, power):
    epochs = flux.shape[0]
    count = power.shape[0]
    side, cols = plan.side, plan.cols
    body = epochs * cols
    size = body + edge_rows
    row = plan.lanes + 2

    def kernel(flux_ref, noise_ref, share_ref, spectrum_ref, power_ref, gain_ref, cross_ref):
        shares = [jnp.broadcast_to(share_ref[row : row + 1, k : k + 1], (8, side)) for k in range(count)]
        none = jnp.zeros((edge_rows - epochs, side), f32)
        gain_ref[body + epochs : size] = none
        cross_ref[body + epochs : size] = none
        cross_ref[size + body + epochs :] = none
        for block in range(plan.band // 8):
            total = jnp.full((8, side), reg_floor, f32)
            for k in range(count):
                total += shares[k] * power_ref[k, block * 8 : block * 8 + 8]
            edge = block == cols // 8
            total = total[:1] if edge else total
            lines = 1 if edge else 8
            root = jnp.sqrt(total)
            inverse_root = 1.0 / root
            for e in range(epochs):
                at = body + e if edge else e * cols + block * 8
                re = spectrum_ref[at : at + lines]
                im = spectrum_ref[size + at : size + at + lines]
                scale, sigma = flux_ref[e], noise_ref[e]
                inverse = lax.rsqrt(
                    sigma * sigma * total + scale * scale * (re * re + im * im) + reg_floor
                )
                ratio = scale * inverse * inverse_root
                gain_ref[at : at + lines] = root * inverse
                cross_ref[at : at + lines] = ratio * re
                cross_ref[size + at : size + at + lines] = ratio * im

    return call(
        kernel,
        [("v", (size, side)), ("v", (2 * size, side))],
        [("s", flux), ("s", noise), ("v", share), ("v", spectrum), ("v", power)],
        micros=1.15,
    )


def column_transform(plan, members, blocks, partial):
    pairs, cols, rows, half, side = plan.pairs, plan.cols, plan.rows, plan.half, plan.side
    epochs = blocks[0].shape[1] // rows
    body = epochs * cols
    size = body + edge_rows
    count = len(members)
    depth = count * rows

    def kernel(*rest):
        far, near = rest[:count], rest[count : 2 * count]
        table_ref, rest = rest[2 * count], rest[2 * count + 1 :]
        if partial is not None:
            partial_ref, rest = rest[0], rest[1:]
        plane_ref, left_high, left_low = rest
        q = slab_of()
        first = (q == 0).astype(f32)
        sign = jnp.where(q < pairs, 1.0, -1.0).astype(f32)
        row = lax.broadcasted_iota(jnp.int32, (cols, rows), 0)
        keep = 1.0 - first * (row == 0).astype(f32)

        def put(row_at, lane_at, entry):
            where = (slice(row_at, row_at + entry.shape[0]), slice(lane_at, lane_at + rows))
            left_high[where], left_low[where] = split(entry)

        for odd in range(2):
            for n in range(count):
                lower, upper = near[n][...], far[n][...]
                value = sign * (lower - upper) if odd else lower + upper
                edges = []
                for e in range(epochs):
                    re = value[:cols, e * rows : (e + 1) * rows]
                    im = value[cols:, e * rows : (e + 1) * rows]
                    edges.append(im[:1] * first)
                    im = im * keep
                    put(e * cols, n * rows, re)
                    put(e * cols, depth + n * rows, im)
                    put(size + e * cols, n * rows, im)
                    put(size + e * cols, depth + n * rows, -re)
                edge = jnp.concatenate(edges + [jnp.zeros((edge_rows - epochs, rows), f32)], 0)
                put(body, n * rows, edge)
                put(body, depth + n * rows, jnp.zeros_like(edge))
                put(size + body, n * rows, jnp.zeros_like(edge))
                put(size + body, depth + n * rows, -edge)
            order = [(q ^ m) % pairs for m in members]
            table = [
                jnp.concatenate([table_ref[n, odd, kind, i] for kind in range(2) for i in order], 0)
                for n in range(2)
            ]
            here = slice(odd * half, (odd + 1) * half)
            plane = mul3((left_high[...], left_low[...]), table)
            plane_ref[:, here] = plane if partial is None else plane + partial_ref[:, here]

    ins = [("v", blocks[m + pairs]) for m in members] + [("v", blocks[m]) for m in members]
    ins.append(("v", plan.down))
    if partial is not None:
        ins.append(("v", partial))
    (plane,) = call(
        kernel,
        [("v", (2 * size, side))],
        ins,
        [pltpu.VMEM((2 * size, 2 * depth), bf16), pltpu.VMEM((2 * size, 2 * depth), bf16)],
        micros=1.0,
    )
    return plane


def column_inverse(plan, spectrum, gain, cross, numer, begin, end):
    slabs, cols, rows, half, side, lanes, halo, tall = (
        plan.slabs, plan.cols, plan.rows, plan.half, plan.side, plan.lanes, plan.halo, plan.tall,
    )
    size = gain.shape[0]
    body = size - edge_rows
    epochs = end - begin
    pieces = len(numer)
    piece = side // pieces

    def kernel(spectrum_ref, gain_ref, cross_ref, *rest):
        numer_refs, table_ref = rest[:pieces], rest[pieces]
        outs = rest[pieces + 1 : pieces + 1 + slabs]
        whole, right_high, right_low, planes = rest[pieces + 1 + slabs :]
        q, z = slab_of(), lax.axis_index("epoch") if pieces > 1 else 0
        for m in range(pieces):
            whole[z ^ m] = numer_refs[m][...]
        flag = jnp.broadcast_to(q, (cols, half)) == 0
        packed = flag & (lax.broadcasted_iota(jnp.int32, (cols, half), 0) == 0)
        results = []
        for odd in range(2):
            here = slice(odd * half, (odd + 1) * half)
            step = min(piece, half)
            parts = [
                whole[at // piece, :, at % piece : at % piece + step]
                for at in range(odd * half, (odd + 1) * half, step)
            ]
            numer_all = parts[0] if len(parts) == 1 else jnp.concatenate(parts, 1)

            def difference(at, lines, nre, nim):
                gain_, cre = gain_ref[at : at + lines, here], cross_ref[at : at + lines, here]
                cim = cross_ref[size + at : size + at + lines, here]
                mre = spectrum_ref[at : at + lines, here]
                mim = spectrum_ref[size + at : size + at + lines, here]
                return gain_ * mre - (cre * nre - cim * nim), gain_ * mim - (cre * nim + cim * nre)

            for i in range(epochs):
                e = begin + i
                edge_re, edge_im = difference(
                    body + e, 1,
                    numer_all[lanes : lanes + 1], numer_all[lanes + 1 : lanes + 2],
                )
                re, im = difference(e * cols, cols, numer_all[:cols], numer_all[cols:lanes])
                im_left = jnp.where(packed, edge_re, im)
                im_right = jnp.where(packed, -edge_im, re)
                for base, start, entry in (
                    (0, 0, re), (0, half, -im), (cols, 0, im_left), (cols, half, im_right),
                ):
                    where = (
                        slice(i * lanes + base, i * lanes + base + cols),
                        slice(start, start + half),
                    )
                    right_high[where], right_low[where] = split(entry)
            results.append(
                mul3((table_ref[0, odd], table_ref[1, odd]), (right_high[...], right_low[...]), True)
            )
        planes[halo : halo + half] = results[0] + results[1]
        planes[halo + half : halo + side] = results[0] - results[1]
        planes[:halo] = planes[side : side + halo]
        planes[halo + side :] = planes[halo : 2 * halo]
        for m in range(slabs):
            start = pl.multiple_of((q ^ m) * rows, rows)
            for i in range(epochs):
                outs[m][i] = planes[pl.ds(start, tall), i * lanes : (i + 1) * lanes]

    return call(
        kernel,
        [("v", (epochs, tall, lanes))] * slabs,
        [("v", spectrum), ("v", gain), ("v", cross)] + [("v", n) for n in numer]
        + [("v", plan.up)],
        [pltpu.VMEM((pieces, lanes + 8, piece), f32),
         pltpu.VMEM((epochs * lanes, side), bf16), pltpu.VMEM((epochs * lanes, side), bf16),
         pltpu.VMEM((side + 2 * halo, epochs * lanes), f32)],
        micros=1.35,
    )


def column_choice(side, src_col):
    groups, group = src_col.shape

    def kernel(col_ref, out_ref):
        column = lax.broadcasted_iota(jnp.int32, (side, group), 0)

        @pl.loop(0, groups)
        def _(g):
            out_ref[g] = (column == col_ref[pl.ds(g, 1)]).astype(f32).astype(bf16)

    (chosen,) = call(
        kernel, [("v", (groups, side, group), bf16)], [("v", src_col)], micros=2.0
    )
    return chosen


def inverse_rows(plan, q, left, table_ref):
    pairs, lanes = plan.pairs, plan.lanes
    sums = []
    for group in range(2):
        table = [
            jnp.concatenate([table_ref[n, d] for d in owners_of(plan, q, group)], 0) for n in range(2)
        ]
        here = slice(group * pairs * lanes, (group + 1) * pairs * lanes)
        sums.append(mul3((left[0][:, here], left[1][:, here]), table))
    sign = jnp.where(q < pairs, 1.0, -1.0).astype(f32)
    return sums[0] + sums[1], sign * (sums[0] - sums[1])


def row_images(plan, returned):
    slabs, rows, half, side, lanes, halo = (
        plan.slabs, plan.rows, plan.half, plan.side, plan.lanes, plan.halo,
    )
    counts = [blocks[0].shape[0] for blocks in returned]
    epochs = sum(counts)

    def kernel(*rest):
        ins, table_ref, diff_ref = rest[: -6], rest[-6], rest[-5]
        left_high, left_low, image_ref, sems = rest[-4:]
        q = slab_of()
        copies = []
        begin = 0
        for i, count in enumerate(counts):
            total = count * rows
            for m in range(slabs):
                here = slice(m * lanes, (m + 1) * lanes)
                value = ins[i * slabs + m][:, halo : halo + rows, :].reshape(total, lanes)
                left_high[:total, here], left_low[:total, here] = split(value)
            left = (left_high[:total], left_low[:total])
            for part, value in enumerate(inverse_rows(plan, q, left, table_ref)):
                image_ref[begin : begin + count, :, part * half : (part + 1) * half] = value.reshape(
                    count, rows, half
                )
            where = pl.ds(begin, count)
            copies.append(pltpu.make_async_copy(image_ref.at[where], diff_ref.at[where], sems.at[i]))
            copies[-1].start()
            begin += count
        for copy in copies:
            copy.wait()

    left = pltpu.VMEM((max(counts) * rows, side), bf16)
    (difference,) = call(
        kernel,
        [("h", (epochs, rows, side))],
        [("v", b) for blocks in returned for b in blocks] + [("v", plan.back)],
        [left, left, pltpu.VMEM((epochs, rows, side), f32), pltpu.SemaphoreType.DMA((len(counts),))],
        micros=2.2,
    )
    return difference


def pick(plan, q, flux_ref, chosen_ref, row_ref, groups):
    rows = plan.rows
    total = flux_ref.shape[0] // 2
    line = lax.broadcasted_iota(jnp.int32, (rows, row_ref.shape[1]), 0)
    parts = []
    for g in groups:
        values = mul(flux_ref[...], chosen_ref[g])
        values = values[:total] + values[total:]
        inside = line == row_ref[pl.ds(g, 1)] - q * rows
        found = [
            jnp.sum(jnp.where(inside, values[at : at + rows], 0.0), axis=0, keepdims=True)
            for at in range(0, total, rows)
        ]
        parts.append(jnp.concatenate(found, 0))
    return jnp.concatenate(parts, 1)


def row_fluxes(plan, order, blocks, taps, begin, epochs, src_row, chosen, earlier):
    slabs, pairs, rows, half, side, lanes, stamp = (
        plan.slabs, plan.pairs, plan.rows, plan.half, plan.side, plan.lanes, plan.stamp,
    )
    mine = blocks[0].shape[0]
    groups, group = src_row.shape
    each = groups // slabs
    total = mine * rows
    step = min(64, rows)
    last = begin + mine == epochs

    def kernel(row_ref, chosen_ref, taps_ref, *rest):
        ins, table_ref, rest = rest[:slabs], rest[slabs], rest[slabs + 1 :]
        ins = [ins[order.index(m)] for m in range(slabs)]
        if begin:
            earlier_ref, rest = rest[0], rest[1:]
        flux_ref, *outs, left_high, left_low = rest
        q = slab_of()
        for m in range(slabs):
            d = q ^ m
            here = slice(m * lanes, (m + 1) * lanes)
            for i in range(mine):
                for start in range(0, rows, step):
                    straight = jnp.zeros((step, lanes), f32)
                    crossed = jnp.zeros((step, lanes), f32)
                    for shift in range(8):
                        shifted = ins[m][i, start + shift : start + shift + step + stamp - 8, :]
                        for base in range(0, stamp, 8):
                            value = shifted[base : base + step]
                            at = (begin + i) * stamp + base + shift
                            straight += taps_ref[0, d, at : at + 1] * value
                            crossed += taps_ref[1, d, at : at + 1] * value
                    at = i * rows + start
                    left_high[at : at + step, here], left_low[at : at + step, here] = split(
                        straight + swap_halves(plan, crossed)
                    )
        for part, value in enumerate(
            inverse_rows(plan, q, (left_high[...], left_low[...]), table_ref)
        ):
            here = slice(part * half, (part + 1) * half)
            flux_ref[:total, here], flux_ref[total:, here] = split(value)
        for m in range(1 if last else 0, slabs):
            owner = q ^ m if last else m
            out = outs[m - 1] if last else outs[0].at[m]
            if begin:
                out[:begin] = earlier_ref[owner]
            out[begin:] = pick(
                plan, q, flux_ref, chosen_ref, row_ref, [owner * each + i for i in range(each)]
            )

    left = pltpu.VMEM((total, side), bf16)
    shape = (begin + mine, each * group)
    ins = [("v", src_row), ("v", chosen), ("v", taps)]
    ins += [("v", blocks[m]) for m in order] + [("v", plan.back)]
    if begin:
        ins.append(("v", earlier))
    flux, *picked = call(
        kernel,
        [("v", (2 * total, side), bf16)] + ([("v", shape)] * (slabs - 1) if last else [("v", (slabs, *shape))]),
        ins,
        [left, left],
        micros=3.5,
    )
    return flux, picked


def own_fluxes(plan, flux, begin, src_row, chosen, earlier):
    groups, group = src_row.shape
    each = groups // plan.slabs
    epochs = begin + flux.shape[0] // 2 // plan.rows

    def kernel(row_ref, chosen_ref, flux_ref, *rest):
        out, q = rest[-1], slab_of()
        if begin:
            out[:begin] = rest[0][q]
        out[begin:] = pick(plan, q, flux_ref, chosen_ref, row_ref, [q * each + i for i in range(each)])

    ins = [("v", src_row), ("v", chosen), ("v", flux)]
    return call(
        kernel,
        [("v", (epochs, each * group))],
        ins + ([("v", earlier)] if begin else []),
        micros=0.9,
    )


def trade(parts, axes, count):
    result = list(parts)
    for m in reversed(range(1, count)):
        result[m] = lax.ppermute(parts[m], axes, [(i, i ^ m) for i in range(count)])
    return result


def make_shards(mesh):
    slabs = mesh.shape["tile"] * mesh.shape["sub"]
    ranks = mesh.shape["epoch"]

    def shards(epoch_images, psf_bank, psf_index, flux_scale, noise_level, src_row, src_col):
        epochs, rows, side = epoch_images.shape
        plan = Plan(side, slabs, psf_bank.shape[1])
        direct = ranks & (ranks - 1) == 0 and side // ranks % 128 == 0
        pieces = ranks if direct else 1
        group = math.gcd(512, src_row.shape[0] // slabs)
        scalars = (psf_index, flux_scale, noise_level)

        edges = list(range(0, epochs, 2)) + [epochs]
        parties = list(zip(edges, edges[1:]))

        far, shares, weighted, images, table = row_transform_far(
            plan, *scalars, epoch_images, psf_bank, side // pieces
        )
        half = slabs // 2
        near, near_rows = row_transform_near(plan, weighted, images, table)
        near = coadd_rest(plan, weighted, near_rows, list(range(half - 1))) + [near]
        (blocks,) = row_transform(plan, images, table, [(0, epochs)])
        numer = trade(near + far, slab_axes, slabs)
        order = list(range(half, slabs)) + list(range(half))[::-1]
        numer, blocks = lax.optimization_barrier(([numer[m] for m in order], blocks))
        numer = numerator(plan, shares, order, numer, pieces)
        bank, numer = lax.optimization_barrier((psf_bank, numer))
        spectrum, power, taps = psf_planes(plan, bank, psf_index)
        blocks = trade(blocks, slab_axes, slabs)
        if direct:
            own = trade(numer, "epoch", ranks)
            own = sum(own[m] for m in [3, 1, 2, 0])
            own, spectrum = lax.optimization_barrier((own, spectrum))
            numer = trade([own] * ranks, "epoch", ranks)
        else:
            own = lax.psum(numer[0], "epoch")
            numer = [own]
        gain, cross = filter_gains(plan, flux_scale, noise_level, own, spectrum, power)
        image = None
        if plan.pairs > 1:
            image = column_transform(plan, [0], blocks, None)
        image = column_transform(plan, list(range(1, plan.pairs)), blocks, image)
        returned = []
        for begin, end in parties:
            rows_back = column_inverse(plan, image, gain, cross, numer, begin, end)
            returned.append(trade(rows_back, slab_axes, slabs))
        chosen = column_choice(side, src_col.reshape(-1, group))
        src_row = src_row.reshape(-1, group)
        earlier = None
        for (begin, end), block in zip(parties, returned):
            flux, picked = row_fluxes(plan, order, block, taps, begin, epochs, src_row, chosen, earlier)
            if end < epochs:
                (earlier,) = picked
        picked = [*own_fluxes(plan, flux, begin, src_row, chosen, earlier), *picked]
        difference = row_images(plan, returned)
        return difference, sum(trade(picked, slab_axes, slabs)[::-1])

    return shards


def solution(mesh):
    in_specs = (
        P(("grp", "epoch"), ("tile", "sub"), None),
        P(),
        P(("grp", "epoch")),
        P(("grp", "epoch")),
        P(("grp", "epoch")),
        P("grp"),
        P("grp"),
    )
    out_specs = (P(("grp", "epoch"), ("tile", "sub"), None), P(("grp", "epoch"), ("tile", "sub")))
    return jax.shard_map(
        make_shards(mesh), mesh=mesh, in_specs=in_specs, out_specs=out_specs, check_vma=False
    )
```

```python
import math

import jax
import jax.numpy as jnp
import ml_dtypes
import numpy as np
from jax import lax
from jax.experimental import pallas as pl
from jax.experimental.pallas import tpu as pltpu
from jax.sharding import PartitionSpec as P

reg_floor = 0.01
vmem_limit = 40 * 1024 * 1024
bf16, f32 = jnp.bfloat16, jnp.float32
hbm_rate = 3.69e6
slab_axes = ("tile", "sub")
edge_rows = 16


def halves(table):
    table = np.asarray(table, np.float64)
    high = table.astype(ml_dtypes.bfloat16)
    return np.stack([high, (table - high.astype(np.float64)).astype(ml_dtypes.bfloat16)])


def split(value):
    high = value.astype(bf16)
    return high, (value - high.astype(f32)).astype(bf16)


def slab_of():
    return lax.axis_index(slab_axes)


def angle(first, second, length):
    return np.outer(first, second) % length * (2.0 * math.pi / length)


def mul(left, right, transposed=False):
    dims = (((1,), (1,)), ((), ())) if transposed else (((1,), (0,)), ((), ()))
    return lax.dot_general(left, right, dims, preferred_element_type=f32)


def mul3(left, right, transposed=False):
    return (
        mul(left[0], right[0], transposed)
        + mul(left[1], right[0], transposed)
        + mul(left[0], right[1], transposed)
    )


class Plan:
    def __init__(self, side, slabs, stamp):
        self.side, self.slabs, self.stamp = side, slabs, stamp
        half = self.half = side // 2
        cols = self.cols = half // slabs
        lanes = self.lanes = 2 * cols
        rows = self.rows = side // slabs
        pairs = self.pairs = slabs // 2
        self.halo = stamp // 2
        self.tall = rows + 2 * self.halo
        self.band = cols + 8
        owner = np.arange(slabs)[:, None]
        freq = 2 * (cols * (owner % pairs) + np.arange(cols)[None, :]) + owner // pairs
        short = np.arange(half)
        taps = np.arange(stamp) - stamp // 2
        order = np.concatenate([2 * short, 2 * short + 1])

        ahead = np.zeros((slabs, 2, cols, half))
        back = np.zeros((slabs, 2, cols, half))
        coef = np.zeros((stamp, 2, slabs, 2, cols))
        shift = np.zeros((slabs, 2, self.band, 2, stamp))
        for d in range(slabs):
            th = angle(freq[d], short, side)
            ahead[d, 0], ahead[d, 1] = np.cos(th), -np.sin(th)
            back[d, 0], back[d, 1] = 2 * np.cos(th) / side, -2 * np.sin(th) / side
            tb = angle(taps, freq[d], side)
            coef[:, 0, d, 0] = coef[:, 0, d, 1] = np.cos(tb)
            coef[:, 1, d, 0], coef[:, 1, d, 1] = np.sin(tb), -np.sin(tb)
            te = angle(np.concatenate([freq[d], [half]]), taps, side)
            ce, se = np.cos(te), np.sin(te)
            shift[d, 0, : cols + 1, 0], shift[d, 0, : cols + 1, 1] = ce, -se
            shift[d, 1, : cols + 1, 0], shift[d, 1, : cols + 1, 1] = -se, -ce
        nyquist = np.cos(math.pi * short)
        ahead[0, 1, 0] = nyquist
        back[0, 0, 0], back[0, 1, 0] = 1.0 / side, nyquist / side
        coef[:, 0, 0, 1, 0], coef[:, 1, 0, 1, 0] = np.cos(math.pi * taps), 0.0
        self.ahead = halves(ahead.reshape(slabs, lanes, half))
        self.back = halves(back.reshape(slabs, lanes, half))
        self.coef = coef.reshape(stamp, 2 * slabs * lanes).astype(np.float32)
        self.shift = halves(shift.reshape(slabs, 2 * self.band, 2 * stamp))

        down = np.zeros((2, 2, half, half))
        up = np.zeros((2, half, 2 * half))
        for odd in range(2):
            th = angle(short, 2 * short + odd, side)
            down[odd, 0], down[odd, 1] = np.cos(th), np.sin(th)
            up[odd, :, :half], up[odd, :, half:] = np.cos(th) / side, np.sin(th) / side
        self.down = halves(down.reshape(2, 2, pairs, rows, half))
        self.up = halves(up)
        tu = angle(taps, order, side)
        high, low = halves(np.concatenate([np.cos(tu), np.sin(tu)], 0))
        self.spread = np.concatenate([high, high, low, np.zeros_like(high)], 0)


def call(kernel, outs, ins, scratch=(), aliases=None, micros=0.0):
    space = {"s": pltpu.SMEM, "v": pltpu.VMEM, "h": pl.ANY, "m": pltpu.HBM}
    ins = [
        (kind, pltpu.with_memory_space_constraint(jnp.asarray(a), pltpu.HBM) if kind == "m" else a)
        for kind, a in ins
    ]
    return pl.pallas_call(
        kernel,
        out_shape=tuple(jax.ShapeDtypeStruct(shape, (*kind, f32)[0]) for _, shape, *kind in outs),
        in_specs=[pl.BlockSpec(memory_space=space[kind]) for kind, _ in ins],
        out_specs=tuple(pl.BlockSpec(memory_space=space[out[0]]) for out in outs),
        scratch_shapes=list(scratch),
        input_output_aliases=aliases or {},
        compiler_params=pltpu.CompilerParams(vmem_limit_bytes=vmem_limit),
        cost_estimate=pl.CostEstimate(flops=0, bytes_accessed=int(micros * hbm_rate), transcendentals=0),
    )(*[a for _, a in ins])


def filter_taps(plan, bank_ref, coef_ref, index_ref, epochs, factor, taps_ref):
    stamp, slabs, lanes = plan.stamp, plan.slabs, plan.lanes
    filters = []
    for e in range(epochs):
        own = bank_ref[index_ref[e]]
        own = own / jnp.sum(own, keepdims=True)
        filters.append(factor(e, own))
    taps = jnp.dot(
        jnp.concatenate(filters, 0), coef_ref[...],
        precision=lax.Precision.HIGHEST, preferred_element_type=f32,
    )
    for kind in range(2):
        for d in range(slabs):
            start = (kind * slabs + d) * lanes
            taps_ref[kind, d] = taps[:, start : start + lanes]


def swap_halves(plan, value):
    return jnp.concatenate([value[:, plan.cols :], value[:, : plan.cols]], 1)


def owners_of(plan, q, group):
    return [q ^ (group * plan.pairs + m) for m in range(plan.pairs)]


def row_operands(plan, q, group, x_ref, table_ref):
    half = plan.half
    x = x_ref[...].reshape(-1, 2 * half)
    first, second = x[:, :half], x[:, half:]
    sign = jnp.where((q >= plan.pairs) != (group == 1), -1.0, 1.0).astype(f32)
    data = split(first + sign * second)
    table = [
        jnp.concatenate([table_ref[n, d] for d in owners_of(plan, q, group)], 0) for n in range(2)
    ]
    return data, table


def lay_rows(plan, q, group, x_ref, table_ref, padded):
    rows, lanes, stamp, pairs = plan.rows, plan.lanes, plan.stamp, plan.pairs
    epochs = x_ref.shape[0]
    padded[:, :, :stamp] = jnp.zeros((pairs, epochs, stamp, lanes), f32)
    padded[:, :, stamp + rows :] = jnp.zeros((pairs, epochs, stamp, lanes), f32)
    data, table = row_operands(plan, q, group, x_ref, table_ref)
    upright = mul3(data, table, True)
    for m in range(pairs):
        for e in range(epochs):
            padded[m, e, stamp : stamp + rows] = upright[
                e * rows : (e + 1) * rows, m * lanes : (m + 1) * lanes
            ]


def coadd_rows(plan, q, mask, padded, taps_ref, out):
    lanes, tall, stamp = plan.lanes, plan.tall, plan.stamp
    step = tall // 2
    d, m = q ^ mask, mask % plan.pairs
    for start in range(0, tall, step):
        straight = jnp.zeros((step, lanes), f32)
        crossed = jnp.zeros((step, lanes), f32)
        for e in range(padded.shape[1]):
            for shift in range(8):
                shifted = padded[m, e, start + shift : start + shift + step + stamp - 8, :]
                for base in range(0, stamp, 8):
                    value = shifted[base : base + step]
                    at = e * stamp + base + shift
                    straight += taps_ref[0, d, at : at + 1] * value
                    crossed += taps_ref[1, d, at : at + 1] * value
        out[start : start + step] = straight + swap_halves(plan, crossed)


def padded_shape(plan, epochs):
    return plan.pairs, epochs, plan.rows + 2 * plan.stamp, plan.lanes


def row_transform_far(plan, index, flux, noise, images, bank, piece):
    epochs = images.shape[0]
    slabs, pairs, lanes, stamp = plan.slabs, plan.pairs, plan.lanes, plan.stamp

    def kernel(*rest):
        sources, outs, rest = rest[:7], rest[7 : 7 + pairs], rest[7 + pairs :]
        shares_ref, taps_ref, x_ref, table_ref, index_ref, flux_ref, noise_ref, bank_ref, coef_ref = rest[:9]
        padded, sems = rest[9:]
        targets = [index_ref, flux_ref, noise_ref, bank_ref, coef_ref, x_ref, table_ref]
        copies = [pltpu.make_async_copy(sources[i], targets[i], sems.at[i]) for i in range(7)]
        for copy in copies:
            copy.start()
        for copy in copies[:5]:
            copy.wait()
        filter_taps(
            plan, bank_ref, coef_ref, index_ref, epochs,
            lambda e, own: own * (flux_ref[e] / (noise_ref[e] * noise_ref[e])), taps_ref,
        )
        lane = lax.broadcasted_iota(jnp.int32, (1, piece), 1)
        shares = jnp.zeros((1, piece), f32)
        for e in range(epochs):
            ratio = flux_ref[e] / noise_ref[e]
            shares += jnp.where(lane == index_ref[e], ratio * ratio, 0.0)
        shares_ref[...] = shares
        for copy in copies[5:]:
            copy.wait()
        lay_rows(plan, slab_of(), 1, x_ref, table_ref, padded)
        for m in range(pairs):
            coadd_rows(plan, slab_of(), pairs + m, padded, taps_ref, outs[m])

    flat = call(
        kernel,
        [("v", (plan.tall, lanes))] * pairs
        + [("v", (1, piece)), ("v", (2, slabs, epochs * stamp, lanes)), ("v", images.shape), ("v", plan.ahead.shape, bf16)],
        [("m", index), ("m", flux), ("m", noise), ("m", bank), ("m", plan.coef),
         ("m", images), ("m", plan.ahead)],
        [pltpu.SMEM(index.shape, jnp.int32), pltpu.SMEM(flux.shape, f32), pltpu.SMEM(noise.shape, f32),
         pltpu.VMEM(bank.shape, f32), pltpu.VMEM(plan.coef.shape, f32)]
        + [pltpu.VMEM(padded_shape(plan, epochs), f32), pltpu.SemaphoreType.DMA((7,))],
        micros=3.2,
    )
    return list(flat[:pairs]), *flat[pairs:]


def row_transform_near(plan, taps, images, table):
    pairs = plan.pairs

    def kernel(taps_ref, x_ref, table_ref, out, padded):
        lay_rows(plan, slab_of(), 0, x_ref, table_ref, padded)
        coadd_rows(plan, slab_of(), pairs - 1, padded, taps_ref, out)

    return call(
        kernel,
        [("v", (plan.tall, plan.lanes)), ("v", padded_shape(plan, images.shape[0]))],
        [("v", taps), ("v", images), ("v", table)],
        micros=1.6,
    )


def coadd_rest(plan, taps, padded, masks):
    def kernel(taps_ref, padded_ref, *outs):
        for mask, out in zip(masks, outs):
            coadd_rows(plan, slab_of(), mask, padded_ref, taps_ref, out)

    return list(call(
        kernel,
        [("v", (plan.tall, plan.lanes))] * len(masks),
        [("v", taps), ("v", padded)],
        micros=1.0 * len(masks),
    ))


def row_transform(plan, images, table, parties):
    slabs, pairs, lanes, rows = plan.slabs, plan.pairs, plan.lanes, plan.rows

    def kernel(x_ref, table_ref, *outs):
        for group in range(2):
            data, table = row_operands(plan, slab_of(), group, x_ref, table_ref)
            result = mul3(table, data, True)
            for i, (begin, end) in enumerate(parties):
                for m in range(pairs):
                    outs[i * slabs + group * pairs + m][...] = result[
                        m * lanes : (m + 1) * lanes, begin * rows : end * rows
                    ]

    flat = call(
        kernel,
        [("v", (lanes, (end - begin) * rows)) for begin, end in parties for _ in range(slabs)],
        [("v", images), ("v", table)],
        micros=1.3,
    )
    return [list(flat[i * slabs : (i + 1) * slabs]) for i in range(len(parties))]


def numerator(plan, shares, order, blocks, pieces):
    slabs, cols, rows, half, side, lanes, halo, tall = (
        plan.slabs, plan.cols, plan.rows, plan.half, plan.side, plan.lanes, plan.halo, plan.tall,
    )
    piece = side // pieces

    def kernel(shares_ref, *rest):
        ins, table_ref = rest[:slabs], rest[slabs]
        outs = rest[slabs + 1 : slabs + 1 + pieces]
        whole, parts = rest[slabs + 1 + pieces :]
        q, z = slab_of(), lax.axis_index("epoch") if pieces > 1 else 0
        whole[...] = jnp.zeros((side + 2 * halo, lanes), f32)
        for m, block in zip(order, ins):
            at = pl.multiple_of((q ^ m) * rows, rows)
            whole[pl.ds(at, tall)] += block[...]
        whole[side : side + halo] += whole[:halo]
        whole[halo : 2 * halo] += whole[side + halo :]
        top, bottom = whole[halo : halo + half], whole[halo + half : halo + side]
        row = lax.broadcasted_iota(jnp.int32, (cols, half), 0)
        first = (q == 0).astype(f32)
        keep = 1.0 - first * (row == 0).astype(f32)
        line = lax.broadcasted_iota(jnp.int32, (edge_rows, half), 0)
        for odd in range(2):
            value = (top - bottom if odd else top + bottom).T
            re, im = value[:cols], value[cols:]
            edge = jnp.broadcast_to(im[:1] * first, (edge_rows, half))
            im = im * keep
            left = jnp.concatenate(
                [
                    jnp.concatenate([re, im, jnp.where(line == 0, edge, 0.0)], 0),
                    jnp.concatenate([im, -re, jnp.where(line == 1, -edge, 0.0)], 0),
                ],
                1,
            )
            table = [
                jnp.concatenate([table_ref[n, odd, kind].reshape(half, half) for kind in range(2)], 0)
                for n in range(2)
            ]
            plane = mul3(split(left), table)[: lanes + 8]
            step = min(piece, half)
            for i in range(half // step):
                at = odd * half + i * step
                parts[at // piece, :, at % piece : at % piece + step] = plane[:, i * step : (i + 1) * step]
        for m in range(pieces):
            parts[m, lanes + 2 : lanes + 3] = shares_ref[...]
        for m in range(pieces):
            outs[m][...] = parts[z ^ m]

    return call(
        kernel,
        [("v", (lanes + 8, piece))] * pieces,
        [("v", shares)] + [("v", b) for b in blocks]
        + [("v", plan.down)],
        [pltpu.VMEM((side + 2 * halo, lanes), f32), pltpu.VMEM((pieces, lanes + 8, piece), f32)],
        micros=1.15,
    )


def psf_planes(plan, bank, index):
    epochs = index.shape[0]
    count, stamp = bank.shape[:2]
    side, cols, band, slabs, lanes = plan.side, plan.cols, plan.band, plan.slabs, plan.lanes
    body = epochs * cols
    size = body + edge_rows
    pitch = 8 * stamp

    def kernel(
        index_ref, bank_ref, shift_ref, spread_ref, coef_ref,
        spectrum_ref, power_ref, taps_ref, right_ref, plane_ref,
    ):
        q = slab_of()
        stamps = bank_ref[...]
        stamps = stamps / jnp.sum(jnp.sum(stamps, axis=2, keepdims=True), axis=1, keepdims=True)
        blank = jnp.zeros((stamp, stamp), f32)
        for k in range(count):
            pair = jnp.concatenate(
                [jnp.concatenate([stamps[k], blank], 1), jnp.concatenate([blank, stamps[k]], 1)], 0
            )
            for copy in range(4):
                at = k * pitch + copy * 2 * stamp
                right_ref[at : at + 2 * stamp] = pair
        right = split(right_ref[...])
        mixed = mul3((shift_ref[0, q], shift_ref[1, q]), right, True)
        lane = lax.broadcasted_iota(jnp.int32, mixed.shape, 1) % pitch
        middle = (lane >= 2 * stamp) & (lane < 4 * stamp)
        high = mixed.astype(bf16).astype(f32)
        left = jnp.where(middle, mixed - high, high).astype(bf16)
        for k in range(count):
            plane = mul(left[:, k * pitch : (k + 1) * pitch], spread_ref[...])
            plane_ref[k] = plane
            power_ref[k] = plane[:band] * plane[:band] + plane[band:] * plane[band:]
        for e in range(epochs):
            k = index_ref[e]
            for base, start in ((0, 0), (size, band)):
                value = plane_ref[k, start : start + band]
                spectrum_ref[base + e * cols : base + (e + 1) * cols] = value[:cols]
                spectrum_ref[base + body + e : base + body + e + 1] = value[cols : cols + 1]
        none = jnp.zeros((edge_rows - epochs, side), f32)
        spectrum_ref[body + epochs : size] = none
        spectrum_ref[size + body + epochs :] = none
        filter_taps(
            plan, bank_ref, coef_ref, index_ref, epochs,
            lambda e, own: own / jnp.sum(own * own, keepdims=True), taps_ref,
        )

    return call(
        kernel,
        [("v", (2 * size, side)), ("v", (count, band, side)), ("v", (2, slabs, epochs * stamp, lanes))],
        [("s", index), ("v", bank), ("v", plan.shift), ("v", plan.spread), ("v", plan.coef)],
        [pltpu.VMEM((count * pitch, 2 * stamp), f32), pltpu.VMEM((count, 2 * band, side), f32)],
        micros=2.35,
    )


def filter_gains(plan, flux, noise, share, spectrum, power):
    epochs = flux.shape[0]
    count = power.shape[0]
    side, cols = plan.side, plan.cols
    body = epochs * cols
    size = body + edge_rows
    row = plan.lanes + 2

    def kernel(flux_ref, noise_ref, share_ref, spectrum_ref, power_ref, gain_ref, cross_ref):
        shares = [jnp.broadcast_to(share_ref[row : row + 1, k : k + 1], (8, side)) for k in range(count)]
        none = jnp.zeros((edge_rows - epochs, side), f32)
        gain_ref[body + epochs : size] = none
        cross_ref[body + epochs : size] = none
        cross_ref[size + body + epochs :] = none
        for block in range(plan.band // 8):
            total = jnp.full((8, side), reg_floor, f32)
            for k in range(count):
                total += shares[k] * power_ref[k, block * 8 : block * 8 + 8]
            edge = block == cols // 8
            total = total[:1] if edge else total
            lines = 1 if edge else 8
            root = jnp.sqrt(total)
            inverse_root = 1.0 / root
            for e in range(epochs):
                at = body + e if edge else e * cols + block * 8
                re = spectrum_ref[at : at + lines]
                im = spectrum_ref[size + at : size + at + lines]
                scale, sigma = flux_ref[e], noise_ref[e]
                inverse = lax.rsqrt(
                    sigma * sigma * total + scale * scale * (re * re + im * im) + reg_floor
                )
                ratio = scale * inverse * inverse_root
                gain_ref[at : at + lines] = root * inverse
                cross_ref[at : at + lines] = ratio * re
                cross_ref[size + at : size + at + lines] = ratio * im

    return call(
        kernel,
        [("v", (size, side)), ("v", (2 * size, side))],
        [("s", flux), ("s", noise), ("v", share), ("v", spectrum), ("v", power)],
        micros=1.15,
    )


def column_transform(plan, members, blocks, partial):
    pairs, cols, rows, half, side = plan.pairs, plan.cols, plan.rows, plan.half, plan.side
    epochs = blocks[0].shape[1] // rows
    body = epochs * cols
    size = body + edge_rows
    count = len(members)
    depth = count * rows

    def kernel(*rest):
        far, near = rest[:count], rest[count : 2 * count]
        table_ref, rest = rest[2 * count], rest[2 * count + 1 :]
        if partial is not None:
            partial_ref, rest = rest[0], rest[1:]
        plane_ref, left_high, left_low = rest
        q = slab_of()
        first = (q == 0).astype(f32)
        sign = jnp.where(q < pairs, 1.0, -1.0).astype(f32)
        row = lax.broadcasted_iota(jnp.int32, (cols, rows), 0)
        keep = 1.0 - first * (row == 0).astype(f32)

        def put(row_at, lane_at, entry):
            where = (slice(row_at, row_at + entry.shape[0]), slice(lane_at, lane_at + rows))
            left_high[where], left_low[where] = split(entry)

        for odd in range(2):
            for n in range(count):
                lower, upper = near[n][...], far[n][...]
                value = sign * (lower - upper) if odd else lower + upper
                edges = []
                for e in range(epochs):
                    re = value[:cols, e * rows : (e + 1) * rows]
                    im = value[cols:, e * rows : (e + 1) * rows]
                    edges.append(im[:1] * first)
                    im = im * keep
                    put(e * cols, n * rows, re)
                    put(e * cols, depth + n * rows, im)
                    put(size + e * cols, n * rows, im)
                    put(size + e * cols, depth + n * rows, -re)
                edge = jnp.concatenate(edges + [jnp.zeros((edge_rows - epochs, rows), f32)], 0)
                put(body, n * rows, edge)
                put(body, depth + n * rows, jnp.zeros_like(edge))
                put(size + body, n * rows, jnp.zeros_like(edge))
                put(size + body, depth + n * rows, -edge)
            order = [(q ^ m) % pairs for m in members]
            table = [
                jnp.concatenate([table_ref[n, odd, kind, i] for kind in range(2) for i in order], 0)
                for n in range(2)
            ]
            here = slice(odd * half, (odd + 1) * half)
            plane = mul3((left_high[...], left_low[...]), table)
            plane_ref[:, here] = plane if partial is None else plane + partial_ref[:, here]

    ins = [("v", blocks[m + pairs]) for m in members] + [("v", blocks[m]) for m in members]
    ins.append(("v", plan.down))
    if partial is not None:
        ins.append(("v", partial))
    (plane,) = call(
        kernel,
        [("v", (2 * size, side))],
        ins,
        [pltpu.VMEM((2 * size, 2 * depth), bf16), pltpu.VMEM((2 * size, 2 * depth), bf16)],
        micros=1.0,
    )
    return plane


def column_inverse(plan, spectrum, gain, cross, numer, begin, end):
    slabs, cols, rows, half, side, lanes, halo, tall = (
        plan.slabs, plan.cols, plan.rows, plan.half, plan.side, plan.lanes, plan.halo, plan.tall,
    )
    size = gain.shape[0]
    body = size - edge_rows
    epochs = end - begin
    pieces = len(numer)
    piece = side // pieces

    def kernel(spectrum_ref, gain_ref, cross_ref, *rest):
        numer_refs, table_ref = rest[:pieces], rest[pieces]
        outs = rest[pieces + 1 : pieces + 1 + slabs]
        whole, right_high, right_low, planes = rest[pieces + 1 + slabs :]
        q, z = slab_of(), lax.axis_index("epoch") if pieces > 1 else 0
        for m in range(pieces):
            whole[z ^ m] = numer_refs[m][...]
        flag = jnp.broadcast_to(q, (cols, half)) == 0
        packed = flag & (lax.broadcasted_iota(jnp.int32, (cols, half), 0) == 0)
        results = []
        for odd in range(2):
            here = slice(odd * half, (odd + 1) * half)
            step = min(piece, half)
            parts = [
                whole[at // piece, :, at % piece : at % piece + step]
                for at in range(odd * half, (odd + 1) * half, step)
            ]
            numer_all = parts[0] if len(parts) == 1 else jnp.concatenate(parts, 1)

            def difference(at, lines, nre, nim):
                gain_, cre = gain_ref[at : at + lines, here], cross_ref[at : at + lines, here]
                cim = cross_ref[size + at : size + at + lines, here]
                mre = spectrum_ref[at : at + lines, here]
                mim = spectrum_ref[size + at : size + at + lines, here]
                return gain_ * mre - (cre * nre - cim * nim), gain_ * mim - (cre * nim + cim * nre)

            for i in range(epochs):
                e = begin + i
                edge_re, edge_im = difference(
                    body + e, 1,
                    numer_all[lanes : lanes + 1], numer_all[lanes + 1 : lanes + 2],
                )
                re, im = difference(e * cols, cols, numer_all[:cols], numer_all[cols:lanes])
                im_left = jnp.where(packed, edge_re, im)
                im_right = jnp.where(packed, -edge_im, re)
                for base, start, entry in (
                    (0, 0, re), (0, half, -im), (cols, 0, im_left), (cols, half, im_right),
                ):
                    where = (
                        slice(i * lanes + base, i * lanes + base + cols),
                        slice(start, start + half),
                    )
                    right_high[where], right_low[where] = split(entry)
            results.append(
                mul3((table_ref[0, odd], table_ref[1, odd]), (right_high[...], right_low[...]), True)
            )
        planes[halo : halo + half] = results[0] + results[1]
        planes[halo + half : halo + side] = results[0] - results[1]
        planes[:halo] = planes[side : side + halo]
        planes[halo + side :] = planes[halo : 2 * halo]
        for m in range(slabs):
            start = pl.multiple_of((q ^ m) * rows, rows)
            for i in range(epochs):
                outs[m][i] = planes[pl.ds(start, tall), i * lanes : (i + 1) * lanes]

    return call(
        kernel,
        [("v", (epochs, tall, lanes))] * slabs,
        [("v", spectrum), ("v", gain), ("v", cross)] + [("v", n) for n in numer]
        + [("v", plan.up)],
        [pltpu.VMEM((pieces, lanes + 8, piece), f32),
         pltpu.VMEM((epochs * lanes, side), bf16), pltpu.VMEM((epochs * lanes, side), bf16),
         pltpu.VMEM((side + 2 * halo, epochs * lanes), f32)],
        micros=1.35,
    )


def column_choice(side, src_col):
    groups, group = src_col.shape

    def kernel(col_ref, out_ref):
        column = lax.broadcasted_iota(jnp.int32, (side, group), 0)

        @pl.loop(0, groups)
        def _(g):
            out_ref[g] = (column == col_ref[pl.ds(g, 1)]).astype(f32).astype(bf16)

    (chosen,) = call(
        kernel, [("v", (groups, side, group), bf16)], [("v", src_col)], micros=2.0
    )
    return chosen


def inverse_rows(plan, q, left, table_ref):
    pairs, lanes = plan.pairs, plan.lanes
    sums = []
    for group in range(2):
        table = [
            jnp.concatenate([table_ref[n, d] for d in owners_of(plan, q, group)], 0) for n in range(2)
        ]
        here = slice(group * pairs * lanes, (group + 1) * pairs * lanes)
        sums.append(mul3((left[0][:, here], left[1][:, here]), table))
    sign = jnp.where(q < pairs, 1.0, -1.0).astype(f32)
    return sums[0] + sums[1], sign * (sums[0] - sums[1])


def row_images(plan, returned):
    slabs, rows, half, side, lanes, halo = (
        plan.slabs, plan.rows, plan.half, plan.side, plan.lanes, plan.halo,
    )
    counts = [blocks[0].shape[0] for blocks in returned]
    epochs = sum(counts)

    def kernel(*rest):
        ins, table_ref, diff_ref = rest[: -6], rest[-6], rest[-5]
        left_high, left_low, image_ref, sems = rest[-4:]
        q = slab_of()
        copies = []
        begin = 0
        for i, count in enumerate(counts):
            total = count * rows
            for m in range(slabs):
                here = slice(m * lanes, (m + 1) * lanes)
                value = ins[i * slabs + m][:, halo : halo + rows, :].reshape(total, lanes)
                left_high[:total, here], left_low[:total, here] = split(value)
            left = (left_high[:total], left_low[:total])
            for part, value in enumerate(inverse_rows(plan, q, left, table_ref)):
                image_ref[begin : begin + count, :, part * half : (part + 1) * half] = value.reshape(
                    count, rows, half
                )
            where = pl.ds(begin, count)
            copies.append(pltpu.make_async_copy(image_ref.at[where], diff_ref.at[where], sems.at[i]))
            copies[-1].start()
            begin += count
        for copy in copies:
            copy.wait()

    left = pltpu.VMEM((max(counts) * rows, side), bf16)
    (difference,) = call(
        kernel,
        [("h", (epochs, rows, side))],
        [("v", b) for blocks in returned for b in blocks] + [("v", plan.back)],
        [left, left, pltpu.VMEM((epochs, rows, side), f32), pltpu.SemaphoreType.DMA((len(counts),))],
        micros=2.2,
    )
    return difference


def pick(plan, q, flux_ref, chosen_ref, row_ref, groups):
    rows = plan.rows
    total = flux_ref.shape[0] // 2
    line = lax.broadcasted_iota(jnp.int32, (rows, row_ref.shape[1]), 0)
    parts = []
    for g in groups:
        values = mul(flux_ref[...], chosen_ref[g])
        values = values[:total] + values[total:]
        inside = line == row_ref[pl.ds(g, 1)] - q * rows
        found = [
            jnp.sum(jnp.where(inside, values[at : at + rows], 0.0), axis=0, keepdims=True)
            for at in range(0, total, rows)
        ]
        parts.append(jnp.concatenate(found, 0))
    return jnp.concatenate(parts, 1)


def row_fluxes(plan, order, blocks, taps, begin, epochs, src_row, chosen, earlier):
    slabs, pairs, rows, half, side, lanes, stamp = (
        plan.slabs, plan.pairs, plan.rows, plan.half, plan.side, plan.lanes, plan.stamp,
    )
    mine = blocks[0].shape[0]
    groups, group = src_row.shape
    each = groups // slabs
    total = mine * rows
    step = min(64, rows)
    last = begin + mine == epochs

    def kernel(row_ref, chosen_ref, taps_ref, *rest):
        ins, table_ref, rest = rest[:slabs], rest[slabs], rest[slabs + 1 :]
        ins = [ins[order.index(m)] for m in range(slabs)]
        if begin:
            earlier_ref, rest = rest[0], rest[1:]
        flux_ref, *outs, left_high, left_low = rest
        q = slab_of()
        for m in range(slabs):
            d = q ^ m
            here = slice(m * lanes, (m + 1) * lanes)
            for i in range(mine):
                for start in range(0, rows, step):
                    straight = jnp.zeros((step, lanes), f32)
                    crossed = jnp.zeros((step, lanes), f32)
                    for shift in range(8):
                        shifted = ins[m][i, start + shift : start + shift + step + stamp - 8, :]
                        for base in range(0, stamp, 8):
                            value = shifted[base : base + step]
                            at = (begin + i) * stamp + base + shift
                            straight += taps_ref[0, d, at : at + 1] * value
                            crossed += taps_ref[1, d, at : at + 1] * value
                    at = i * rows + start
                    left_high[at : at + step, here], left_low[at : at + step, here] = split(
                        straight + swap_halves(plan, crossed)
                    )
        for part, value in enumerate(
            inverse_rows(plan, q, (left_high[...], left_low[...]), table_ref)
        ):
            here = slice(part * half, (part + 1) * half)
            flux_ref[:total, here], flux_ref[total:, here] = split(value)
        for m in range(1 if last else 0, slabs):
            owner = q ^ m if last else m
            out = outs[m - 1] if last else outs[0].at[m]
            if begin:
                out[:begin] = earlier_ref[owner]
            out[begin:] = pick(
                plan, q, flux_ref, chosen_ref, row_ref, [owner * each + i for i in range(each)]
            )

    left = pltpu.VMEM((total, side), bf16)
    shape = (begin + mine, each * group)
    ins = [("v", src_row), ("v", chosen), ("v", taps)]
    ins += [("v", blocks[m]) for m in order] + [("v", plan.back)]
    if begin:
        ins.append(("v", earlier))
    flux, *picked = call(
        kernel,
        [("v", (2 * total, side), bf16)] + ([("v", shape)] * (slabs - 1) if last else [("v", (slabs, *shape))]),
        ins,
        [left, left],
        micros=3.5,
    )
    return flux, picked


def own_fluxes(plan, flux, begin, src_row, chosen, earlier):
    groups, group = src_row.shape
    each = groups // plan.slabs
    epochs = begin + flux.shape[0] // 2 // plan.rows

    def kernel(row_ref, chosen_ref, flux_ref, *rest):
        out, q = rest[-1], slab_of()
        if begin:
            out[:begin] = rest[0][q]
        out[begin:] = pick(plan, q, flux_ref, chosen_ref, row_ref, [q * each + i for i in range(each)])

    ins = [("v", src_row), ("v", chosen), ("v", flux)]
    return call(
        kernel,
        [("v", (epochs, each * group))],
        ins + ([("v", earlier)] if begin else []),
        micros=0.9,
    )


def trade(parts, axes, count):
    result = list(parts)
    for m in reversed(range(1, count)):
        result[m] = lax.ppermute(parts[m], axes, [(i, i ^ m) for i in range(count)])
    return result


def make_shards(mesh):
    slabs = mesh.shape["tile"] * mesh.shape["sub"]
    ranks = mesh.shape["epoch"]

    def shards(epoch_images, psf_bank, psf_index, flux_scale, noise_level, src_row, src_col):
        epochs, rows, side = epoch_images.shape
        plan = Plan(side, slabs, psf_bank.shape[1])
        direct = ranks & (ranks - 1) == 0 and side // ranks % 128 == 0
        pieces = ranks if direct else 1
        group = math.gcd(512, src_row.shape[0] // slabs)
        scalars = (psf_index, flux_scale, noise_level)

        edges = list(range(0, epochs, 2)) + [epochs]
        parties = list(zip(edges, edges[1:]))

        far, shares, weighted, images, table = row_transform_far(
            plan, *scalars, epoch_images, psf_bank, side // pieces
        )
        half = slabs // 2
        near, near_rows = row_transform_near(plan, weighted, images, table)
        near = coadd_rest(plan, weighted, near_rows, list(range(half - 1))) + [near]
        (blocks,) = row_transform(plan, images, table, [(0, epochs)])
        numer = trade(near + far, slab_axes, slabs)
        order = list(range(half, slabs)) + list(range(half))[::-1]
        numer, blocks = lax.optimization_barrier(([numer[m] for m in order], blocks))
        numer = numerator(plan, shares, order, numer, pieces)
        bank, numer = lax.optimization_barrier((psf_bank, numer))
        spectrum, power, taps = psf_planes(plan, bank, psf_index)
        blocks = trade(blocks, slab_axes, slabs)
        if direct:
            own = trade(numer, "epoch", ranks)
            own = sum(own[m] for m in [*range(1, ranks)[-1:], *range(1, ranks - 1), 0])
            own, spectrum = lax.optimization_barrier((own, spectrum))
            numer = trade([own] * ranks, "epoch", ranks)
        else:
            own = lax.psum(numer[0], "epoch")
            numer = [own]
        gain, cross = filter_gains(plan, flux_scale, noise_level, own, spectrum, power)
        image = None
        if plan.pairs > 1:
            image = column_transform(plan, [0], blocks, None)
        image = column_transform(plan, list(range(1, plan.pairs)), blocks, image)
        returned = []
        for begin, end in parties:
            rows_back = column_inverse(plan, image, gain, cross, numer, begin, end)
            returned.append(trade(rows_back, slab_axes, slabs))
        chosen = column_choice(side, src_col.reshape(-1, group))
        src_row = src_row.reshape(-1, group)
        earlier = None
        for (begin, end), block in zip(parties, returned):
            flux, picked = row_fluxes(plan, order, block, taps, begin, epochs, src_row, chosen, earlier)
            if end < epochs:
                (earlier,) = picked
        picked = [*own_fluxes(plan, flux, begin, src_row, chosen, earlier), *picked]
        difference = row_images(plan, returned)
        return difference, sum(trade(picked, slab_axes, slabs)[::-1])

    return shards


def solution(mesh):
    in_specs = (
        P(("grp", "epoch"), ("tile", "sub"), None),
        P(),
        P(("grp", "epoch")),
        P(("grp", "epoch")),
        P(("grp", "epoch")),
        P("grp"),
        P("grp"),
    )
    out_specs = (P(("grp", "epoch"), ("tile", "sub"), None), P(("grp", "epoch"), ("tile", "sub")))
    return jax.shard_map(
        make_shards(mesh), mesh=mesh, in_specs=in_specs, out_specs=out_specs, check_vma=False
    )
```
